32 devices in a mesh: row: 8 (over z, x), col: 4 (over y, core).
Axes of the slice: x: 2, y: 2, z: 4, core: 2. Of those that a mesh axis runs over, the one named last changes fastest.
Arguments:
- amplitudes: bfloat16 [8192, 8192], P('row', 'col'), may hold values from -6 to 6
- integrals: bfloat16 [8192, 2048], P('col', 'row'), may hold values from -0.0625 to 0.0625
- amp_mask: int32 [64, 64], P('row', 'col'), may hold values 0 or 1
- int_mask: int32 [64, 16], P('col', 'row'), may hold values 0 or 1
Outputs:
- ladder: bfloat16 [8192, 2048], P('row', 'col')
The draws below stay inside these ranges and needn't reach their ends.
All inputs are finite; a program needn't handle non-finite values. No bound on the sum of `amp_mask` or of `int_mask` on one device may be relied on, other than what follows from the above.
Results may differ from the reference program's by a relative error of at most 0.001.
Values may be sent and summed in bfloat16 or wider, within the bound.
No kernel may reach another device: no remote copies, remote signals or barrier semaphores. Data moves between devices by JAX's collectives and lax.ppermute only.
A program may use at most 128 MiB of HBM per device.

```python
import jax
import jax.numpy as jnp

TILE = 128
PAIRS = 8192
CONTR = 8192
COLS = 2048


def touch_ends(array, rng, least, top_value):
    longest = array.shape.index(max(array.shape))
    spots = []
    for shift in (0, 1):
        where = [jax.random.randint(jax.random.fold_in(rng, axis), (), 0, length) for axis, length in enumerate(array.shape)]
        where[longest] = (where[longest] + shift) % array.shape[longest]
        spots.append(tuple(where))
    return array.at[spots[0]].set(least).at[spots[1]].set(top_value)


def shard_levels(rng, dims, split, smallest, top_value):
    def one(axis_at, shards_of):
        draws = jax.random.uniform(jax.random.fold_in(jax.random.fold_in(rng, 6), axis_at), (shards_of,), jnp.float32, smallest / len(split), top_value / len(split))
        return jnp.repeat(jnp.exp(draws), dims[axis_at] // shards_of).reshape((-1,) + (1,) * (len(dims) - axis_at - 1))

    gain = one(*split[0])
    for cut in split[1:]:
        gain = gain * one(*cut)
    return gain


def noise(own_key, extent, scale, reach, pieces=(), held_as=jnp.bfloat16):
    result = scale * jax.random.normal(own_key, extent, jnp.float32)
    if pieces:
        result = result * shard_levels(own_key, extent, pieces, -0.22, 0.18)
    return jnp.clip(result, -reach, reach).astype(held_as)


def setup_inputs(seed: int = 0) -> dict:
    arg_keys = jax.random.split(jax.random.key(seed), 5)
    return {
        "amplitudes": noise(arg_keys[0], (PAIRS, CONTR), 1.0, 6.0, ((0, 8), (1, 4))),
        "integrals": noise(arg_keys[1], (CONTR, COLS), CONTR ** -0.5, 0.0625, ((0, 4), (1, 8))),
        "amp_mask": touch_ends((jax.random.randint(arg_keys[2], (PAIRS // TILE, CONTR // TILE), 0, 2) < 1).astype(jnp.int32), jax.random.fold_in(arg_keys[2], 1), 0, 1),
        "int_mask": touch_ends((jax.random.randint(arg_keys[3], (CONTR // TILE, COLS // TILE), 0, 2) < 1).astype(jnp.int32), jax.random.fold_in(arg_keys[3], 1), 0, 1),
    }


def expand(mask):
    spread = jnp.repeat(jnp.repeat(mask, TILE, axis=0), TILE, axis=1)
    return spread.astype(jnp.bfloat16)


def reference(amplitudes, integrals, amp_mask, int_mask):
    sparse_amp = amplitudes * expand(amp_mask)
    sparse_int = integrals * expand(int_mask)
    ladder = jnp.dot(sparse_amp, sparse_int, preferred_element_type=jnp.float32)
    return ladder.astype(jnp.bfloat16)
```

```python
import functools

import jax
import jax.numpy as jnp
from jax import lax
from jax.experimental import pallas as pl
from jax.experimental.pallas import tpu as pltpu
from jax.sharding import PartitionSpec as P

TILE = 128
VMEM_LIMIT = 48 * 1024 * 1024


def expand(mask):
    spread = jnp.repeat(jnp.repeat(mask, TILE, axis=0), TILE, axis=1)
    return spread.astype(jnp.bfloat16)


def dense_ladder(amplitudes, integrals, amp_mask, int_mask):
    sparse_amp = amplitudes * expand(amp_mask)
    sparse_int = integrals * expand(int_mask)
    partial_value = jnp.dot(
        sparse_amp,
        lax.all_gather(sparse_int, "row", axis=1, tiled=True),
        preferred_element_type=jnp.float32,
    )
    ladder = lax.psum_scatter(partial_value, "col", scatter_dimension=1, tiled=True)
    return ladder.astype(jnp.bfloat16)


def pack_tiles(integrals, flat_mask, cap):
    wide = integrals.shape[1] // TILE
    tiles = flat_mask.shape[1]

    def kernel(mask_ref, b_ref, out_ref):
        place = jnp.int32(0)
        for t in range(tiles):
            k, n = divmod(t, wide)
            keep = mask_ref[0, t] != 0

            @pl.when(keep & (place < cap))
            def _(k=k, n=n, place=place):
                at = pl.multiple_of(place * TILE, TILE)
                out_ref[pl.ds(at, TILE), :] = b_ref[k * TILE:(k + 1) * TILE, n * TILE:(n + 1) * TILE]

            place = place + keep.astype(jnp.int32)

    return pl.pallas_call(
        kernel,
        out_shape=jax.ShapeDtypeStruct((cap * TILE, TILE), integrals.dtype),
        in_specs=[pl.BlockSpec(memory_space=pltpu.SMEM), pl.BlockSpec(memory_space=pltpu.VMEM)],
        out_specs=pl.BlockSpec(memory_space=pltpu.VMEM),
        compiler_params=pltpu.CompilerParams(vmem_limit_bytes=VMEM_LIMIT),
        cost_estimate=pl.CostEstimate(flops=0, bytes_accessed=2 << 20, transcendentals=0),
        name="pack_tiles",
    )(flat_mask, integrals)


def mask_tiles(amplitudes, mask):
    rows, cols = amplitudes.shape

    def kernel(mask_ref, a_ref, out_ref):
        i = pl.program_id(0)
        for t in range(cols // TILE):
            at = slice(t * TILE, (t + 1) * TILE)
            tile = a_ref[:, at]
            out_ref[:, at] = jnp.where(mask_ref[i, t] != 0, tile, jnp.zeros_like(tile))

    block = pl.BlockSpec((TILE, cols), lambda i: (i, 0))
    return pl.pallas_call(
        kernel,
        grid=(rows // TILE,),
        out_shape=jax.ShapeDtypeStruct(amplitudes.shape, amplitudes.dtype),
        in_specs=[pl.BlockSpec(memory_space=pltpu.SMEM), block],
        out_specs=block,
        compiler_params=pltpu.CompilerParams(vmem_limit_bytes=VMEM_LIMIT),
        cost_estimate=pl.CostEstimate(flops=0, bytes_accessed=2 * amplitudes.size * 2, transcendentals=0),
        name="mask_tiles",
    )(mask, amplitudes)


def shard_product(amps, masks, pick, shard, choices):
    rows, depth = amps.shape
    tiles = masks.shape[1]
    wide = tiles * TILE // depth
    cap = sum(part.shape[0] for part in choices[0])
    parts = []
    for choice in choices:
        for part in choice:
            if not any(part is p for p in parts):
                parts.append(part)
    step = 256

    def kernel(pick_ref, masks_ref, a_ref, *rest):
        refs = rest[:len(parts)]
        out_ref, packed, wide_ref, sem = rest[len(parts):]

        @pl.when(pl.program_id(0) == 0)
        def _():
            for number, choice in enumerate(choices):
                @pl.when(pick_ref[0] == number)
                def _(choice=choice):
                    at = 0
                    copies = []
                    for part in choice:
                        index = [part is p for p in parts].index(True)
                        copies.append(pltpu.make_async_copy(
                            refs[index], packed.at[pl.ds(at, part.shape[0])], sem.at[len(copies)]))
                        at += part.shape[0]
                    for copy in copies:
                        copy.start()
                    for copy in copies:
                        copy.wait()

            place = jnp.int32(0)
            for t in range(tiles):
                k, n = divmod(t, wide)
                rows_at = slice(k * TILE, (k + 1) * TILE)
                cols_at = slice(n * TILE, (n + 1) * TILE)
                keep = masks_ref[pick_ref[1], t] != 0
                at = pl.multiple_of(jnp.minimum(place * TILE, cap - TILE), TILE)
                tile = packed[pl.ds(at, TILE), :]
                wide_ref[rows_at, cols_at] = jnp.where(keep, tile, jnp.zeros_like(tile))
                place = place + keep.astype(jnp.int32)

        out_ref[...] = jnp.dot(a_ref[...], wide_ref[...], preferred_element_type=jnp.float32)

    return pl.pallas_call(
        kernel,
        out_shape=jax.ShapeDtypeStruct((rows, wide * TILE), jnp.float32),
        grid_spec=pltpu.PrefetchScalarGridSpec(
            num_scalar_prefetch=2,
            grid=(rows // step,),
            in_specs=[pl.BlockSpec((step, depth), lambda i, *_: (i, 0))]
            + [pl.BlockSpec(memory_space=pl.ANY)] * len(parts),
            out_specs=pl.BlockSpec((step, wide * TILE), lambda i, *_: (i, 0)),
            scratch_shapes=[
                pltpu.VMEM((cap, TILE), amps.dtype),
                pltpu.VMEM((depth, wide * TILE), amps.dtype),
                pltpu.SemaphoreType.DMA((2,)),
            ],
        ),
        compiler_params=pltpu.CompilerParams(vmem_limit_bytes=VMEM_LIMIT),
        cost_estimate=pl.CostEstimate(
            flops=2 * rows * depth * wide * TILE, bytes_accessed=amps.size * 2 + (2 << 20), transcendentals=0),
        name="shard_product",
    )(jnp.stack([pick, shard]).astype(jnp.int32), masks, amps, *parts)


Z, X, Y = 4, 2, 2


def row_moves(to):
    return [(z * 2 + x, to(z, x)[0] * 2 + to(z, x)[1]) for z in range(Z) for x in range(X) if to(z, x) is not None]


ENDS, MIDDLE = (0, 3), (1, 2)
ACROSS_X = row_moves(lambda z, x: (z, 1 - x))
ACROSS_X_ENDS = row_moves(lambda z, x: (z, 1 - x) if z in ENDS else None)
ACROSS_X_MIDDLE = row_moves(lambda z, x: (z, 1 - x) if z in MIDDLE else None)
PAIR = row_moves(lambda z, x: (z ^ 1, x))
CENTRE = row_moves(lambda z, x: (3 - z, x) if z in MIDDLE else None)
OUTWARD = row_moves(lambda z, x: (z ^ 1, x) if z in MIDDLE else None)
CORES = [(0, 1), (1, 0), (2, 3), (3, 2)]


def across_y(far):
    pairs = []
    for z in range(Z):
        home = (z // 2) ^ int(far)
        for x in range(X):
            for c in range(2):
                row = z * 2 + x
                pairs.append((row * 4 + (1 - home) * 2 + c, row * 4 + home * 2 + c))
    return pairs


def sparse_ladder(amplitudes, integrals, amp_mask, int_mask):
    barrier = lax.optimization_barrier
    tiles = int_mask.size
    cap = tiles * 3 // 4
    row, col = lax.axis_index("row"), lax.axis_index("col")
    z, x = row // 2, row % 2
    y, c = col // 2, col % 2
    end = (z == 0) | (z == 3)

    flat_mask = int_mask.reshape(1, tiles)
    masks = lax.all_gather(flat_mask, "row", axis=0, tiled=True)
    most = jnp.max(jnp.sum((masks != 0).astype(jnp.int32), axis=1))
    too_many = jnp.max(lax.all_gather(most, "col", axis=0)) > cap

    own = pack_tiles(integrals, flat_mask, cap)
    amps = mask_tiles(amplitudes, amp_mask)

    move = lambda value, pairs: lax.ppermute(value, "row", pairs)
    half = cap * TILE // 2
    pair, centre, own_x = barrier((move(own, PAIR), move(own, CENTRE), move(own, ACROSS_X)))
    two_end, two_mid, pair_x = barrier((move(centre, OUTWARD), move(pair, CENTRE), move(pair, ACROSS_X)))
    three_end, three_mid_x, two_x_end, two_x_mid = barrier((
        move(two_mid, OUTWARD), move(own_x, CENTRE), move(two_end, ACROSS_X_ENDS), move(two_mid, ACROSS_X_MIDDLE)))
    three_x_end = (move(three_end[:half], ACROSS_X_ENDS), move(two_x_mid[half:], OUTWARD))

    product = functools.partial(shard_product, amps, masks)
    is_end = end.astype(jnp.int32)

    def stage(first, second, first_z, second_z, at_x, far):
        choices = first[0] + second[0]
        first_pick, second_pick = first[1], second[1] + len(first[0])
        keep_first = first_z % 2 == c
        send = product(
            jnp.where(keep_first, second_pick, first_pick), jnp.where(keep_first, second_z, first_z) * 2 + at_x, choices)
        got = lax.ppermute(send, "col", CORES)
        keep = product(
            jnp.where(keep_first, first_pick, second_pick), jnp.where(keep_first, first_z, second_z) * 2 + at_x, choices)
        total = keep + got
        return total, lax.ppermute(total, ("row", "col"), across_y(far))

    zero = jnp.int32(0)
    near_own = stage(([[own]], zero), ([[pair]], zero), z, z ^ 1, x, False)
    near_x = stage(([[own_x]], zero), ([[pair_x]], zero), z, z ^ 1, 1 - x, False)
    far_own = stage(
        ([[two_mid], [two_end]], is_end), ([[centre], [three_end]], is_end), z ^ 2, z ^ 3, x, True)
    far_x = stage(
        ([[two_x_mid], [two_x_end]], is_end), ([[three_mid_x], list(three_x_end)], is_end), z ^ 2, z ^ 3, 1 - x, True)

    near = z // 2 == y
    mine = jnp.where(near, near_own[0] + near_own[1], far_own[0] + far_own[1]).astype(jnp.bfloat16)
    other = jnp.where(near, near_x[0] + near_x[1], far_x[0] + far_x[1]).astype(jnp.bfloat16)
    ladder = jnp.concatenate([jnp.where(x == 0, mine, other), jnp.where(x == 0, other, mine)], axis=1)
    return lax.cond(
        too_many, lambda: dense_ladder(amplitudes, integrals, amp_mask, int_mask), lambda: ladder)


def solution(mesh):
    in_specs = (P("row", "col"), P("col", "row"), P("row", "col"), P("col", "row"))
    out_specs = P("row", "col")
    here = dict(mesh.shape)
    per_device = sparse_ladder if here == {"row": Z * X, "col": Y * 2} else dense_ladder
    return jax.shard_map(
        per_device, mesh=mesh, in_specs=in_specs, out_specs=out_specs, check_vma=False
    )
```

```python
import jax
import jax.numpy as jnp
from jax import lax
from jax.experimental import pallas as pl
from jax.experimental.pallas import tpu as pltpu
from jax.sharding import PartitionSpec as P

TILE = 128
VMEM_LIMIT = 12 * 1024 * 1024


def expand(mask):
    spread = jnp.repeat(jnp.repeat(mask, TILE, axis=0), TILE, axis=1)
    return spread.astype(jnp.bfloat16)


def dense_ladder(amplitudes, integrals, amp_mask, int_mask):
    rows, cols = lax.axis_size("row"), lax.axis_size("col")
    row, col = lax.axis_index("row"), lax.axis_index("col")
    sparse_amp = amplitudes * expand(amp_mask)
    sparse_int = integrals * expand(int_mask)
    width = integrals.shape[1]
    share = rows * width // cols
    sums = jnp.zeros((amplitudes.shape[0], rows * width), jnp.float32)
    for step in range(rows):
        shard = lax.ppermute(sparse_int, "row", [((r + step) % rows, r) for r in range(rows)]) if step else sparse_int
        part = jnp.dot(sparse_amp, shard, preferred_element_type=jnp.float32)
        sums = lax.dynamic_update_slice(sums, part, (0, (row + step) % rows * width))
    ladder = lax.dynamic_slice(sums, (0, col * share), (sums.shape[0], share))
    for step in range(1, cols):
        part = lax.dynamic_slice(sums, (0, (col + step) % cols * share), (sums.shape[0], share))
        ladder = ladder + lax.ppermute(part, "col", [(c, (c + step) % cols) for c in range(cols)])
    return ladder.astype(jnp.bfloat16)


TOKEN = jax.ShapeDtypeStruct((8, TILE), jnp.float32)
LIGHT = pl.CostEstimate(flops=1, bytes_accessed=1, transcendentals=0)
META = 16


def in_hbm(array):
    return pltpu.with_memory_space_constraint(array, pltpu.HBM)


def call(kernel, name, **kwargs):
    return pl.pallas_call(
        kernel,
        compiler_params=pltpu.CompilerParams(vmem_limit_bytes=VMEM_LIMIT),
        cost_estimate=LIGHT,
        name=name,
        **kwargs,
    )


VMEM = pl.BlockSpec(memory_space=pltpu.VMEM)
SMEM = pl.BlockSpec(memory_space=pltpu.SMEM)
ANY = pl.BlockSpec(memory_space=pl.ANY)


def pack_tiles(shards, masks, across_masks, cap):
    wide = shards[0].shape[1] // TILE
    tiles = masks[0].shape[0]
    count = len(shards)

    def kernel(*refs):
        mask_refs, across_refs, b_refs, out_ref = refs[:count], refs[count:2 * count], refs[2 * count:-1], refs[-1]
        place = across = jnp.int32(0)
        lane = lax.broadcasted_iota(jnp.int32, (META, TILE), 1)
        sub = lax.broadcasted_iota(jnp.int32, (META, TILE), 0)
        meta = jnp.zeros((META, TILE), jnp.float32)
        for s in range(count):
            for t in range(tiles):
                k, n = divmod(t, wide)
                keep = mask_refs[s][t] != 0

                @pl.when(keep & (place < cap))
                def _(s=s, k=k, n=n, place=place):
                    at = pl.multiple_of(place * TILE, TILE)
                    out_ref[pl.ds(at, TILE), :] = b_refs[s][k * TILE:(k + 1) * TILE, n * TILE:(n + 1) * TILE]

                place = place + keep.astype(jnp.int32)
                across = across + (across_refs[s][t] != 0).astype(jnp.int32)
                meta = jnp.where((lane == s * tiles + t) & keep, 1.0, meta)
        more = jnp.maximum(place, across) > cap
        meta = jnp.where(sub == 0, meta, jnp.where((sub == 1) & more, 1.0, 0.0))
        out_ref[cap * TILE:, :] = meta.astype(out_ref.dtype)

    return call(
        kernel, "pack_tiles",
        out_shape=jax.ShapeDtypeStruct((cap * TILE + META, TILE), shards[0].dtype),
        in_specs=[SMEM] * (2 * count) + [VMEM] * count,
        out_specs=VMEM,
    )(*masks, *across_masks, *shards)


def mask_tiles(amplitudes, mask):
    rows, cols = amplitudes.shape
    step = 2

    def kernel(mask_ref, a_ref, out_ref, token_ref):
        i = pl.program_id(0)
        token_ref[...] = jnp.zeros_like(token_ref)
        for r in range(step):
            for t in range(cols // TILE):
                spot = (slice(r * TILE, (r + 1) * TILE), slice(t * TILE, (t + 1) * TILE))
                keep = mask_ref[i * step + r, t] != 0

                @pl.when(keep)
                def _(spot=spot):
                    out_ref[spot] = a_ref[spot]

                @pl.when(jnp.logical_not(keep))
                def _(spot=spot):
                    out_ref[spot] = jnp.zeros((TILE, TILE), out_ref.dtype)

    block = pl.BlockSpec((step * TILE, cols), lambda i: (i, 0))
    return call(
        kernel, "mask_tiles",
        grid=(rows // TILE // step,),
        out_shape=(jax.ShapeDtypeStruct(amplitudes.shape, amplitudes.dtype), TOKEN),
        in_specs=[SMEM, block],
        out_specs=(block, pl.BlockSpec(TOKEN.shape, lambda i: (0, 0))),
    )(mask, amplitudes)


def shard_product(amps, picks, step, choices, tokens):
    rows, depth = amps[0].shape
    count = len(amps)
    height = sum(part.shape[0] for part in choices[0])
    cap = height - META
    wide = 2
    tiles = count * wide * depth // TILE
    word = 16
    parts = []
    for choice in choices:
        for part in choice:
            if not any(part is p for p in parts):
                parts.append(part)

    def kernel(picks_ref, *refs):
        token_refs, refs = refs[:len(tokens)], refs[len(tokens):]
        a_refs, refs = refs[:count], refs[count:]
        p_any, refs = refs[:len(parts)], refs[len(parts):]
        out_ref, token_ref, packed, wide_ref, sem = refs
        pick = picks_ref[step]
        token_ref[...] = sum(ref[...] for ref in token_refs)
        for number, choice in enumerate(choices):
            @pl.when(pick == number)
            def _(choice=choice):
                at = 0
                copies = []
                for part in choice:
                    index = [part is p for p in parts].index(True)
                    copies.append(pltpu.make_async_copy(
                        p_any[index], packed.at[pl.ds(at, part.shape[0])], sem.at[len(copies)]))
                    at += part.shape[0]
                for copy in copies:
                    copy.start()
                for copy in copies:
                    copy.wait()

        @pl.when(pick >= 0)
        def _():
            meta = packed[cap:, :].astype(jnp.float32)
            lane = lax.broadcasted_iota(jnp.int32, meta.shape, 1)
            sub = lax.broadcasted_iota(jnp.int32, meta.shape, 0)
            first = (sub == 0) & (meta != 0)
            bits = [
                jnp.sum(jnp.where(
                    first & (lane >= lo) & (lane < lo + word), jnp.left_shift(1, (lane - lo) & (word - 1)), 0))
                for lo in range(0, tiles, word)]
            token_ref[...] += jnp.where(sub == 1, meta, 0.0)[:token_ref.shape[0]]
            place = jnp.int32(0)
            for s in range(count):
                for t in range(s * tiles // count, (s + 1) * tiles // count):
                    k, n = divmod(t, wide)
                    keep = ((bits[t // word] >> (t % word)) & 1) != 0
                    at = pl.multiple_of(jnp.minimum(place * TILE, cap - TILE), TILE)
                    tile = packed[pl.ds(at, TILE), :]
                    wide_ref[k * TILE:(k + 1) * TILE, n * TILE:(n + 1) * TILE] = jnp.where(
                        keep, tile, jnp.zeros_like(tile))
                    place = place + keep.astype(jnp.int32)
                term = jnp.dot(
                    a_refs[s][...], wide_ref[s * depth:(s + 1) * depth, :], preferred_element_type=jnp.float32)
                if s:
                    out_ref[...] += term
                else:
                    out_ref[...] = term

    return call(
        kernel, "shard_product",
        out_shape=(jax.ShapeDtypeStruct((rows, wide * TILE), jnp.float32), TOKEN),
        in_specs=[SMEM] + [VMEM] * (len(tokens) + count) + [ANY] * len(parts),
        out_specs=(VMEM, VMEM),
        scratch_shapes=[
            pltpu.VMEM((height, TILE), amps[0].dtype),
            pltpu.VMEM((count * depth, wide * TILE), amps[0].dtype),
            pltpu.SemaphoreType.DMA((2,)),
        ],
    )(picks, *tokens, *amps, *map(in_hbm, parts))


def add_sums(one, two):
    def kernel(one_ref, two_ref, out_ref, token_ref):
        token_ref[...] = jnp.zeros_like(token_ref)
        out_ref[...] = one_ref[...] + two_ref[...]

    return call(
        kernel, "add_sums",
        out_shape=(jax.ShapeDtypeStruct(one.shape, one.dtype), TOKEN),
        in_specs=[VMEM, VMEM],
        out_specs=(VMEM, VMEM),
    )(one, two)


def top_and_rest(one, two, at):
    def kernel(one_ref, two_ref, top_ref, rest_ref, sem):
        copies = [
            pltpu.make_async_copy(one_ref.at[pl.ds(0, at)], top_ref, sem.at[0]),
            pltpu.make_async_copy(two_ref.at[pl.ds(at, two.shape[0] - at)], rest_ref, sem.at[1])]
        for copy in copies:
            copy.start()
        for copy in copies:
            copy.wait()

    return call(
        kernel, "top_and_rest",
        out_shape=(
            jax.ShapeDtypeStruct((at, one.shape[1]), one.dtype),
            jax.ShapeDtypeStruct((two.shape[0] - at, two.shape[1]), two.dtype)),
        in_specs=[ANY, ANY],
        out_specs=(VMEM, VMEM),
        scratch_shapes=[pltpu.SemaphoreType.DMA((2,))],
    )(in_hbm(one), in_hbm(two))


Z, X, Y = 4, 2, 2
AXES = ("row", "col")


def device(z, x, y, c):
    return (z * X + x) * Y * 2 + y * 2 + c


def moves(to, home=True):
    pairs = []
    for z in range(Z):
        for x in range(X):
            for y in range(Y):
                if to(z, x) is not None:
                    c = z % 2 if home else 1 - z % 2
                    pairs.append((device(z, x, y, c), device(*to(z, x), y, c)))
    return pairs


def across_x(z, x):
    return z, 1 - x


def across_x_ends(z, x):
    return (z, 1 - x) if z in (0, 3) else None


def across_x_middle(z, x):
    return (z, 1 - x) if z in (1, 2) else None


def to_pair(z, x):
    return z ^ 1, x


def over_centre(z, x):
    return (3 - z, x) if z in (1, 2) else None


def outward(z, x):
    return (z ^ 1, x) if z in (1, 2) else None


def to_y(far, cores):
    pairs = []
    for z in range(Z):
        end = (z // 2) ^ int(far)
        for x in range(X):
            for c in cores(z):
                pairs.append((device(z, x, 1 - end, c), device(z, x, end, c)))
    return pairs


def both(z):
    return 0, 1


def home_core(z):
    return (z % 2,)


def other_core(z):
    return (1 - z % 2,)


FROM_OTHER_CORE = [
    (device(z, x, y, 1 - z % 2), device(z, x, y, z % 2)) for z in range(Z) for x in range(X) for y in range(Y)]
CORES = [(0, 1), (1, 0), (2, 3), (3, 2)]
CHIPS_Y = [(0, 2), (2, 0), (1, 3), (3, 1)]
CROSSWISE = [(0, 3), (3, 0), (1, 2), (2, 1)]


def sparse_ladder(amplitudes, integrals, amp_mask, int_mask):
    barrier = lax.optimization_barrier
    tiles = int_mask.size
    cap = 2 * tiles * 11 // 16
    half = cap * TILE // 2
    row, col = lax.axis_index("row"), lax.axis_index("col")
    z, x = row // X, row % X
    y, c = col // 2, col % 2
    is_end = ((z == 0) | (z == Z - 1)).astype(jnp.int32)
    home = z % 2 == c

    def move(value, pairs):
        return lax.ppermute(value, AXES, pairs)

    def after(*tokens):
        return lambda *shards: barrier((*shards, tokens))

    picks = jnp.stack([
        jnp.where(home, 0, 1),
        jnp.where(home, is_end, -1),
        jnp.where(home, 0, 1),
        jnp.where(home, is_end, 2 + is_end),
        jnp.where(home, -1, is_end),
    ]).astype(jnp.int32)

    flat_mask = int_mask.reshape(tiles)
    other = move(integrals, FROM_OTHER_CORE)
    other_mask, across, other_across = [lax.ppermute(flat_mask, "col", p) for p in (CORES, CHIPS_Y, CROSSWISE)]
    other_mask, amplitudes_now, picks = barrier((other_mask, amplitudes, picks))
    masked, masked_token = mask_tiles(amplitudes_now, amp_mask)
    own = pack_tiles((integrals, other), (flat_mask, other_mask), (across, other_across), cap)

    amps = (masked, lax.ppermute(masked, "col", CORES))
    one, centre, own_x, tokens = after(masked_token)(
        move(own, moves(to_pair)), move(own, moves(over_centre)), move(own, moves(across_x)))

    a_sum, token = shard_product(amps, picks, 0, [[own], [one]], tokens)
    a_far = move(a_sum, to_y(False, both))
    two_end, two_mid, one_x, tokens = after(token)(
        move(centre, moves(outward, False)), move(one, moves(over_centre, False)), move(one, moves(across_x, False)))

    c_sum, token = shard_product(amps, picks, 1, [[two_mid], [two_end]], tokens)
    c_far = move(c_sum, to_y(True, home_core))
    b_sum, token = shard_product(amps, picks, 2, [[own_x], [one_x]], (token,))
    b_far = move(b_sum, to_y(False, both))
    a_both, a_token = add_sums(a_sum, a_far)
    three_end, three_mid_x, two_x_end, two_x_mid, tokens = after(token, a_token)(
        move(two_mid, moves(outward)), move(own_x, moves(over_centre)),
        move(two_end, moves(across_x_ends)), move(two_mid, moves(across_x_middle)))

    d_sum, token = shard_product(
        amps, picks, 3, [[two_x_mid], [two_x_end], [centre], [three_end]], tokens)
    top, rest = top_and_rest(three_end, two_x_mid, half)
    three_x, three_x_rest, tokens = after(token)(
        move(top, moves(across_x_ends, False)), move(rest, moves(outward)))

    d_far = move(d_sum, to_y(True, both))
    e_sum, token = shard_product(amps, picks, 4, [[three_mid_x], [three_x, three_x_rest]], tokens)
    e_far = move(e_sum, to_y(True, other_core))
    excess = token + lax.ppermute(token, "col", CORES)

    def finish():
        near = z // 2 == y
        d_both = d_sum + d_far
        mine = jnp.where(near, a_both, jnp.where(home, c_sum + c_far, d_both)).astype(jnp.bfloat16)
        rest = jnp.where(near, b_sum + b_far, jnp.where(home, d_both, e_sum + e_far)).astype(jnp.bfloat16)
        return jnp.concatenate([jnp.where(x == 0, mine, rest), jnp.where(x == 0, rest, mine)], axis=1)

    return lax.cond(
        jnp.max(excess) > 0, lambda: dense_ladder(amplitudes, integrals, amp_mask, int_mask), finish)


def solution(mesh):
    in_specs = (P("row", "col"), P("col", "row"), P("row", "col"), P("col", "row"))
    out_specs = P("row", "col")
    here = dict(mesh.shape)
    per_device = sparse_ladder if here == {"row": Z * X, "col": Y * 2} else dense_ladder
    return jax.shard_map(
        per_device, mesh=mesh, in_specs=in_specs, out_specs=out_specs, check_vma=False
    )
```

```python
import jax
import jax.numpy as jnp
from jax import lax
from jax.experimental import pallas as pl
from jax.experimental.pallas import tpu as pltpu
from jax.sharding import PartitionSpec as P

TILE = 128
VMEM_LIMIT = 12 * 1024 * 1024


def expand(mask):
    spread = jnp.repeat(jnp.repeat(mask, TILE, axis=0), TILE, axis=1)
    return spread.astype(jnp.bfloat16)


def dense_ladder(amplitudes, integrals, amp_mask, int_mask):
    rows, cols = lax.axis_size("row"), lax.axis_size("col")
    row, col = lax.axis_index("row"), lax.axis_index("col")
    sparse_amp = amplitudes * expand(amp_mask)
    sparse_int = integrals * expand(int_mask)
    width = integrals.shape[1]
    share = rows * width // cols
    sums = jnp.zeros((amplitudes.shape[0], rows * width), jnp.float32)
    for step in range(rows):
        shard = lax.ppermute(sparse_int, "row", [((r + step) % rows, r) for r in range(rows)]) if step else sparse_int
        part = jnp.dot(sparse_amp, shard, preferred_element_type=jnp.float32)
        sums = lax.dynamic_update_slice(sums, part, (0, (row + step) % rows * width))
    ladder = lax.dynamic_slice(sums, (0, col * share), (sums.shape[0], share))
    for step in range(1, cols):
        part = lax.dynamic_slice(sums, (0, (col + step) % cols * share), (sums.shape[0], share))
        ladder = ladder + lax.ppermute(part, "col", [(c, (c + step) % cols) for c in range(cols)])
    return ladder.astype(jnp.bfloat16)


TOKEN = jax.ShapeDtypeStruct((8, TILE), jnp.float32)
LIGHT = pl.CostEstimate(flops=1, bytes_accessed=1, transcendentals=0)
STEPS = 5
TOP = 12
LOW = 4
BITS = 16 + LOW
GROUP = 128
META = 16


def in_hbm(array):
    return pltpu.with_memory_space_constraint(array, pltpu.HBM)


def call(kernel, name, cost=LIGHT, **kwargs):
    return pl.pallas_call(
        kernel,
        compiler_params=pltpu.CompilerParams(vmem_limit_bytes=VMEM_LIMIT),
        cost_estimate=cost,
        name=name,
        **kwargs,
    )


VMEM = pl.BlockSpec(memory_space=pltpu.VMEM)
SMEM = pl.BlockSpec(memory_space=pltpu.SMEM)
ANY = pl.BlockSpec(memory_space=pl.ANY)


def pack_tiles(shards, masks, across_masks, cap):
    wide = shards[0].shape[1] // TILE
    tiles = masks[0].size
    count = len(shards)

    def kernel(*refs):
        mask_refs, across_refs, b_refs, out_ref = refs[:count], refs[count:2 * count], refs[2 * count:-1], refs[-1]
        place = across = jnp.int32(0)
        lane = lax.broadcasted_iota(jnp.int32, (META, TILE), 1)
        sub = lax.broadcasted_iota(jnp.int32, (META, TILE), 0)
        meta = jnp.zeros((META, TILE), jnp.float32)
        for s in range(count):
            for t in range(tiles):
                k, n = divmod(t, wide)
                keep = mask_refs[s][k, n] != 0

                @pl.when(keep & (place < cap))
                def _(s=s, k=k, n=n, place=place):
                    at = pl.multiple_of(place * TILE, TILE)
                    out_ref[pl.ds(at, TILE), :] = b_refs[s][k * TILE:(k + 1) * TILE, n * TILE:(n + 1) * TILE]

                place = place + keep.astype(jnp.int32)
                across = across + (across_refs[s][k, n] != 0).astype(jnp.int32)
                meta = jnp.where((lane == s * tiles + t) & keep, 1.0, meta)
        more = jnp.maximum(place, across) > cap
        meta = jnp.where(sub == 0, meta, jnp.where((sub == 1) & more, 1.0, 0.0))
        out_ref[cap * TILE:, :] = meta.astype(out_ref.dtype)

    return call(
        kernel, "pack_tiles",
        out_shape=jax.ShapeDtypeStruct((cap * TILE + META, TILE), shards[0].dtype),
        in_specs=[SMEM] * (2 * count) + [VMEM] * count,
        out_specs=VMEM,
    )(*masks, *across_masks, *shards)


def mask_tiles(amplitudes, mask):
    rows, cols = amplitudes.shape
    step = 2

    def kernel(mask_ref, a_ref, out_ref, token_ref):
        i = pl.program_id(0)
        token_ref[...] = jnp.zeros_like(token_ref)
        for r in range(step):
            for t in range(cols // TILE):
                spot = (slice(r * TILE, (r + 1) * TILE), slice(t * TILE, (t + 1) * TILE))
                keep = mask_ref[i * step + r, t] != 0

                @pl.when(keep)
                def _(spot=spot):
                    out_ref[spot] = a_ref[spot]

                @pl.when(jnp.logical_not(keep))
                def _(spot=spot):
                    out_ref[spot] = jnp.zeros((TILE, TILE), out_ref.dtype)

    block = pl.BlockSpec((step * TILE, cols), lambda i: (i, 0))
    return call(
        kernel, "mask_tiles", pl.CostEstimate(flops=0, bytes_accessed=4 * amplitudes.size, transcendentals=0),
        grid=(rows // TILE // step,),
        out_shape=(jax.ShapeDtypeStruct(amplitudes.shape, amplitudes.dtype), TOKEN),
        in_specs=[SMEM, block],
        out_specs=(block, pl.BlockSpec(TOKEN.shape, lambda i: (0, 0))),
    )(mask, amplitudes)


def shard_product(amps, picks, step, choices, tokens):
    rows, depth = amps[0].shape
    count = len(amps)
    height = sum(part.shape[0] for part in choices[0])
    cap = height - META
    wide = 2
    tiles = count * wide * depth // TILE
    word = 16
    parts = []
    for choice in choices:
        for part in choice:
            if not any(part is p for p in parts):
                parts.append(part)

    def kernel(picks_ref, *refs):
        token_refs, refs = refs[:len(tokens)], refs[len(tokens):]
        a_refs, refs = refs[:count], refs[count:]
        p_any, refs = refs[:len(parts)], refs[len(parts):]
        out_ref, coded_ref, token_ref, packed, wide_ref, sem = refs
        pick = picks_ref[step]
        token_ref[...] = sum(ref[...] for ref in token_refs)
        for number, choice in enumerate(choices):
            @pl.when(pick == number)
            def _(choice=choice):
                at = 0
                copies = []
                for part in choice:
                    index = [part is p for p in parts].index(True)
                    copies.append(pltpu.make_async_copy(
                        p_any[index], packed.at[pl.ds(at, part.shape[0])], sem.at[len(copies)]))
                    at += part.shape[0]
                for copy in copies:
                    copy.start()
                for copy in copies:
                    copy.wait()

        @pl.when(pick >= 0)
        def _():
            meta = packed[cap:, :].astype(jnp.float32)
            lane = lax.broadcasted_iota(jnp.int32, meta.shape, 1)
            sub = lax.broadcasted_iota(jnp.int32, meta.shape, 0)
            first = (sub == 0) & (meta != 0)
            bits = [
                jnp.sum(jnp.where(
                    first & (lane >= lo) & (lane < lo + word), jnp.left_shift(1, (lane - lo) & (word - 1)), 0))
                for lo in range(0, tiles, word)]
            token_ref[...] += jnp.where(sub == 1, meta, 0.0)[:token_ref.shape[0]]
            place = jnp.int32(0)
            for s in range(count):
                for t in range(s * tiles // count, (s + 1) * tiles // count):
                    k, n = divmod(t, wide)
                    keep = ((bits[t // word] >> (t % word)) & 1) != 0
                    at = pl.multiple_of(jnp.minimum(place * TILE, cap - TILE), TILE)
                    tile = packed[pl.ds(at, TILE), :]
                    wide_ref[k * TILE:(k + 1) * TILE, n * TILE:(n + 1) * TILE] = jnp.where(
                        keep, tile, jnp.zeros_like(tile))
                    place = place + keep.astype(jnp.int32)
                term = jnp.dot(
                    a_refs[s][...], wide_ref[s * depth:(s + 1) * depth, :], preferred_element_type=jnp.float32)
                if s:
                    out_ref[...] += term
                else:
                    out_ref[...] = term

        @pl.when((pick >= 0) & (picks_ref[STEPS + step] != 0))
        def _():
            encode(out_ref, coded_ref)

    return call(
        kernel, "shard_product",
        out_shape=(
            jax.ShapeDtypeStruct((rows, wide * TILE), jnp.float32),
            jax.ShapeDtypeStruct((coded_rows(rows), wide * TILE), jnp.int16),
            TOKEN),
        in_specs=[SMEM] + [VMEM] * (len(tokens) + count) + [ANY] * len(parts),
        out_specs=(VMEM, VMEM, VMEM),
        scratch_shapes=[
            pltpu.VMEM((height, TILE), amps[0].dtype),
            pltpu.VMEM((count * depth, wide * TILE), amps[0].dtype),
            pltpu.SemaphoreType.DMA((2,)),
        ],
    )(picks, *tokens, *amps, *map(in_hbm, parts))


def coded_rows(rows):
    return rows + rows // (16 // LOW) + META


def step_factors(exponent):
    power = BITS - 1 - TOP - exponent
    factors = []
    for part in (power // 2, power - power // 2):
        factor = jnp.ones(part.shape, jnp.float32)
        for bit in range(7):
            factor = factor * jnp.where((part >> bit) & 1 != 0, 2.0 ** (1 << bit), 1.0)
        factors.append(factor)
    return factors


def encode(sums_ref, coded_ref):
    rows, cols = sums_ref.shape
    groups = rows // GROUP
    largest = jnp.concatenate([
        jnp.max(jnp.abs(sums_ref[g * GROUP:(g + 1) * GROUP, :]), axis=0, keepdims=True) for g in range(groups)])
    rest = largest * 2.0 ** -TOP
    exponent = jnp.zeros(rest.shape, jnp.int32)
    for bit in (64, 32, 16, 8, 4, 2, 1):
        small = rest < 2.0 ** -bit
        rest = jnp.where(small, rest * 2.0 ** bit, rest)
        exponent = jnp.where(small, exponent - bit, exponent)
    one, two = step_factors(exponent)
    share = 16 // LOW
    block = rows // share
    for start in range(0, block, GROUP):
        low = jnp.zeros((GROUP, cols), jnp.int32)
        for part in range(share):
            at = part * block + start
            g = at // GROUP
            value = sums_ref[at:at + GROUP, :] * one[g:g + 1] * two[g:g + 1]
            value = jnp.minimum(jnp.round(value).astype(jnp.int32), (1 << (BITS - 1)) - 1)
            coded_ref[at:at + GROUP, :] = (value >> LOW).astype(jnp.int16)
            low = low | ((value & ((1 << LOW) - 1)) << (LOW * part))
        coded_ref[rows + start:rows + start + GROUP, :] = (low - 32768).astype(jnp.int16)
    coded_ref[rows + block:, :] = jnp.concatenate([exponent] * (META // groups)).astype(jnp.int16)


def add_coded(sums, coded):
    rows, cols = sums.shape
    groups = rows // GROUP
    share = 16 // LOW
    block = rows // share

    def kernel(sums_ref, coded_ref, out_ref, token_ref):
        token_ref[...] = jnp.zeros_like(token_ref)
        one, two = step_factors(coded_ref[rows + block:, :].astype(jnp.int32)[:groups])
        one, two = 1.0 / one, 1.0 / two
        for start in range(0, block, GROUP):
            low = coded_ref[rows + start:rows + start + GROUP, :].astype(jnp.int32) + 32768
            for part in range(share):
                at = part * block + start
                g = at // GROUP
                high = coded_ref[at:at + GROUP, :].astype(jnp.int32)
                value = (high << LOW) | ((low >> (LOW * part)) & ((1 << LOW) - 1))
                far = value.astype(jnp.float32) * one[g:g + 1] * two[g:g + 1]
                out_ref[at:at + GROUP, :] = (sums_ref[at:at + GROUP, :] + far).astype(out_ref.dtype)

    return call(
        kernel, "add_coded",
        out_shape=(jax.ShapeDtypeStruct(sums.shape, jnp.bfloat16), TOKEN),
        in_specs=[VMEM, VMEM],
        out_specs=(VMEM, VMEM),
    )(sums, coded)


def top_and_rest(one, two, at):
    def kernel(one_ref, two_ref, top_ref, rest_ref, sem):
        copies = [
            pltpu.make_async_copy(one_ref.at[pl.ds(0, at)], top_ref, sem.at[0]),
            pltpu.make_async_copy(two_ref.at[pl.ds(at, two.shape[0] - at)], rest_ref, sem.at[1])]
        for copy in copies:
            copy.start()
        for copy in copies:
            copy.wait()

    return call(
        kernel, "top_and_rest",
        out_shape=(
            jax.ShapeDtypeStruct((at, one.shape[1]), one.dtype),
            jax.ShapeDtypeStruct((two.shape[0] - at, two.shape[1]), two.dtype)),
        in_specs=[ANY, ANY],
        out_specs=(VMEM, VMEM),
        scratch_shapes=[pltpu.SemaphoreType.DMA((2,))],
    )(one, two)


Z, X, Y = 4, 2, 2
AXES = ("row", "col")


def device(z, x, y, c):
    return (z * X + x) * Y * 2 + y * 2 + c


def moves(to, home=True):
    pairs = []
    for z in range(Z):
        for x in range(X):
            for y in range(Y):
                if to(z, x) is not None:
                    c = z % 2 if home else 1 - z % 2
                    pairs.append((device(z, x, y, c), device(*to(z, x), y, c)))
    return pairs


def across_x(z, x):
    return z, 1 - x


def across_x_ends(z, x):
    return (z, 1 - x) if z in (0, 3) else None


def across_x_middle(z, x):
    return (z, 1 - x) if z in (1, 2) else None


def to_pair(z, x):
    return z ^ 1, x


def over_centre(z, x):
    return (3 - z, x) if z in (1, 2) else None


def outward(z, x):
    return (z ^ 1, x) if z in (1, 2) else None


def to_y(far, cores):
    pairs = []
    for z in range(Z):
        end = (z // 2) ^ int(far)
        for x in range(X):
            for c in cores(z):
                pairs.append((device(z, x, 1 - end, c), device(z, x, end, c)))
    return pairs


def both(z):
    return 0, 1


def home_core(z):
    return (z % 2,)


def other_core(z):
    return (1 - z % 2,)


FROM_OTHER_CORE = [
    (device(z, x, y, 1 - z % 2), device(z, x, y, z % 2)) for z in range(Z) for x in range(X) for y in range(Y)]
CORES = [(0, 1), (1, 0), (2, 3), (3, 2)]
CHIPS_Y = [(0, 2), (2, 0), (1, 3), (3, 1)]
CROSSWISE = [(0, 3), (3, 0), (1, 2), (2, 1)]


def sparse_ladder(amplitudes, integrals, amp_mask, int_mask):
    barrier = lax.optimization_barrier
    tiles = int_mask.size
    cap = 2 * tiles * 11 // 16
    half = cap * TILE // 2
    row, col = lax.axis_index("row"), lax.axis_index("col")
    z, x = row // X, row % X
    y, c = col // 2, col % 2
    is_end = ((z == 0) | (z == Z - 1)).astype(jnp.int32)
    home = z % 2 == c

    def move(value, pairs):
        return lax.ppermute(value, AXES, pairs)

    def after(*tokens):
        return lambda *shards: barrier((*shards, tokens))

    near = z // 2 == y
    picks = jnp.stack([
        jnp.where(home, 0, 1),
        jnp.where(home, is_end, -1),
        jnp.where(home, 0, 1),
        jnp.where(home, is_end, 2 + is_end),
        jnp.where(home, -1, is_end),
    ] + [jnp.where(near, s, 1 - s) for s in (0, 1, 0, 1, 1)]).astype(jnp.int32)

    other = move(integrals, FROM_OTHER_CORE)
    other_mask, across, other_across = [lax.ppermute(int_mask, "col", p) for p in (CORES, CHIPS_Y, CROSSWISE)]
    own = pack_tiles((integrals, other), (int_mask, other_mask), (across, other_across), cap)
    own, picks, amplitudes_now = barrier((own, picks, amplitudes))

    masked, masked_token = mask_tiles(amplitudes_now, amp_mask)
    amps = (masked, lax.ppermute(masked, "col", CORES))
    one, centre, own_x, tokens = after(masked_token)(
        move(own, moves(to_pair)), move(own, moves(over_centre)), move(own, moves(across_x)))

    a_sum, a_coded, token = shard_product(amps, picks, 0, [[own], [one]], tokens)
    a_far = move(a_coded, to_y(False, both))
    two_end, two_mid, one_x, own_x, tokens = after(token)(
        move(centre, moves(outward, False)), move(one, moves(over_centre, False)), move(one, moves(across_x, False)),
        own_x)

    c_sum, c_coded, token = shard_product(amps, picks, 1, [[two_mid], [two_end]], tokens)
    c_far = move(c_coded, to_y(True, home_core))
    b_sum, b_coded, token = shard_product(amps, picks, 2, [[own_x], [one_x]], (token,))
    b_far = move(b_coded, to_y(False, both))
    a_both, a_token = add_coded(a_sum, a_far)
    three_end, three_mid_x, two_x_end, two_x_mid, tokens = after(token, a_token)(
        move(two_mid, moves(outward)), move(own_x, moves(over_centre)),
        move(two_end, moves(across_x_ends)), move(two_mid, moves(across_x_middle)))

    d_sum, d_coded, token = shard_product(
        amps, picks, 3, [[two_x_mid], [two_x_end], [centre], [three_end]], tokens)
    top, rest = top_and_rest(three_end, two_x_mid, half)
    c_both, c_token = add_coded(c_sum, c_far)
    three_x, three_x_rest, tokens = after(token, c_token)(
        move(top, moves(across_x_ends, False)), move(rest, moves(outward)))

    d_far = move(d_coded, to_y(True, both))
    e_sum, e_coded, token = shard_product(amps, picks, 4, [[three_mid_x], [three_x, three_x_rest]], tokens)
    e_far = move(e_coded, to_y(True, other_core))
    excess = token + lax.ppermute(token, "col", CORES)
    b_both, _ = add_coded(b_sum, b_far)
    d_both, _ = add_coded(d_sum, d_far)
    e_both, _ = add_coded(e_sum, e_far)

    def finish():
        mine = jnp.where(near, a_both, jnp.where(home, c_both, d_both))
        rest = jnp.where(near, b_both, jnp.where(home, d_both, e_both))
        return jnp.concatenate([jnp.where(x == 0, mine, rest), jnp.where(x == 0, rest, mine)], axis=1)

    return lax.cond(
        jnp.max(excess) > 0, lambda: dense_ladder(amplitudes, integrals, amp_mask, int_mask), finish)


def solution(mesh):
    in_specs = (P("row", "col"), P("col", "row"), P("row", "col"), P("col", "row"))
    out_specs = P("row", "col")
    here = dict(mesh.shape)
    per_device = sparse_ladder if here == {"row": Z * X, "col": Y * 2} else dense_ladder
    return jax.shard_map(
        per_device, mesh=mesh, in_specs=in_specs, out_specs=out_specs, check_vma=False
    )
```

```python
import jax
import jax.numpy as jnp
from jax import lax
from jax.experimental import pallas as pl
from jax.experimental.pallas import tpu as pltpu
from jax.sharding import PartitionSpec as P

TILE = 128
VMEM_LIMIT = 12 * 1024 * 1024


def expand(mask):
    spread = jnp.repeat(jnp.repeat(mask, TILE, axis=0), TILE, axis=1)
    return spread.astype(jnp.bfloat16)


def dense_ladder(amplitudes, integrals, amp_mask, int_mask):
    rows, cols = lax.axis_size("row"), lax.axis_size("col")
    row, col = lax.axis_index("row"), lax.axis_index("col")
    sparse_amp = amplitudes * expand(amp_mask)
    sparse_int = integrals * expand(int_mask)
    width = integrals.shape[1]
    share = rows * width // cols
    sums = jnp.zeros((amplitudes.shape[0], rows * width), jnp.float32)
    for step in range(rows):
        shard = lax.ppermute(sparse_int, "row", [((r + step) % rows, r) for r in range(rows)]) if step else sparse_int
        part = jnp.dot(sparse_amp, shard, preferred_element_type=jnp.float32)
        sums = lax.dynamic_update_slice(sums, part, (0, (row + step) % rows * width))
    ladder = lax.dynamic_slice(sums, (0, col * share), (sums.shape[0], share))
    for step in range(1, cols):
        part = lax.dynamic_slice(sums, (0, (col + step) % cols * share), (sums.shape[0], share))
        ladder = ladder + lax.ppermute(part, "col", [(c, (c + step) % cols) for c in range(cols)])
    return ladder.astype(jnp.bfloat16)


TOKEN = jax.ShapeDtypeStruct((8, TILE), jnp.float32)
LIGHT = pl.CostEstimate(flops=1, bytes_accessed=1, transcendentals=0)
STEPS = 5
TOP = 12
LOW = 4
BITS = 16 + LOW
GROUP = 128
META = 16


def in_hbm(array):
    return pltpu.with_memory_space_constraint(array, pltpu.HBM)


def call(kernel, name, cost=LIGHT, **kwargs):
    return pl.pallas_call(
        kernel,
        compiler_params=pltpu.CompilerParams(vmem_limit_bytes=VMEM_LIMIT),
        cost_estimate=cost,
        name=name,
        **kwargs,
    )


VMEM = pl.BlockSpec(memory_space=pltpu.VMEM)
SMEM = pl.BlockSpec(memory_space=pltpu.SMEM)
ANY = pl.BlockSpec(memory_space=pl.ANY)


def pack_tiles(shards, masks, cap):
    wide = shards[0].shape[1] // TILE
    tiles = masks[0].size
    count = len(shards)

    def kernel(*refs):
        mask_refs, b_refs, out_ref = refs[:count], refs[count:-1], refs[-1]
        place = jnp.int32(0)
        lane = lax.broadcasted_iota(jnp.int32, (META, TILE), 1)
        sub = lax.broadcasted_iota(jnp.int32, (META, TILE), 0)
        meta = jnp.zeros((META, TILE), jnp.float32)
        for s in range(count):
            for t in range(tiles):
                k, n = divmod(t, wide)
                keep = mask_refs[s][n, k] != 0

                @pl.when(keep & (place < cap))
                def _(s=s, k=k, n=n, place=place):
                    at = pl.multiple_of(place * TILE, TILE)
                    out_ref[pl.ds(at, TILE), :] = b_refs[s][k * TILE:(k + 1) * TILE, n * TILE:(n + 1) * TILE]

                place = place + keep.astype(jnp.int32)
                meta = jnp.where((lane == s * tiles + t) & keep, 1.0, meta)
        meta = jnp.where(sub == 0, meta, jnp.where((sub == 1) & (place > cap), 1.0, 0.0))
        out_ref[cap * TILE:, :] = meta.astype(out_ref.dtype)

    return call(
        kernel, "pack_tiles",
        out_shape=jax.ShapeDtypeStruct((cap * TILE + META, TILE), shards[0].dtype),
        in_specs=[SMEM] * count + [VMEM] * count,
        out_specs=VMEM,
    )(*masks, *shards)


def mask_tiles(amplitudes, mask):
    rows, cols = amplitudes.shape

    def kernel(mask_ref, a_any, out_ref, token_ref, sem):
        token_ref[...] = jnp.zeros_like(token_ref)
        copies = [
            pltpu.make_async_copy(a_any.at[pl.ds(at, TILE)], out_ref.at[pl.ds(at, TILE)], sem.at[at // TILE])
            for at in range(0, rows, TILE)]
        for copy in copies:
            copy.start()
        for r in range(rows // TILE):
            copies[r].wait()
            for t in range(cols // TILE):
                @pl.when(mask_ref[r, t] == 0)
                def _(r=r, t=t):
                    out_ref[r * TILE:(r + 1) * TILE, t * TILE:(t + 1) * TILE] = jnp.zeros((TILE, TILE), out_ref.dtype)

    return call(
        kernel, "mask_tiles",
        out_shape=(jax.ShapeDtypeStruct(amplitudes.shape, amplitudes.dtype), TOKEN),
        in_specs=[SMEM, ANY],
        out_specs=(VMEM, VMEM),
        scratch_shapes=[pltpu.SemaphoreType.DMA((rows // TILE,))],
    )(mask, amplitudes)


def shard_product(amps, picks, step, choices, tokens):
    rows, depth = amps[0].shape
    count = len(amps)
    height = sum(part.shape[0] for part in choices[0])
    cap = height - META
    wide = 2
    tiles = count * wide * depth // TILE
    word = 16
    parts = []
    for choice in choices:
        for part in choice:
            if not any(part is p for p in parts):
                parts.append(part)

    def kernel(picks_ref, *refs):
        token_refs, refs = refs[:len(tokens)], refs[len(tokens):]
        a_refs, refs = refs[:count], refs[count:]
        p_any, refs = refs[:len(parts)], refs[len(parts):]
        out_ref, coded_ref, token_ref, packed, wide_ref, sem = refs
        pick = picks_ref[step]
        token_ref[...] = sum(ref[...] for ref in token_refs)
        for number, choice in enumerate(choices):
            @pl.when(pick == number)
            def _(choice=choice):
                at = 0
                copies = []
                for part in choice:
                    index = [part is p for p in parts].index(True)
                    copies.append(pltpu.make_async_copy(
                        p_any[index], packed.at[pl.ds(at, part.shape[0])], sem.at[len(copies)]))
                    at += part.shape[0]
                for copy in copies:
                    copy.start()
                for copy in copies:
                    copy.wait()

        @pl.when(pick >= 0)
        def _():
            meta = packed[cap:, :].astype(jnp.float32)
            lane = lax.broadcasted_iota(jnp.int32, meta.shape, 1)
            sub = lax.broadcasted_iota(jnp.int32, meta.shape, 0)
            first = (sub == 0) & (meta != 0)
            bits = [
                jnp.sum(jnp.where(
                    first & (lane >= lo) & (lane < lo + word), jnp.left_shift(1, (lane - lo) & (word - 1)), 0))
                for lo in range(0, tiles, word)]
            token_ref[...] += jnp.where(sub == 1, meta, 0.0)[:token_ref.shape[0]]
            place = jnp.int32(0)
            for s in range(count):
                for t in range(s * tiles // count, (s + 1) * tiles // count):
                    k, n = divmod(t, wide)
                    keep = ((bits[t // word] >> (t % word)) & 1) != 0
                    at = pl.multiple_of(jnp.minimum(place * TILE, cap - TILE), TILE)
                    tile = packed[pl.ds(at, TILE), :]
                    wide_ref[k * TILE:(k + 1) * TILE, n * TILE:(n + 1) * TILE] = jnp.where(
                        keep, tile, jnp.zeros_like(tile))
                    place = place + keep.astype(jnp.int32)
                term = jnp.dot(
                    a_refs[s][...], wide_ref[s * depth:(s + 1) * depth, :], preferred_element_type=jnp.float32)
                if s:
                    out_ref[...] += term
                else:
                    out_ref[...] = term

        @pl.when((pick >= 0) & (picks_ref[STEPS + step] != 0))
        def _():
            encode(out_ref, coded_ref)

    return call(
        kernel, "shard_product",
        out_shape=(
            jax.ShapeDtypeStruct((rows, wide * TILE), jnp.float32),
            jax.ShapeDtypeStruct((coded_rows(rows), wide * TILE), jnp.int16),
            TOKEN),
        in_specs=[SMEM] + [VMEM] * (len(tokens) + count) + [ANY] * len(parts),
        out_specs=(VMEM, VMEM, VMEM),
        scratch_shapes=[
            pltpu.VMEM((height, TILE), amps[0].dtype),
            pltpu.VMEM((count * depth, wide * TILE), amps[0].dtype),
            pltpu.SemaphoreType.DMA((2,)),
        ],
    )(picks, *tokens, *amps, *map(in_hbm, parts))


def coded_rows(rows):
    return rows + rows // (16 // LOW) + META


def step_factors(exponent):
    power = BITS - 1 - TOP - exponent
    factors = []
    for part in (power // 2, power - power // 2):
        factor = jnp.ones(part.shape, jnp.float32)
        for bit in range(7):
            factor = factor * jnp.where((part >> bit) & 1 != 0, 2.0 ** (1 << bit), 1.0)
        factors.append(factor)
    return factors


def encode(sums_ref, coded_ref):
    rows, cols = sums_ref.shape
    groups = rows // GROUP
    largest = jnp.concatenate([
        jnp.max(jnp.abs(sums_ref[g * GROUP:(g + 1) * GROUP, :]), axis=0, keepdims=True) for g in range(groups)])
    rest = largest * 2.0 ** -TOP
    exponent = jnp.zeros(rest.shape, jnp.int32)
    for bit in (64, 32, 16, 8, 4, 2, 1):
        small = rest < 2.0 ** -bit
        rest = jnp.where(small, rest * 2.0 ** bit, rest)
        exponent = jnp.where(small, exponent - bit, exponent)
    one, two = step_factors(exponent)
    share = 16 // LOW
    block = rows // share
    for start in range(0, block, GROUP):
        low = jnp.zeros((GROUP, cols), jnp.int32)
        for part in range(share):
            at = part * block + start
            g = at // GROUP
            value = sums_ref[at:at + GROUP, :] * one[g:g + 1] * two[g:g + 1]
            value = jnp.minimum(jnp.round(value).astype(jnp.int32), (1 << (BITS - 1)) - 1)
            coded_ref[at:at + GROUP, :] = (value >> LOW).astype(jnp.int16)
            low = low | ((value & ((1 << LOW) - 1)) << (LOW * part))
        coded_ref[rows + start:rows + start + GROUP, :] = (low - 32768).astype(jnp.int16)
    coded_ref[rows + block:, :] = jnp.concatenate([exponent] * (META // groups)).astype(jnp.int16)


def decode(coded_ref, rows, put):
    groups = rows // GROUP
    share = 16 // LOW
    block = rows // share
    one, two = step_factors(coded_ref[rows + block:, :].astype(jnp.int32)[:groups])
    one, two = 1.0 / one, 1.0 / two
    for start in range(0, block, GROUP):
        low = coded_ref[rows + start:rows + start + GROUP, :].astype(jnp.int32) + 32768
        for part in range(share):
            at = part * block + start
            g = at // GROUP
            high = coded_ref[at:at + GROUP, :].astype(jnp.int32)
            value = (high << LOW) | ((low >> (LOW * part)) & ((1 << LOW) - 1))
            put(at, value.astype(jnp.float32) * one[g:g + 1] * two[g:g + 1])


def add_coded(sums, coded):
    def kernel(sums_ref, coded_ref, out_ref, token_ref):
        token_ref[...] = jnp.zeros_like(token_ref)

        def put(at, far):
            out_ref[at:at + GROUP, :] = (sums_ref[at:at + GROUP, :] + far).astype(out_ref.dtype)

        decode(coded_ref, sums.shape[0], put)

    return call(
        kernel, "add_coded",
        out_shape=(jax.ShapeDtypeStruct(sums.shape, jnp.bfloat16), TOKEN),
        in_specs=[VMEM, VMEM],
        out_specs=(VMEM, VMEM),
    )(sums, coded)


def lay_out(place, mine, rest):
    rows, width = mine[0].shape
    arrays = []
    for choice in jax.tree.leaves((mine, rest)):
        if not any(choice is array for array in arrays):
            arrays.append(choice)

    def index(array):
        return [array is known for known in arrays].index(True)

    def kernel(place_ref, *refs):
        ins, out_ref = refs[:len(arrays)], refs[-1]
        for x in range(2):
            own, other = slice(x * width, (x + 1) * width), slice((1 - x) * width, (2 - x) * width)
            for number in range(len(mine)):
                @pl.when((place_ref[0] == number) & (place_ref[1] == x))
                def _(own=own, other=other, number=number):
                    out_ref[:, own] = ins[index(mine[number])][...]
                    if isinstance(rest[number], tuple):
                        sums_ref, coded_ref = [ins[index(array)] for array in rest[number]]

                        def put(at, far):
                            out_ref[at:at + GROUP, other] = (sums_ref[at:at + GROUP, :] + far).astype(out_ref.dtype)

                        decode(coded_ref, rows, put)
                    else:
                        out_ref[:, other] = ins[index(rest[number])][...]

    return call(
        kernel, "lay_out",
        out_shape=jax.ShapeDtypeStruct((rows, 2 * width), jnp.bfloat16),
        in_specs=[SMEM] + [VMEM] * len(arrays),
        out_specs=VMEM,
    )(place, *arrays)


def top_and_rest(one, two, at):
    def kernel(one_ref, two_ref, top_ref, rest_ref, sem):
        copies = [
            pltpu.make_async_copy(one_ref.at[pl.ds(0, at)], top_ref, sem.at[0]),
            pltpu.make_async_copy(two_ref.at[pl.ds(at, two.shape[0] - at)], rest_ref, sem.at[1])]
        for copy in copies:
            copy.start()
        for copy in copies:
            copy.wait()

    return call(
        kernel, "top_and_rest",
        out_shape=(
            jax.ShapeDtypeStruct((at, one.shape[1]), one.dtype),
            jax.ShapeDtypeStruct((two.shape[0] - at, two.shape[1]), two.dtype)),
        in_specs=[ANY, ANY],
        out_specs=(VMEM, VMEM),
        scratch_shapes=[pltpu.SemaphoreType.DMA((2,))],
    )(one, two)


Z, X, Y = 4, 2, 2
AXES = ("row", "col")


def device(z, x, y, c):
    return (z * X + x) * Y * 2 + y * 2 + c


def moves(to, home=True):
    pairs = []
    for z in range(Z):
        for x in range(X):
            for y in range(Y):
                if to(z, x) is not None:
                    c = z % 2 if home else 1 - z % 2
                    pairs.append((device(z, x, y, c), device(*to(z, x), y, c)))
    return pairs


def across_x(z, x):
    return z, 1 - x


def across_x_ends(z, x):
    return (z, 1 - x) if z in (0, 3) else None


def across_x_middle(z, x):
    return (z, 1 - x) if z in (1, 2) else None


def to_pair(z, x):
    return z ^ 1, x


def over_centre(z, x):
    return (3 - z, x) if z in (1, 2) else None


def outward(z, x):
    return (z ^ 1, x) if z in (1, 2) else None


def to_y(far, cores):
    pairs = []
    for z in range(Z):
        end = (z // 2) ^ int(far)
        for x in range(X):
            for c in cores(z):
                pairs.append((device(z, x, 1 - end, c), device(z, x, end, c)))
    return pairs


def both(z):
    return 0, 1


def home_core(z):
    return (z % 2,)


def other_core(z):
    return (1 - z % 2,)


FROM_OTHER_CORE = [
    (device(z, x, y, 1 - z % 2), device(z, x, y, z % 2)) for z in range(Z) for x in range(X) for y in range(Y)]
CORES = [(0, 1), (1, 0), (2, 3), (3, 2)]
CHIPS_Y = [(0, 2), (2, 0), (1, 3), (3, 1)]


def sparse_ladder(amplitudes, integrals, amp_mask, int_mask):
    barrier = lax.optimization_barrier
    tiles = int_mask.size
    cap = 2 * tiles * 11 // 16
    half = cap * TILE // 2
    row, col = lax.axis_index("row"), lax.axis_index("col")
    z, x = row // X, row % X
    y, c = col // 2, col % 2
    is_end = ((z == 0) | (z == Z - 1)).astype(jnp.int32)
    home = z % 2 == c

    def move(value, pairs):
        return lax.ppermute(value, AXES, pairs)

    def after(*tokens):
        return lambda *shards: barrier((*shards, tokens))

    near = z // 2 == y
    picks = jnp.stack([
        jnp.where(home, 0, 1),
        jnp.where(home, is_end, -1),
        jnp.where(home, 0, 1),
        jnp.where(home, is_end, 2 + is_end),
        jnp.where(home, -1, is_end),
    ] + [jnp.where(near, s, 1 - s) for s in (0, 1, 0, 1, 1)]).astype(jnp.int32)

    other = move(integrals, FROM_OTHER_CORE)
    other_mask = lax.ppermute(int_mask.T, "col", CORES)
    own = pack_tiles((integrals, other), (int_mask.T, other_mask), cap)
    own, picks, amplitudes_now = barrier((own, picks, amplitudes))

    masked, masked_token = mask_tiles(amplitudes_now, amp_mask)
    amps = (masked, lax.ppermute(masked, "col", CORES))
    one, centre, own_x, tokens = after(masked_token)(
        move(own, moves(to_pair)), move(own, moves(over_centre)), move(own, moves(across_x)))

    a_sum, a_coded, token = shard_product(amps, picks, 0, [[own], [one]], tokens)
    a_far = move(a_coded, to_y(False, both))
    two_end, two_mid, one_x, own_x, tokens = after(token)(
        move(centre, moves(outward, False)), move(one, moves(over_centre, False)), move(one, moves(across_x, False)),
        own_x)

    c_sum, c_coded, token = shard_product(amps, picks, 1, [[two_mid], [two_end]], tokens)
    c_far = move(c_coded, to_y(True, home_core))
    b_sum, b_coded, token = shard_product(amps, picks, 2, [[own_x], [one_x]], (token,))
    a_both, a_token = add_coded(a_sum, a_far)
    three_end, three_mid_x, two_x_end, two_x_mid, tokens = after(token, a_token)(
        move(two_mid, moves(outward)), move(own_x, moves(over_centre)),
        move(two_end, moves(across_x_ends)), move(two_mid, moves(across_x_middle)))

    d_sum, d_coded, token = shard_product(
        amps, picks, 3, [[two_x_mid], [two_x_end], [centre], [three_end]], tokens)
    b_coded, token = barrier((b_coded, token))
    b_far = move(b_coded, to_y(False, both))
    top, rest = top_and_rest(three_end, two_x_mid, half)
    c_both, c_token = add_coded(c_sum, c_far)
    three_x, three_x_rest, tokens = after(token, c_token)(
        move(top, moves(across_x_ends, False)), move(rest, moves(outward)))

    d_far = move(d_coded, to_y(True, both))
    e_sum, e_coded, token = shard_product(amps, picks, 4, [[three_mid_x], [three_x, three_x_rest]], tokens)
    e_far = move(e_coded, to_y(True, other_core))
    b_both, b_token = add_coded(b_sum, b_far)
    d_both, d_token = add_coded(d_sum, d_far)
    excess = token + lax.ppermute(token, "col", CHIPS_Y)
    excess, b_both, d_both = barrier((excess, b_both, d_both))
    excess = excess + lax.ppermute(excess, "col", CORES)
    place = jnp.stack([jnp.where(near, 0, jnp.where(home, 1, 2)), x]).astype(jnp.int32)

    def finish():
        return lay_out(place, (a_both, c_both, d_both), (b_both, d_both, (e_sum, e_far)))

    return lax.cond(
        jnp.max(excess) > 0, lambda: dense_ladder(amplitudes, integrals, amp_mask, int_mask), finish)


def solution(mesh):
    in_specs = (P("row", "col"), P("col", "row"), P("row", "col"), P("col", "row"))
    out_specs = P("row", "col")
    here = dict(mesh.shape)
    per_device = sparse_ladder if here == {"row": Z * X, "col": Y * 2} else dense_ladder
    return jax.shard_map(
        per_device, mesh=mesh, in_specs=in_specs, out_specs=out_specs, check_vma=False
    )
```

```python
import jax
import jax.numpy as jnp
from jax import lax
from jax.experimental import pallas as pl
from jax.experimental.pallas import tpu as pltpu
from jax.sharding import PartitionSpec as P

TILE = 128
VMEM_LIMIT = 12 * 1024 * 1024


def expand(mask):
    spread = jnp.repeat(jnp.repeat(mask, TILE, axis=0), TILE, axis=1)
    return spread.astype(jnp.bfloat16)


def dense_ladder(amplitudes, integrals, amp_mask, int_mask):
    rows, cols = lax.axis_size("row"), lax.axis_size("col")
    row, col = lax.axis_index("row"), lax.axis_index("col")
    sparse_amp = amplitudes * expand(amp_mask)
    sparse_int = integrals * expand(int_mask)
    width = integrals.shape[1]
    share = rows * width // cols
    sums = jnp.zeros((amplitudes.shape[0], rows * width), jnp.float32)
    for step in range(rows):
        shard = lax.ppermute(sparse_int, "row", [((r + step) % rows, r) for r in range(rows)]) if step else sparse_int
        part = jnp.dot(sparse_amp, shard, preferred_element_type=jnp.float32)
        sums = lax.dynamic_update_slice(sums, part, (0, (row + step) % rows * width))
    ladder = lax.dynamic_slice(sums, (0, col * share), (sums.shape[0], share))
    for step in range(1, cols):
        part = lax.dynamic_slice(sums, (0, (col + step) % cols * share), (sums.shape[0], share))
        ladder = ladder + lax.ppermute(part, "col", [(c, (c + step) % cols) for c in range(cols)])
    return ladder.astype(jnp.bfloat16)


TOKEN = jax.ShapeDtypeStruct((8, TILE), jnp.float32)
LIGHT = pl.CostEstimate(flops=1, bytes_accessed=1, transcendentals=0)
STEPS = 5
TOP = 12
LOW = 4
BITS = 16 + LOW
GROUP = 128
META = 16


def in_hbm(array):
    return pltpu.with_memory_space_constraint(array, pltpu.HBM)


def call(kernel, name, cost=LIGHT, **kwargs):
    return pl.pallas_call(
        kernel,
        compiler_params=pltpu.CompilerParams(vmem_limit_bytes=VMEM_LIMIT),
        cost_estimate=cost,
        name=name,
        **kwargs,
    )


VMEM = pl.BlockSpec(memory_space=pltpu.VMEM)
SMEM = pl.BlockSpec(memory_space=pltpu.SMEM)
ANY = pl.BlockSpec(memory_space=pl.ANY)


def pack_tiles(shards, masks, swap, cap):
    wide = shards[0].shape[1] // TILE
    tiles = masks[0].size
    count = len(shards)

    def kernel(swap_ref, *refs):
        mask_refs, b_refs, out_ref = refs[:count], refs[count:-1], refs[-1]

        @pl.when(swap_ref[0] == 0)
        def _():
            pack(mask_refs, b_refs, out_ref)

        @pl.when(swap_ref[0] != 0)
        def _():
            pack(mask_refs[::-1], b_refs[::-1], out_ref)

    def pack(mask_refs, b_refs, out_ref):
        place = jnp.int32(0)
        lane = lax.broadcasted_iota(jnp.int32, (META, TILE), 1)
        sub = lax.broadcasted_iota(jnp.int32, (META, TILE), 0)
        meta = jnp.zeros((META, TILE), jnp.float32)
        for s in range(count):
            for t in range(tiles):
                k, n = divmod(t, wide)
                keep = mask_refs[s][n, k] != 0

                @pl.when(keep & (place < cap))
                def _(s=s, k=k, n=n, place=place):
                    at = pl.multiple_of(place * TILE, TILE)
                    out_ref[pl.ds(at, TILE), :] = b_refs[s][k * TILE:(k + 1) * TILE, n * TILE:(n + 1) * TILE]

                place = place + keep.astype(jnp.int32)
                meta = jnp.where((lane == s * tiles + t) & keep, 1.0, meta)
        meta = jnp.where(sub == 0, meta, jnp.where((sub == 1) & (place > cap), 1.0, 0.0))
        out_ref[cap * TILE:, :] = meta.astype(out_ref.dtype)

    return call(
        kernel, "pack_tiles",
        out_shape=jax.ShapeDtypeStruct((cap * TILE + META, TILE), shards[0].dtype),
        in_specs=[SMEM] * (1 + count) + [VMEM] * count,
        out_specs=VMEM,
    )(swap, *masks, *shards)


def mask_tiles(amplitudes, mask):
    rows, cols = amplitudes.shape

    def kernel(mask_ref, a_any, out_ref, token_ref, sem):
        token_ref[...] = jnp.zeros_like(token_ref)
        copies = [
            pltpu.make_async_copy(a_any.at[pl.ds(at, TILE)], out_ref.at[pl.ds(at, TILE)], sem.at[at // TILE])
            for at in range(0, rows, TILE)]
        for copy in copies:
            copy.start()
        for r in range(rows // TILE):
            copies[r].wait()
            for t in range(cols // TILE):
                @pl.when(mask_ref[r, t] == 0)
                def _(r=r, t=t):
                    out_ref[r * TILE:(r + 1) * TILE, t * TILE:(t + 1) * TILE] = jnp.zeros((TILE, TILE), out_ref.dtype)

    return call(
        kernel, "mask_tiles",
        out_shape=(jax.ShapeDtypeStruct(amplitudes.shape, amplitudes.dtype), TOKEN),
        in_specs=[SMEM, ANY],
        out_specs=(VMEM, VMEM),
        scratch_shapes=[pltpu.SemaphoreType.DMA((rows // TILE,))],
    )(mask, amplitudes)


def shard_product(amps, picks, step, choices, tokens, before=None, held=in_hbm):
    rows, depth = amps[0].shape
    count = len(amps)
    height = sum(part.shape[0] for part in choices[0])
    cap = height - META
    wide = 2
    tiles = count * wide * depth // TILE
    word = 16
    first_row = 0 if before is None else before.shape[0]
    parts = []
    for choice in choices:
        for part in choice:
            if not any(part is p for p in parts):
                parts.append(part)

    def kernel(picks_ref, *refs):
        if first_row:
            before_ref, refs = refs[0], refs[1:]
        token_refs, refs = refs[:len(tokens)], refs[len(tokens):]
        a_refs, refs = refs[:count], refs[count:]
        p_any, refs = refs[:len(parts)], refs[len(parts):]
        out_ref, coded_ref, token_ref, packed, wide_ref, sem = refs
        pick = picks_ref[step]
        token_ref[...] = sum(ref[...] for ref in token_refs)
        for number, choice in enumerate(choices):
            @pl.when(pick == number)
            def _(choice=choice):
                at = 0
                copies = []
                for part in choice:
                    index = [part is p for p in parts].index(True)
                    copies.append(pltpu.make_async_copy(
                        p_any[index], packed.at[pl.ds(at, part.shape[0])], sem.at[len(copies)]))
                    at += part.shape[0]
                for copy in copies:
                    copy.start()
                for copy in copies:
                    copy.wait()

        @pl.when(pick >= 0)
        def _():
            meta = packed[cap:, :].astype(jnp.float32)
            lane = lax.broadcasted_iota(jnp.int32, meta.shape, 1)
            sub = lax.broadcasted_iota(jnp.int32, meta.shape, 0)
            first = (sub == 0) & (meta != 0)
            bits = [
                jnp.sum(jnp.where(
                    first & (lane >= lo) & (lane < lo + word), jnp.left_shift(1, (lane - lo) & (word - 1)), 0))
                for lo in range(0, tiles, word)]
            token_ref[...] += jnp.where(sub == 1, meta, 0.0)[:token_ref.shape[0]]
            place = jnp.int32(0)
            for s in range(count):
                for t in range(s * tiles // count, (s + 1) * tiles // count):
                    k, n = divmod(t, wide)
                    keep = ((bits[t // word] >> (t % word)) & 1) != 0
                    at = pl.multiple_of(jnp.minimum(place * TILE, cap - TILE), TILE)
                    tile = packed[pl.ds(at, TILE), :]
                    wide_ref[k * TILE:(k + 1) * TILE, n * TILE:(n + 1) * TILE] = jnp.where(
                        keep, tile, jnp.zeros_like(tile))
                    place = place + keep.astype(jnp.int32)
                term = jnp.dot(
                    a_refs[s][...], wide_ref[s * depth:(s + 1) * depth, :], preferred_element_type=jnp.float32)
                if s:
                    out_ref[...] += term
                else:
                    out_ref[...] = term

        @pl.when((pick >= 0) & (picks_ref[STEPS + step] != 0))
        def _():
            if first_row:
                coded_ref[:first_row, :] = before_ref[...]
            encode(out_ref, coded_ref, first_row)

    return call(
        kernel, "shard_product",
        out_shape=(
            jax.ShapeDtypeStruct((rows, wide * TILE), jnp.float32),
            jax.ShapeDtypeStruct((first_row + coded_rows(rows), wide * TILE), jnp.int16),
            TOKEN),
        in_specs=[SMEM] + [VMEM] * (bool(first_row) + len(tokens) + count) + [ANY] * len(parts),
        out_specs=(VMEM, VMEM, VMEM),
        scratch_shapes=[
            pltpu.VMEM((height, TILE), amps[0].dtype),
            pltpu.VMEM((count * depth, wide * TILE), amps[0].dtype),
            pltpu.SemaphoreType.DMA((2,)),
        ],
    )(picks, *([before] if first_row else []), *tokens, *amps, *map(held, parts))


def coded_rows(rows):
    return rows + rows // (16 // LOW) + META


def step_factors(exponent):
    power = BITS - 1 - TOP - exponent
    factors = []
    for part in (power // 2, power - power // 2):
        factor = jnp.ones(part.shape, jnp.float32)
        for bit in range(7):
            factor = factor * jnp.where((part >> bit) & 1 != 0, 2.0 ** (1 << bit), 1.0)
        factors.append(factor)
    return factors


def encode(sums_ref, coded_ref, first_row):
    rows, cols = sums_ref.shape
    groups = rows // GROUP
    largest = jnp.concatenate([
        jnp.max(jnp.abs(sums_ref[g * GROUP:(g + 1) * GROUP, :]), axis=0, keepdims=True) for g in range(groups)])
    rest = largest * 2.0 ** -TOP
    exponent = jnp.zeros(rest.shape, jnp.int32)
    for bit in (64, 32, 16, 8, 4, 2, 1):
        small = rest < 2.0 ** -bit
        rest = jnp.where(small, rest * 2.0 ** bit, rest)
        exponent = jnp.where(small, exponent - bit, exponent)
    one, two = step_factors(exponent)
    share = 16 // LOW
    block = rows // share
    for start in range(0, block, GROUP):
        low = jnp.zeros((GROUP, cols), jnp.int32)
        for part in range(share):
            at = part * block + start
            g = at // GROUP
            value = sums_ref[at:at + GROUP, :] * one[g:g + 1] * two[g:g + 1]
            value = jnp.minimum(jnp.round(value).astype(jnp.int32), (1 << (BITS - 1)) - 1)
            coded_ref[first_row + at:first_row + at + GROUP, :] = (value >> LOW).astype(jnp.int16)
            low = low | ((value & ((1 << LOW) - 1)) << (LOW * part))
        low_at = first_row + rows + start
        coded_ref[low_at:low_at + GROUP, :] = (low - 32768).astype(jnp.int16)
    coded_ref[first_row + rows + block:, :] = jnp.concatenate([exponent] * (META // groups)).astype(jnp.int16)


def decode(coded_ref, rows, put, first_row=0):
    groups = rows // GROUP
    share = 16 // LOW
    block = rows // share
    exponent_at = first_row + rows + block
    one, two = step_factors(coded_ref[exponent_at:exponent_at + META, :].astype(jnp.int32)[:groups])
    one, two = 1.0 / one, 1.0 / two
    for start in range(0, block, GROUP):
        low_at = first_row + rows + start
        low = coded_ref[low_at:low_at + GROUP, :].astype(jnp.int32) + 32768
        for part in range(share):
            at = part * block + start
            g = at // GROUP
            high = coded_ref[first_row + at:first_row + at + GROUP, :].astype(jnp.int32)
            value = (high << LOW) | ((low >> (LOW * part)) & ((1 << LOW) - 1))
            put(at, value.astype(jnp.float32) * one[g:g + 1] * two[g:g + 1])


def add_coded(sums, coded):
    rows = sums[0].shape[0]
    count = len(sums)

    def kernel(*refs):
        sums_refs, coded_ref, out_refs, token_ref = refs[:count], refs[count], refs[count + 1:-1], refs[-1]
        token_ref[...] = jnp.zeros_like(token_ref)
        for number in range(count):
            def put(at, far, number=number):
                out_refs[number][at:at + GROUP, :] = (
                    sums_refs[number][at:at + GROUP, :] + far).astype(jnp.bfloat16)

            decode(coded_ref, rows, put, number * coded_rows(rows))

    return call(
        kernel, "add_coded",
        out_shape=tuple(jax.ShapeDtypeStruct(part.shape, jnp.bfloat16) for part in sums) + (TOKEN,),
        in_specs=[VMEM] * (count + 1),
        out_specs=(VMEM,) * (count + 1),
    )(*sums, coded)


def lay_out(place, mine, rest):
    rows, width = mine[0].shape
    arrays = []
    for choice in jax.tree.leaves((mine, rest)):
        if not any(choice is array for array in arrays):
            arrays.append(choice)

    def index(array):
        return [array is known for known in arrays].index(True)

    def kernel(place_ref, *refs):
        ins, out_any, out_ref, sem = refs[:len(arrays)], *refs[len(arrays):]
        for x in range(2):
            own, other = slice(x * width, (x + 1) * width), slice((1 - x) * width, (2 - x) * width)
            for number in range(len(mine)):
                @pl.when((place_ref[0] == number) & (place_ref[1] == x))
                def _(own=own, other=other, number=number):
                    out_ref[:, own] = ins[index(mine[number])][...]
                    if isinstance(rest[number], tuple):
                        sums_ref, coded_ref = [ins[index(array)] for array in rest[number]]

                        def put(at, far):
                            out_ref[at:at + GROUP, other] = (sums_ref[at:at + GROUP, :] + far).astype(out_ref.dtype)

                        decode(coded_ref, rows, put)
                    else:
                        out_ref[:, other] = ins[index(rest[number])][...]
        copy = pltpu.make_async_copy(out_ref, out_any, sem)
        copy.start()
        copy.wait()

    return call(
        kernel, "lay_out",
        out_shape=pltpu.HBM((rows, 2 * width), jnp.bfloat16),
        in_specs=[SMEM] + [VMEM] * len(arrays),
        out_specs=ANY,
        scratch_shapes=[pltpu.VMEM((rows, 2 * width), jnp.bfloat16), pltpu.SemaphoreType.DMA],
    )(place, *arrays)


def top_and_rest(one, two, at):
    def kernel(one_ref, two_ref, top_ref, rest_ref, sem):
        copies = [
            pltpu.make_async_copy(one_ref.at[pl.ds(0, at)], top_ref, sem.at[0]),
            pltpu.make_async_copy(two_ref.at[pl.ds(at, two.shape[0] - at)], rest_ref, sem.at[1])]
        for copy in copies:
            copy.start()
        for copy in copies:
            copy.wait()

    return call(
        kernel, "top_and_rest",
        out_shape=(
            jax.ShapeDtypeStruct((at, one.shape[1]), one.dtype),
            jax.ShapeDtypeStruct((two.shape[0] - at, two.shape[1]), two.dtype)),
        in_specs=[ANY, ANY],
        out_specs=(VMEM, VMEM),
        scratch_shapes=[pltpu.SemaphoreType.DMA((2,))],
    )(one, two)


Z, X, Y = 4, 2, 2
AXES = ("row", "col")


def device(z, x, y, c):
    return (z * X + x) * Y * 2 + y * 2 + c


def moves(to, home=True):
    pairs = []
    for z in range(Z):
        for x in range(X):
            for y in range(Y):
                if to(z, x) is not None:
                    c = z % 2 if home else 1 - z % 2
                    pairs.append((device(z, x, y, c), device(*to(z, x), y, c)))
    return pairs


def across_x(z, x):
    return z, 1 - x


def across_x_ends(z, x):
    return (z, 1 - x) if z in (0, 3) else None


def across_x_middle(z, x):
    return (z, 1 - x) if z in (1, 2) else None


def over_centre(z, x):
    return (3 - z, x) if z in (1, 2) else None


def outward(z, x):
    return (z ^ 1, x) if z in (1, 2) else None


def to_y(far, cores):
    pairs = []
    for z in range(Z):
        end = (z // 2) ^ int(far)
        for x in range(X):
            for c in cores(z):
                pairs.append((device(z, x, 1 - end, c), device(z, x, end, c)))
    return pairs


def both(z):
    return 0, 1


def home_core(z):
    return (z % 2,)


def other_core(z):
    return (1 - z % 2,)


OWN_TO_PAIR = [
    (device(z, x, y, 1 - z % 2), device(z ^ 1, x, y, z % 2)) for z in range(Z) for x in range(X) for y in range(Y)]
CORES = [(0, 1), (1, 0), (2, 3), (3, 2)]
CHIPS_Y = [(0, 2), (2, 0), (1, 3), (3, 1)]
CROSSWISE = [(0, 3), (3, 0), (1, 2), (2, 1)]


def sparse_ladder(amplitudes, integrals, amp_mask, int_mask):
    barrier = lax.optimization_barrier
    tiles = int_mask.size
    cap = 2 * tiles * 11 // 16
    half = cap * TILE // 2
    row, col = lax.axis_index("row"), lax.axis_index("col")
    z, x = row // X, row % X
    y, c = col // 2, col % 2
    is_end = ((z == 0) | (z == Z - 1)).astype(jnp.int32)
    home = z % 2 == c

    def move(value, pairs):
        return lax.ppermute(value, AXES, pairs)

    def after(*tokens):
        return lambda *shards: barrier((*shards, tokens))

    near = z // 2 == y
    picks = jnp.stack([
        jnp.where(home, 0, 1),
        jnp.where(home, is_end, -1),
        jnp.where(home, 0, 1),
        jnp.where(home, is_end, 2 + is_end),
        jnp.where(home, -1, is_end),
    ] + [jnp.where(near, s, 1 - s) for s in (0, 1, 0, 1, 1)]).astype(jnp.int32)

    place = jnp.stack([jnp.where(near, 0, jnp.where(home, 1, 2)), x]).astype(jnp.int32)

    other = lax.ppermute(integrals, "col", CORES)
    other_mask = lax.ppermute(int_mask.T, "col", CORES)
    swap = jnp.where(home, 0, 1).astype(jnp.int32).reshape(1)
    own = pack_tiles((integrals, other), (int_mask.T, other_mask), swap, cap)
    own, picks, place, amplitudes_now = barrier((own, picks, place, amplitudes))

    masked, masked_token = mask_tiles(amplitudes_now, amp_mask)
    amps = (masked, lax.ppermute(masked, "col", CORES))
    one, centre, own_x, tokens = after(masked_token)(
        move(own, OWN_TO_PAIR), move(own, moves(over_centre)), move(own, moves(across_x)))

    a_sum, a_coded, token = shard_product(amps, picks, 0, [[own], [one]], tokens)
    two_end, two_mid, one_x, own_x, tokens = after(token)(
        move(centre, moves(outward, False)), move(one, moves(over_centre, False)), move(one, moves(across_x, False)),
        own_x)

    c_sum, c_coded, token = shard_product(amps, picks, 1, [[two_mid], [two_end]], tokens)
    c_far = move(c_coded, to_y(True, home_core))
    b_sum, ab_coded, token = shard_product(amps, picks, 2, [[own_x], [one_x]], (token,), a_coded)
    c_both, c_token = add_coded((c_sum,), c_far)
    three_end, three_mid_x, two_x_end, two_x_mid, tokens = after(token, c_token)(
        move(two_mid, moves(outward)), move(own_x, moves(over_centre)),
        move(two_end, moves(across_x_ends)), move(two_mid, moves(across_x_middle)))

    d_sum, d_coded, token = shard_product(
        amps, picks, 3, [[two_x_mid], [two_x_end], [centre], [three_end]], tokens)
    ab_far = move(ab_coded, to_y(False, both))
    top, rest = top_and_rest(three_end, two_x_mid, half)
    three_x, three_x_rest, tokens = after(token)(
        move(top, moves(across_x_ends, False)), move(rest, moves(outward)))

    d_far = move(d_coded, to_y(True, both))
    e_sum, e_coded, token = shard_product(amps, picks, 4, [[three_mid_x], [three_x, three_x_rest]], tokens,
        held=lambda part: in_hbm(part) if part is three_mid_x else part)
    e_far = move(e_coded, to_y(True, other_core))
    ab_far, token = barrier((ab_far, token))
    a_both, b_both, _ = add_coded((a_sum, b_sum), ab_far)
    d_both, _ = add_coded((d_sum,), d_far)
    flags = [token] + [lax.ppermute(token, "col", pairs) for pairs in (CORES, CHIPS_Y, CROSSWISE)]
    flags, a_both, b_both, d_both = barrier((flags, a_both, b_both, d_both))

    def finish():
        return lay_out(place, (a_both, c_both, d_both), (b_both, d_both, (e_sum, e_far)))

    return lax.cond(
        jnp.max(sum(flags)) > 0, lambda: dense_ladder(amplitudes, integrals, amp_mask, int_mask), finish)


def solution(mesh):
    in_specs = (P("row", "col"), P("col", "row"), P("row", "col"), P("col", "row"))
    out_specs = P("row", "col")
    here = dict(mesh.shape)
    per_device = sparse_ladder if here == {"row": Z * X, "col": Y * 2} else dense_ladder
    return jax.shard_map(
        per_device, mesh=mesh, in_specs=in_specs, out_specs=out_specs, check_vma=False
    )
```

```python
import jax
import jax.numpy as jnp
from jax import lax
from jax.experimental import pallas as pl
from jax.experimental.pallas import tpu as pltpu
from jax.sharding import PartitionSpec as P

TILE = 128
VMEM_LIMIT = 12 * 1024 * 1024


def expand(mask):
    spread = jnp.repeat(jnp.repeat(mask, TILE, axis=0), TILE, axis=1)
    return spread.astype(jnp.bfloat16)


def dense_ladder(amplitudes, integrals, amp_mask, int_mask):
    rows, cols = lax.axis_size("row"), lax.axis_size("col")
    row, col = lax.axis_index("row"), lax.axis_index("col")
    sparse_amp = amplitudes * expand(amp_mask)
    sparse_int = integrals * expand(int_mask)
    width = integrals.shape[1]
    share = rows * width // cols
    sums = jnp.zeros((amplitudes.shape[0], rows * width), jnp.float32)
    for step in range(rows):
        shard = lax.ppermute(sparse_int, "row", [((r + step) % rows, r) for r in range(rows)]) if step else sparse_int
        part = jnp.dot(sparse_amp, shard, preferred_element_type=jnp.float32)
        sums = lax.dynamic_update_slice(sums, part, (0, (row + step) % rows * width))
    ladder = lax.dynamic_slice(sums, (0, col * share), (sums.shape[0], share))
    for step in range(1, cols):
        part = lax.dynamic_slice(sums, (0, (col + step) % cols * share), (sums.shape[0], share))
        ladder = ladder + lax.ppermute(part, "col", [(c, (c + step) % cols) for c in range(cols)])
    return ladder.astype(jnp.bfloat16)


TOKEN = jax.ShapeDtypeStruct((8, TILE), jnp.float32)
LIGHT = pl.CostEstimate(flops=1, bytes_accessed=1, transcendentals=0)
STEPS = 5
TOP = 12
LOW = 4
BITS = 16 + LOW
GROUP = 128
META = 16


def in_hbm(array):
    return pltpu.with_memory_space_constraint(array, pltpu.HBM)


def call(kernel, name, cost=LIGHT, **kwargs):
    return pl.pallas_call(
        kernel,
        compiler_params=pltpu.CompilerParams(vmem_limit_bytes=VMEM_LIMIT),
        cost_estimate=cost,
        name=name,
        **kwargs,
    )


VMEM = pl.BlockSpec(memory_space=pltpu.VMEM)
SMEM = pl.BlockSpec(memory_space=pltpu.SMEM)
ANY = pl.BlockSpec(memory_space=pl.ANY)


def pack_tiles(shards, masks, swap, cap):
    wide = shards[0].shape[1] // TILE
    tiles = masks[0].size
    count = len(shards)

    def kernel(swap_ref, *refs):
        mask_refs, b_refs, out_ref = refs[:count], refs[count:-1], refs[-1]

        @pl.when(swap_ref[0] == 0)
        def _():
            pack(mask_refs, b_refs, out_ref)

        @pl.when(swap_ref[0] != 0)
        def _():
            pack(mask_refs[::-1], b_refs[::-1], out_ref)

    def pack(mask_refs, b_refs, out_ref):
        place = jnp.int32(0)
        lane = lax.broadcasted_iota(jnp.int32, (META, TILE), 1)
        sub = lax.broadcasted_iota(jnp.int32, (META, TILE), 0)
        meta = jnp.zeros((META, TILE), jnp.float32)
        for s in range(count):
            for t in range(tiles):
                k, n = divmod(t, wide)
                keep = mask_refs[s][n, k] != 0

                @pl.when(keep & (place < cap))
                def _(s=s, k=k, n=n, place=place):
                    at = pl.multiple_of(place * TILE, TILE)
                    out_ref[pl.ds(at, TILE), :] = b_refs[s][k * TILE:(k + 1) * TILE, n * TILE:(n + 1) * TILE]

                place = place + keep.astype(jnp.int32)
                meta = jnp.where((lane == s * tiles + t) & keep, 1.0, meta)
        meta = jnp.where(sub == 0, meta, jnp.where((sub == 1) & (place > cap), 1.0, 0.0))
        out_ref[cap * TILE:, :] = meta.astype(out_ref.dtype)

    return call(
        kernel, "pack_tiles",
        out_shape=jax.ShapeDtypeStruct((cap * TILE + META, TILE), shards[0].dtype),
        in_specs=[SMEM] * (1 + count) + [VMEM] * count,
        out_specs=VMEM,
    )(swap, *masks, *shards)


def mask_tiles(amplitudes, masks):
    rows, cols = amplitudes[0].shape
    count = len(amplitudes)

    def kernel(*refs):
        mask_refs, a_refs, out_refs, token_ref, sem = (
            refs[:count], refs[count:2 * count], refs[2 * count:3 * count], *refs[3 * count:])
        token_ref[...] = jnp.zeros_like(token_ref)
        copies = [
            [pltpu.make_async_copy(a_refs[s].at[pl.ds(at, TILE)], out_refs[s].at[pl.ds(at, TILE)], sem.at[s, at // TILE])
             for at in range(0, rows, TILE)] for s in range(count)]
        for copy in sum(copies, []):
            copy.start()
        for s in range(count):
            for r in range(rows // TILE):
                copies[s][r].wait()
                for t in range(cols // TILE):
                    @pl.when(mask_refs[s][r, t] == 0)
                    def _(s=s, r=r, t=t):
                        out_refs[s][r * TILE:(r + 1) * TILE, t * TILE:(t + 1) * TILE] = jnp.zeros(
                            (TILE, TILE), out_refs[s].dtype)

    return call(
        kernel, "mask_tiles",
        out_shape=tuple(jax.ShapeDtypeStruct(part.shape, part.dtype) for part in amplitudes) + (TOKEN,),
        in_specs=[SMEM] * count + [ANY] * count,
        out_specs=(VMEM,) * (count + 1),
        scratch_shapes=[pltpu.SemaphoreType.DMA((count, rows // TILE))],
    )(*masks, *amplitudes)


def shard_product(amps, picks, step, choices, tokens, before=None, split=False, held=in_hbm):
    rows, depth = amps[0].shape
    count = len(amps)
    height = sum(part.shape[0] for part in choices[0])
    cap = height - META
    wide = 2
    tiles = count * wide * depth // TILE
    word = 16
    first_row = 0 if before is None else before.shape[0]
    half_rows = coded_rows(rows // 2)
    parts = []
    for choice in choices:
        for part in choice:
            if not any(part is p for p in parts):
                parts.append(part)

    def kernel(picks_ref, *refs):
        if first_row:
            before_ref, refs = refs[0], refs[1:]
        token_refs, refs = refs[:len(tokens)], refs[len(tokens):]
        a_refs, refs = refs[:count], refs[count:]
        p_any, refs = refs[:len(parts)], refs[len(parts):]
        out_ref, *coded_refs, token_ref, packed, wide_ref, sem = refs
        pick = picks_ref[step]
        token_ref[...] = sum(ref[...] for ref in token_refs)
        for number, choice in enumerate(choices):
            @pl.when(pick == number)
            def _(choice=choice):
                at = 0
                copies = []
                for part in choice:
                    index = [part is p for p in parts].index(True)
                    copies.append(pltpu.make_async_copy(
                        p_any[index], packed.at[pl.ds(at, part.shape[0])], sem.at[len(copies)]))
                    at += part.shape[0]
                for copy in copies:
                    copy.start()
                for copy in copies:
                    copy.wait()

        @pl.when(pick >= 0)
        def _():
            meta = packed[cap:, :].astype(jnp.float32)
            lane = lax.broadcasted_iota(jnp.int32, meta.shape, 1)
            sub = lax.broadcasted_iota(jnp.int32, meta.shape, 0)
            first = (sub == 0) & (meta != 0)
            bits = [
                jnp.sum(jnp.where(
                    first & (lane >= lo) & (lane < lo + word), jnp.left_shift(1, (lane - lo) & (word - 1)), 0))
                for lo in range(0, tiles, word)]
            token_ref[...] += jnp.where(sub == 1, meta, 0.0)[:token_ref.shape[0]]
            place = jnp.int32(0)
            for s in range(count):
                for t in range(s * tiles // count, (s + 1) * tiles // count):
                    k, n = divmod(t, wide)
                    keep = ((bits[t // word] >> (t % word)) & 1) != 0
                    at = pl.multiple_of(jnp.minimum(place * TILE, cap - TILE), TILE)
                    tile = packed[pl.ds(at, TILE), :]
                    wide_ref[k * TILE:(k + 1) * TILE, n * TILE:(n + 1) * TILE] = jnp.where(
                        keep, tile, jnp.zeros_like(tile))
                    place = place + keep.astype(jnp.int32)
                term = jnp.dot(
                    a_refs[s][...], wide_ref[s * depth:(s + 1) * depth, :], preferred_element_type=jnp.float32)
                if s:
                    out_ref[...] += term
                else:
                    out_ref[...] = term

        @pl.when((pick >= 0) & (picks_ref[STEPS + step] != 0))
        def _():
            if first_row:
                coded_refs[0][:first_row, :] = before_ref[...]
            for h, (first, length, at) in enumerate(halves(rows, first_row)):
                spot = coded_refs[h] if split else coded_refs[0].at[pl.ds(at, coded_rows(length))]
                encode(out_ref.at[pl.ds(first, length)], spot)

    return call(
        kernel, "shard_product",
        out_shape=(
            jax.ShapeDtypeStruct((rows, wide * TILE), jnp.float32),
            *([jax.ShapeDtypeStruct((half_rows, wide * TILE), jnp.int16)] * 2 if split else
              [jax.ShapeDtypeStruct((first_row + 2 * half_rows, wide * TILE), jnp.int16)]),
            TOKEN),
        in_specs=[SMEM] + [VMEM] * (bool(first_row) + len(tokens) + count) + [ANY] * len(parts),
        out_specs=(VMEM,) * (4 if split else 3),
        scratch_shapes=[
            pltpu.VMEM((height, TILE), amps[0].dtype),
            pltpu.VMEM((count * depth, wide * TILE), amps[0].dtype),
            pltpu.SemaphoreType.DMA((2,)),
        ],
    )(picks, *([before] if first_row else []), *tokens, *amps, *map(held, parts))


def coded_rows(rows):
    return rows + rows // (16 // LOW) + META


def halves(rows, first_row=0):
    half = rows // 2
    return [(h * half, half, first_row + h * coded_rows(half)) for h in range(2)]


def step_factors(exponent):
    power = BITS - 1 - TOP - exponent
    factors = []
    for part in (power // 2, power - power // 2):
        factor = jnp.ones(part.shape, jnp.float32)
        for bit in range(7):
            factor = factor * jnp.where((part >> bit) & 1 != 0, 2.0 ** (1 << bit), 1.0)
        factors.append(factor)
    return factors


def encode(sums_ref, coded_ref):
    rows, cols = sums_ref.shape
    groups = rows // GROUP
    largest = jnp.concatenate([
        jnp.max(jnp.abs(sums_ref[g * GROUP:(g + 1) * GROUP, :]), axis=0, keepdims=True) for g in range(groups)])
    rest = largest * 2.0 ** -TOP
    exponent = jnp.zeros(rest.shape, jnp.int32)
    for bit in (64, 32, 16, 8, 4, 2, 1):
        small = rest < 2.0 ** -bit
        rest = jnp.where(small, rest * 2.0 ** bit, rest)
        exponent = jnp.where(small, exponent - bit, exponent)
    one, two = step_factors(exponent)
    share = 16 // LOW
    block = rows // share
    for start in range(0, block, GROUP):
        low = jnp.zeros((GROUP, cols), jnp.int32)
        for part in range(share):
            at = part * block + start
            g = at // GROUP
            value = sums_ref[at:at + GROUP, :] * one[g:g + 1] * two[g:g + 1]
            value = jnp.minimum(jnp.round(value).astype(jnp.int32), (1 << (BITS - 1)) - 1)
            coded_ref[at:at + GROUP, :] = (value >> LOW).astype(jnp.int16)
            low = low | ((value & ((1 << LOW) - 1)) << (LOW * part))
        coded_ref[rows + start:rows + start + GROUP, :] = (low - 32768).astype(jnp.int16)
    coded_ref[rows + block:, :] = jnp.concatenate([exponent] * (META // groups)).astype(jnp.int16)


def decode(coded_ref, rows, put):
    groups = rows // GROUP
    share = 16 // LOW
    block = rows // share
    one, two = step_factors(coded_ref[rows + block:, :].astype(jnp.int32)[:groups])
    one, two = 1.0 / one, 1.0 / two
    for start in range(0, block, GROUP):
        low = coded_ref[rows + start:rows + start + GROUP, :].astype(jnp.int32) + 32768
        for part in range(share):
            at = part * block + start
            g = at // GROUP
            high = coded_ref[at:at + GROUP, :].astype(jnp.int32)
            value = (high << LOW) | ((low >> (LOW * part)) & ((1 << LOW) - 1))
            put(at, value.astype(jnp.float32) * one[g:g + 1] * two[g:g + 1])


def add_coded(sums, coded, tokens=()):
    count = len(sums)
    arrays = []
    for array, _ in [pair for one in coded for pair in one]:
        if not any(array is known for known in arrays):
            arrays.append(array)

    def kernel(*refs):
        token_refs, refs = refs[:len(tokens)], refs[len(tokens):]
        sums_refs, coded_refs, out_refs, token_ref = refs[:count], refs[count:-count - 1], refs[-count - 1:-1], refs[-1]
        token_ref[...] = sum((ref[...] for ref in token_refs), jnp.zeros(token_ref.shape, token_ref.dtype))
        for number in range(count):
            for (first, length, _), (array, at) in zip(halves(sums[number].shape[0]), coded[number]):
                ref = coded_refs[[array is known for known in arrays].index(True)]
                add_half(sums_refs[number], ref.at[pl.ds(at, coded_rows(length))], out_refs[number], first, length)

    return call(
        kernel, "add_coded",
        out_shape=tuple(jax.ShapeDtypeStruct(part.shape, jnp.bfloat16) for part in sums) + (TOKEN,),
        in_specs=[VMEM] * (len(tokens) + count + len(arrays)),
        out_specs=(VMEM,) * (count + 1),
    )(*tokens, *sums, *arrays)


def add_half(sums_ref, coded_ref, out_ref, first, length):
    def put(at, far):
        spot = pl.ds(first + at, GROUP)
        out_ref[spot, :] = (sums_ref[spot, :] + far).astype(out_ref.dtype)

    decode(coded_ref, length, put)


def both_halves(sums, coded, first_row=0):
    return [(coded, at) for _, _, at in halves(sums.shape[0], first_row)]


def lay_out(place, mine, rest):
    choices = [(one if isinstance(one, tuple) else (one,), two if isinstance(two, tuple) else (two,))
               for one, two in zip(mine, rest)]
    arrays = []
    for array in jax.tree.leaves(choices):
        if not any(array is known for known in arrays):
            arrays.append(array)
    rows, width = arrays[0].shape

    def kernel(place_ref, *refs):
        ins = refs[:len(arrays)]
        out_any, round_ref, sums_ref, coded_ref, sems = refs[len(arrays):]
        parts_of = halves(rows)

        def store(side, first, length):
            at = pl.multiple_of((place_ref[1] ^ side) * width, width)
            return pltpu.make_async_copy(
                round_ref.at[side, pl.ds(first, length)], out_any.at[pl.ds(first, length), pl.ds(at, width)],
                sems.at[2, 2 * side + first // length])

        for number, choice in enumerate(choices):
            @pl.when(place_ref[0] == number)
            def _(choice=choice):
                fetch = {}
                for side, parts in enumerate(choice):
                    refs_in = [ins[[part is array for array in arrays].index(True)] for part in parts]
                    for h, (first, length, at) in enumerate(parts_of):
                        wanted = [(refs_in[0], first, length, (round_ref if len(parts) == 1 else sums_ref).at[side])]
                        if len(parts) == 2:
                            wanted.append((refs_in[1], at, coded_rows(length), coded_ref.at[side]))
                        fetch[side, h] = [
                            pltpu.make_async_copy(
                                source.at[pl.ds(start, size)], target.at[pl.ds(start, size)], sems.at[n, 2 * side + h])
                            for n, (source, start, size, target) in enumerate(wanted)]
                for copy in sum(fetch.values(), []):
                    copy.start()
                for side, parts in enumerate(choice):
                    for h, (first, length, at) in enumerate(parts_of):
                        for copy in fetch[side, h]:
                            copy.wait()
                        if len(parts) == 2:
                            add_half(
                                sums_ref.at[side], coded_ref.at[side, pl.ds(at, coded_rows(length))],
                                round_ref.at[side], first, length)
                        store(side, first, length).start()

        for side in range(2):
            for first, length, _ in parts_of:
                store(side, first, length).wait()

    return call(
        kernel, "lay_out",
        out_shape=pltpu.HBM((rows, 2 * width), jnp.bfloat16),
        in_specs=[SMEM] + [ANY] * len(arrays),
        out_specs=ANY,
        scratch_shapes=[
            pltpu.VMEM((2, rows, width), jnp.bfloat16),
            pltpu.VMEM((2, rows, width), jnp.float32),
            pltpu.VMEM((2, 2 * coded_rows(rows // 2), width), jnp.int16),
            pltpu.SemaphoreType.DMA((3, 4))],
    )(place, *arrays)


Z, X, Y = 4, 2, 2
AXES = ("row", "col")


def device(z, x, y, c):
    return (z * X + x) * Y * 2 + y * 2 + c


def moves(to, home=True):
    pairs = []
    for z in range(Z):
        for x in range(X):
            for y in range(Y):
                if to(z, x) is not None:
                    c = z % 2 if home else 1 - z % 2
                    pairs.append((device(z, x, y, c), device(*to(z, x), y, c)))
    return pairs


def across_x(z, x):
    return z, 1 - x


def across_x_ends(z, x):
    return (z, 1 - x) if z in (0, 3) else None


def across_x_middle(z, x):
    return (z, 1 - x) if z in (1, 2) else None


def over_centre(z, x):
    return (3 - z, x) if z in (1, 2) else None


def outward(z, x):
    return (z ^ 1, x) if z in (1, 2) else None


def to_y(far, cores):
    pairs = []
    for z in range(Z):
        end = (z // 2) ^ int(far)
        for x in range(X):
            for c in cores(z):
                pairs.append((device(z, x, 1 - end, c), device(z, x, end, c)))
    return pairs


def both(z):
    return 0, 1


def early_cores(z):
    return (0, 1) if z in (1, 2) else (z % 2,)


def late_cores(z):
    return () if z in (1, 2) else (1 - z % 2,)


OWN_TO_PAIR = [
    (device(z, x, y, 1 - z % 2), device(z ^ 1, x, y, z % 2)) for z in range(Z) for x in range(X) for y in range(Y)]
CORES = [(0, 1), (1, 0), (2, 3), (3, 2)]
CHIPS_Y = [(0, 2), (2, 0), (1, 3), (3, 1)]


def sparse_ladder(amplitudes, integrals, amp_mask, int_mask):
    barrier = lax.optimization_barrier
    tiles = int_mask.size
    cap = 2 * tiles * 11 // 16
    row, col = lax.axis_index("row"), lax.axis_index("col")
    z, x = row // X, row % X
    y, c = col // 2, col % 2
    is_end = ((z == 0) | (z == Z - 1)).astype(jnp.int32)
    home = z % 2 == c

    def move(value, pairs):
        return lax.ppermute(value, AXES, pairs)

    def after(*tokens):
        return lambda *shards: barrier((*shards, tokens))

    near = z // 2 == y
    picks = jnp.stack([
        jnp.where(home, 0, 1),
        jnp.where(home, is_end, jnp.where(is_end, -1, 2)),
        jnp.where(home, 0, 1),
        jnp.where(home, is_end, 2 + is_end),
        jnp.where(home, -1, is_end - 1),
    ] + [jnp.where(near, s, 1 - s) for s in (0, 1, 0, 1, 1)]).astype(jnp.int32)

    place = jnp.stack([jnp.where(near, 0, jnp.where(home | (is_end == 0), 1, 2)), x]).astype(jnp.int32)

    other = lax.ppermute(integrals, "col", CORES)
    other_mask = lax.ppermute(int_mask.T, "col", CORES)
    other_amp_mask = lax.ppermute(amp_mask, "col", CORES)
    swap = jnp.where(home, 0, 1).astype(jnp.int32).reshape(1)
    own = pack_tiles((integrals, other), (int_mask.T, other_mask), swap, cap)
    own, picks, place, other_amp_mask, amplitudes_now = barrier((own, picks, place, other_amp_mask, amplitudes))
    other_amps = lax.ppermute(amplitudes_now, "col", CORES)

    *amps, masked_token = mask_tiles((amplitudes, other_amps), (amp_mask, other_amp_mask))
    one, centre, own_x, tokens = after(masked_token)(
        move(own, OWN_TO_PAIR), move(own, moves(over_centre)), move(own, moves(across_x)))

    a_sum, a_coded, a_rest, token = shard_product(amps, picks, 0, [[own], [one]], tokens, split=True)
    a_far = move(a_coded, to_y(False, both))
    two_end, two_mid, one_x, own_x, a_far, tokens = after(token)(
        move(centre, moves(outward, False)), move(one, moves(over_centre, False)), move(one, moves(across_x, False)),
        own_x, a_far)

    c_sum, c_coded, token = shard_product(amps, picks, 1, [[two_mid], [two_end], [centre]], tokens)
    c_far = move(c_coded, to_y(True, early_cores))
    b_sum, ab_coded, token = shard_product(amps, picks, 2, [[own_x], [one_x]], (token,), a_rest)
    three_end, three_mid_x, two_x_end, two_x_mid, c_far, tokens = after(token)(
        move(two_mid, moves(outward)), move(own_x, moves(over_centre)),
        move(two_end, moves(across_x_ends)), move(two_mid, moves(across_x_middle)), c_far)

    d_sum, d_coded, token = shard_product(
        amps, picks, 3, [[two_x_mid], [two_x_end], [three_mid_x], [three_end]], tokens)
    ab_far = move(ab_coded, to_y(False, both))
    three_x, tokens = after(token)(move(three_end, moves(across_x_ends, False)))

    d_far = move(d_coded, to_y(True, both))
    e_sum, e_coded, token = shard_product(amps, picks, 4, [[three_x]], tokens, held=lambda part: part)
    e_far = move(e_coded, to_y(True, late_cores))
    c_far, _ = barrier((c_far, token))
    ab_far, a_far, _ = barrier((ab_far, a_far, token))
    c_both, token = add_coded((c_sum,), [both_halves(c_sum, c_far)], (token, lax.ppermute(token, "col", CORES)))
    a_both, b_both, _ = add_coded(
        (a_sum, b_sum), ([(a_far, 0), (ab_far, 0)], both_halves(b_sum, ab_far, a_rest.shape[0])))
    flags = [token, lax.ppermute(token, "col", CHIPS_Y)]
    flags, a_both, b_both, c_both, d_far = barrier((flags, a_both, b_both, c_both, d_far))

    def finish():
        return lay_out(place, (a_both, c_both, (d_sum, d_far)), (b_both, (d_sum, d_far), (e_sum, e_far)))

    return lax.cond(
        jnp.max(sum(flags)) > 0, lambda: dense_ladder(amplitudes, integrals, amp_mask, int_mask), finish)


def solution(mesh):
    in_specs = (P("row", "col"), P("col", "row"), P("row", "col"), P("col", "row"))
    out_specs = P("row", "col")
    here = dict(mesh.shape)
    per_device = sparse_ladder if here == {"row": Z * X, "col": Y * 2} else dense_ladder
    return jax.shard_map(
        per_device, mesh=mesh, in_specs=in_specs, out_specs=out_specs, check_vma=False
    )
```

```python
import jax
import jax.numpy as jnp
from jax import lax
from jax.experimental import pallas as pl
from jax.experimental.pallas import tpu as pltpu
from jax.sharding import PartitionSpec as P

TILE = 128
VMEM_LIMIT = 12 * 1024 * 1024


def expand(mask):
    spread = jnp.repeat(jnp.repeat(mask, TILE, axis=0), TILE, axis=1)
    return spread.astype(jnp.bfloat16)


def dense_ladder(amplitudes, integrals, amp_mask, int_mask):
    rows, cols = lax.axis_size("row"), lax.axis_size("col")
    row, col = lax.axis_index("row"), lax.axis_index("col")
    sparse_amp = amplitudes * expand(amp_mask)
    sparse_int = integrals * expand(int_mask)
    width = integrals.shape[1]
    share = rows * width // cols
    sums = jnp.zeros((amplitudes.shape[0], rows * width), jnp.float32)
    for step in range(rows):
        shard = lax.ppermute(sparse_int, "row", [((r + step) % rows, r) for r in range(rows)]) if step else sparse_int
        part = jnp.dot(sparse_amp, shard, preferred_element_type=jnp.float32)
        sums = lax.dynamic_update_slice(sums, part, (0, (row + step) % rows * width))
    ladder = lax.dynamic_slice(sums, (0, col * share), (sums.shape[0], share))
    for step in range(1, cols):
        part = lax.dynamic_slice(sums, (0, (col + step) % cols * share), (sums.shape[0], share))
        ladder = ladder + lax.ppermute(part, "col", [(c, (c + step) % cols) for c in range(cols)])
    return ladder.astype(jnp.bfloat16)


TOKEN = jax.ShapeDtypeStruct((8, TILE), jnp.float32)
LIGHT = pl.CostEstimate(flops=1, bytes_accessed=1, transcendentals=0)
STEPS = 5
TOP = 12
LOW = 4
BITS = 16 + LOW
GROUP = 128
META = 16


def in_hbm(array):
    return pltpu.with_memory_space_constraint(array, pltpu.HBM)


def call(kernel, name, cost=LIGHT, **kwargs):
    return pl.pallas_call(
        kernel,
        compiler_params=pltpu.CompilerParams(vmem_limit_bytes=VMEM_LIMIT),
        cost_estimate=cost,
        name=name,
        **kwargs,
    )


VMEM = pl.BlockSpec(memory_space=pltpu.VMEM)
SMEM = pl.BlockSpec(memory_space=pltpu.SMEM)
ANY = pl.BlockSpec(memory_space=pl.ANY)


def pack_tiles(shards, masks, swap, cap):
    wide = shards[0].shape[1] // TILE
    tiles = masks[0].size
    count = len(shards)

    def kernel(swap_ref, *refs):
        mask_refs, b_refs, out_ref = refs[:count], refs[count:-1], refs[-1]

        @pl.when(swap_ref[0] == 0)
        def _():
            pack(mask_refs, b_refs, out_ref)

        @pl.when(swap_ref[0] != 0)
        def _():
            pack(mask_refs[::-1], b_refs[::-1], out_ref)

    def pack(mask_refs, b_refs, out_ref):
        place = jnp.int32(0)
        lane = lax.broadcasted_iota(jnp.int32, (META, TILE), 1)
        sub = lax.broadcasted_iota(jnp.int32, (META, TILE), 0)
        meta = jnp.zeros((META, TILE), jnp.float32)
        for s in range(count):
            for t in range(tiles):
                k, n = divmod(t, wide)
                keep = mask_refs[s][n, k] != 0

                @pl.when(keep & (place < cap))
                def _(s=s, k=k, n=n, place=place):
                    at = pl.multiple_of(place * TILE, TILE)
                    out_ref[pl.ds(at, TILE), :] = b_refs[s][k * TILE:(k + 1) * TILE, n * TILE:(n + 1) * TILE]

                place = place + keep.astype(jnp.int32)
                meta = jnp.where((lane == s * tiles + t) & keep, 1.0, meta)
        meta = jnp.where(sub == 0, meta, jnp.where((sub == 1) & (place > cap), 1.0, 0.0))
        out_ref[cap * TILE:, :] = meta.astype(out_ref.dtype)

    return call(
        kernel, "pack_tiles",
        out_shape=jax.ShapeDtypeStruct((cap * TILE + META, TILE), shards[0].dtype),
        in_specs=[SMEM] * (1 + count) + [VMEM] * count,
        out_specs=VMEM,
    )(swap, *masks, *shards)


def mask_tiles(amplitudes, masks):
    rows, cols = amplitudes[0].shape
    count = len(amplitudes)

    def kernel(*refs):
        mask_refs, a_refs, out_refs, token_ref, sem = (
            refs[:count], refs[count:2 * count], refs[2 * count:3 * count], *refs[3 * count:])
        token_ref[...] = jnp.zeros_like(token_ref)
        copies = [
            [pltpu.make_async_copy(a_refs[s].at[pl.ds(at, TILE)], out_refs[s].at[pl.ds(at, TILE)], sem.at[s, at // TILE])
             for at in range(0, rows, TILE)] for s in range(count)]
        for copy in sum(copies, []):
            copy.start()
        for s in range(count):
            for r in range(rows // TILE):
                copies[s][r].wait()
                for t in range(cols // TILE):
                    @pl.when(mask_refs[s][r, t] == 0)
                    def _(s=s, r=r, t=t):
                        out_refs[s][r * TILE:(r + 1) * TILE, t * TILE:(t + 1) * TILE] = jnp.zeros(
                            (TILE, TILE), out_refs[s].dtype)

    return call(
        kernel, "mask_tiles",
        out_shape=tuple(jax.ShapeDtypeStruct(part.shape, part.dtype) for part in amplitudes) + (TOKEN,),
        in_specs=[SMEM] * count + [ANY] * count,
        out_specs=(VMEM,) * (count + 1),
        scratch_shapes=[pltpu.SemaphoreType.DMA((count, rows // TILE))],
    )(*masks, *amplitudes)


def shard_product(amps, picks, step, choices, tokens, before=None, split=False, held=in_hbm):
    rows, depth = amps[0].shape
    count = len(amps)
    height = sum(part.shape[0] for part in choices[0])
    cap = height - META
    wide = 2
    tiles = count * wide * depth // TILE
    word = 16
    first_row = 0 if before is None else before.shape[0]
    half_rows = coded_rows(rows // 2)
    parts = []
    for choice in choices:
        for part in choice:
            if not any(part is p for p in parts):
                parts.append(part)

    def kernel(picks_ref, *refs):
        if first_row:
            before_ref, refs = refs[0], refs[1:]
        token_refs, refs = refs[:len(tokens)], refs[len(tokens):]
        a_refs, refs = refs[:count], refs[count:]
        p_any, refs = refs[:len(parts)], refs[len(parts):]
        out_ref, *coded_refs, token_ref, packed, wide_ref, sem = refs
        pick = picks_ref[step]
        token_ref[...] = sum(ref[...] for ref in token_refs)
        for number, choice in enumerate(choices):
            @pl.when(pick == number)
            def _(choice=choice):
                at = 0
                copies = []
                for part in choice:
                    index = [part is p for p in parts].index(True)
                    copies.append(pltpu.make_async_copy(
                        p_any[index], packed.at[pl.ds(at, part.shape[0])], sem.at[len(copies)]))
                    at += part.shape[0]
                for copy in copies:
                    copy.start()
                for copy in copies:
                    copy.wait()

        @pl.when(pick >= 0)
        def _():
            meta = packed[cap:, :].astype(jnp.float32)
            lane = lax.broadcasted_iota(jnp.int32, meta.shape, 1)
            sub = lax.broadcasted_iota(jnp.int32, meta.shape, 0)
            first = (sub == 0) & (meta != 0)
            bits = [
                jnp.sum(jnp.where(
                    first & (lane >= lo) & (lane < lo + word), jnp.left_shift(1, (lane - lo) & (word - 1)), 0))
                for lo in range(0, tiles, word)]
            token_ref[...] += jnp.where(sub == 1, meta, 0.0)[:token_ref.shape[0]]
            place = jnp.int32(0)
            for s in range(count):
                for t in range(s * tiles // count, (s + 1) * tiles // count):
                    k, n = divmod(t, wide)
                    keep = ((bits[t // word] >> (t % word)) & 1) != 0
                    at = pl.multiple_of(jnp.minimum(place * TILE, cap - TILE), TILE)
                    tile = packed[pl.ds(at, TILE), :]
                    wide_ref[k * TILE:(k + 1) * TILE, n * TILE:(n + 1) * TILE] = jnp.where(
                        keep, tile, jnp.zeros_like(tile))
                    place = place + keep.astype(jnp.int32)
                term = jnp.dot(
                    a_refs[s][...], wide_ref[s * depth:(s + 1) * depth, :], preferred_element_type=jnp.float32)
                if s:
                    out_ref[...] += term
                else:
                    out_ref[...] = term

        @pl.when((pick >= 0) & (picks_ref[STEPS + step] != 0))
        def _():
            if first_row:
                coded_refs[0][:first_row, :] = before_ref[...]
            for h, (first, length, at) in enumerate(halves(rows, first_row)):
                spot = coded_refs[h] if split else coded_refs[0].at[pl.ds(at, coded_rows(length))]
                encode(out_ref.at[pl.ds(first, length)], spot)

    return call(
        kernel, "shard_product",
        out_shape=(
            jax.ShapeDtypeStruct((rows, wide * TILE), jnp.float32),
            *([jax.ShapeDtypeStruct((half_rows, wide * TILE), jnp.int16)] * 2 if split else
              [jax.ShapeDtypeStruct((first_row + 2 * half_rows, wide * TILE), jnp.int16)]),
            TOKEN),
        in_specs=[SMEM] + [VMEM] * (bool(first_row) + len(tokens) + count) + [ANY] * len(parts),
        out_specs=(VMEM,) * (4 if split else 3),
        scratch_shapes=[
            pltpu.VMEM((height, TILE), amps[0].dtype),
            pltpu.VMEM((count * depth, wide * TILE), amps[0].dtype),
            pltpu.SemaphoreType.DMA((2,)),
        ],
    )(picks, *([before] if first_row else []), *tokens, *amps, *map(held, parts))


def coded_rows(rows):
    return rows + rows // (16 // LOW) + META


def halves(rows, first_row=0):
    half = rows // 2
    return [(h * half, half, first_row + h * coded_rows(half)) for h in range(2)]


def step_factors(exponent):
    power = BITS - 1 - TOP - exponent
    factors = []
    for part in (power // 2, power - power // 2):
        factor = jnp.ones(part.shape, jnp.float32)
        for bit in range(7):
            factor = factor * jnp.where((part >> bit) & 1 != 0, 2.0 ** (1 << bit), 1.0)
        factors.append(factor)
    return factors


def encode(sums_ref, coded_ref):
    rows, cols = sums_ref.shape
    groups = rows // GROUP
    largest = jnp.concatenate([
        jnp.max(jnp.abs(sums_ref[g * GROUP:(g + 1) * GROUP, :]), axis=0, keepdims=True) for g in range(groups)])
    rest = largest * 2.0 ** -TOP
    exponent = jnp.zeros(rest.shape, jnp.int32)
    for bit in (64, 32, 16, 8, 4, 2, 1):
        small = rest < 2.0 ** -bit
        rest = jnp.where(small, rest * 2.0 ** bit, rest)
        exponent = jnp.where(small, exponent - bit, exponent)
    one, two = step_factors(exponent)
    share = 16 // LOW
    block = rows // share
    for start in range(0, block, GROUP):
        low = jnp.zeros((GROUP, cols), jnp.int32)
        for part in range(share):
            at = part * block + start
            g = at // GROUP
            value = sums_ref[at:at + GROUP, :] * one[g:g + 1] * two[g:g + 1]
            value = jnp.minimum(jnp.round(value).astype(jnp.int32), (1 << (BITS - 1)) - 1)
            coded_ref[at:at + GROUP, :] = (value >> LOW).astype(jnp.int16)
            low = low | ((value & ((1 << LOW) - 1)) << (LOW * part))
        coded_ref[rows + start:rows + start + GROUP, :] = (low - 32768).astype(jnp.int16)
    coded_ref[rows + block:, :] = jnp.concatenate([exponent] * (META // groups)).astype(jnp.int16)


def decode(coded_ref, rows, put):
    groups = rows // GROUP
    share = 16 // LOW
    block = rows // share
    one, two = step_factors(coded_ref[rows + block:, :].astype(jnp.int32)[:groups])
    one, two = 1.0 / one, 1.0 / two
    for start in range(0, block, GROUP):
        low = coded_ref[rows + start:rows + start + GROUP, :].astype(jnp.int32) + 32768
        for part in range(share):
            at = part * block + start
            g = at // GROUP
            high = coded_ref[at:at + GROUP, :].astype(jnp.int32)
            value = (high << LOW) | ((low >> (LOW * part)) & ((1 << LOW) - 1))
            put(at, value.astype(jnp.float32) * one[g:g + 1] * two[g:g + 1])


def add_coded(sums, coded, tokens=()):
    count = len(sums)
    arrays = []
    for array, _ in [pair for one in coded for pair in one]:
        if not any(array is known for known in arrays):
            arrays.append(array)

    def kernel(*refs):
        token_refs, refs = refs[:len(tokens)], refs[len(tokens):]
        sums_refs, coded_refs, out_refs, token_ref = refs[:count], refs[count:-count - 1], refs[-count - 1:-1], refs[-1]
        token_ref[...] = sum((ref[...] for ref in token_refs), jnp.zeros(token_ref.shape, token_ref.dtype))
        for number in range(count):
            for (first, length, _), (array, at) in zip(halves(sums[number].shape[0]), coded[number]):
                ref = coded_refs[[array is known for known in arrays].index(True)]
                add_half(sums_refs[number], ref.at[pl.ds(at, coded_rows(length))], out_refs[number], first, length)

    return call(
        kernel, "add_coded",
        out_shape=tuple(jax.ShapeDtypeStruct(part.shape, jnp.bfloat16) for part in sums) + (TOKEN,),
        in_specs=[VMEM] * (len(tokens) + count + len(arrays)),
        out_specs=(VMEM,) * (count + 1),
    )(*tokens, *sums, *arrays)


def add_half(sums_ref, coded_ref, out_ref, first, length):
    def put(at, far):
        spot = pl.ds(first + at, GROUP)
        out_ref[spot, :] = (sums_ref[spot, :] + far).astype(out_ref.dtype)

    decode(coded_ref, length, put)


def both_halves(sums, coded, first_row=0):
    return [(coded, at) for _, _, at in halves(sums.shape[0], first_row)]


def lay_out(place, mine, rest):
    choices = list(zip(mine, rest))
    arrays = []
    for choice in choices:
        for sums, *coded in choice:
            for array in (sums, *[array for array, _ in coded]):
                if not any(array is known for known in arrays):
                    arrays.append(array)
    rows, width = arrays[0].shape
    parts = halves(rows)

    def kernel(place_ref, *refs):
        ins = refs[:len(arrays)]
        out_any, round_ref, sums_ref, coded_ref, sems = refs[len(arrays):]

        def place_of(array):
            return ins[[array is known for known in arrays].index(True)]

        def store(side, first, length):
            at = pl.multiple_of((place_ref[1] ^ side) * width, width)
            return pltpu.make_async_copy(
                round_ref.at[side, pl.ds(first, length)], out_any.at[pl.ds(first, length), pl.ds(at, width)],
                sems.at[2, 2 * side + first // length])

        for number, choice in enumerate(choices):
            @pl.when(place_ref[0] == number)
            def _(choice=choice):
                fetch = {}
                for side, (sums, *coded) in enumerate(choice):
                    for h, (first, length, _) in enumerate(parts):
                        fetch[side, h] = [pltpu.make_async_copy(
                            place_of(sums).at[pl.ds(first, length)],
                            (sums_ref if coded else round_ref).at[side, pl.ds(first, length)], sems.at[0, 2 * side + h])]
                        if coded:
                            array, at = coded[h]
                            fetch[side, h].append(pltpu.make_async_copy(
                                place_of(array).at[pl.ds(at, coded_rows(length))], coded_ref.at[side, h],
                                sems.at[1, 2 * side + h]))
                for copy in sum(fetch.values(), []):
                    copy.start()
                for side, (sums, *coded) in enumerate(choice):
                    for h, (first, length, _) in enumerate(parts):
                        for copy in fetch[side, h]:
                            copy.wait()
                        if coded:
                            add_half(sums_ref.at[side], coded_ref.at[side, h], round_ref.at[side], first, length)
                        store(side, first, length).start()

        for side in range(2):
            for first, length, _ in parts:
                store(side, first, length).wait()

    return call(
        kernel, "lay_out",
        out_shape=pltpu.HBM((rows, 2 * width), jnp.bfloat16),
        in_specs=[SMEM] + [ANY] * len(arrays),
        out_specs=ANY,
        scratch_shapes=[
            pltpu.VMEM((2, rows, width), jnp.bfloat16),
            pltpu.VMEM((2, rows, width), jnp.float32),
            pltpu.VMEM((2, 2, coded_rows(rows // 2), width), jnp.int16),
            pltpu.SemaphoreType.DMA((3, 4))],
    )(place, *arrays)


Z, X, Y = 4, 2, 2
AXES = ("row", "col")


def device(z, x, y, c):
    return (z * X + x) * Y * 2 + y * 2 + c


def moves(to, home=True):
    pairs = []
    for z in range(Z):
        for x in range(X):
            for y in range(Y):
                if to(z, x) is not None:
                    c = z % 2 if home else 1 - z % 2
                    pairs.append((device(z, x, y, c), device(*to(z, x), y, c)))
    return pairs


def across_x(z, x):
    return z, 1 - x


def across_x_ends(z, x):
    return (z, 1 - x) if z in (0, 3) else None


def across_x_middle(z, x):
    return (z, 1 - x) if z in (1, 2) else None


def over_centre(z, x):
    return (3 - z, x) if z in (1, 2) else None


def outward(z, x):
    return (z ^ 1, x) if z in (1, 2) else None


def to_y(far, cores):
    pairs = []
    for z in range(Z):
        end = (z // 2) ^ int(far)
        for x in range(X):
            for c in cores(z):
                pairs.append((device(z, x, 1 - end, c), device(z, x, end, c)))
    return pairs


def both(z):
    return 0, 1


def early_cores(z):
    return (0, 1) if z in (1, 2) else (z % 2,)


def late_cores(z):
    return () if z in (1, 2) else (1 - z % 2,)


OWN_TO_PAIR = [
    (device(z, x, y, 1 - z % 2), device(z ^ 1, x, y, z % 2)) for z in range(Z) for x in range(X) for y in range(Y)]
CORES = [(0, 1), (1, 0), (2, 3), (3, 2)]
CHIPS_Y = [(0, 2), (2, 0), (1, 3), (3, 1)]


def sparse_ladder(amplitudes, integrals, amp_mask, int_mask):
    barrier = lax.optimization_barrier
    tiles = int_mask.size
    cap = 2 * tiles * 11 // 16
    row, col = lax.axis_index("row"), lax.axis_index("col")
    z, x = row // X, row % X
    y, c = col // 2, col % 2
    is_end = ((z == 0) | (z == Z - 1)).astype(jnp.int32)
    home = z % 2 == c

    def move(value, pairs):
        return lax.ppermute(value, AXES, pairs)

    def after(*tokens):
        return lambda *shards: barrier((*shards, tokens))

    near = z // 2 == y
    picks = jnp.stack([
        jnp.where(home, 0, 1),
        jnp.where(home, is_end, jnp.where(is_end, -1, 2)),
        jnp.where(home, 0, 1),
        jnp.where(home, is_end, 2 + is_end),
        jnp.where(home, -1, is_end - 1),
    ] + [jnp.where(near, s, 1 - s) for s in (0, 1, 0, 1, 1)]).astype(jnp.int32)

    place = jnp.stack([jnp.where(near, 0, jnp.where(home | (is_end == 0), 1, 2)), x]).astype(jnp.int32)

    other = lax.ppermute(integrals, "col", CORES)
    other_mask = lax.ppermute(int_mask.T, "col", CORES)
    other_amp_mask = lax.ppermute(amp_mask, "col", CORES)
    swap = jnp.where(home, 0, 1).astype(jnp.int32).reshape(1)
    own = pack_tiles((integrals, other), (int_mask.T, other_mask), swap, cap)
    own, picks, place, other_amp_mask, amplitudes_now = barrier((own, picks, place, other_amp_mask, amplitudes))
    other_amps = lax.ppermute(amplitudes_now, "col", CORES)

    *amps, masked_token = mask_tiles((amplitudes, other_amps), (amp_mask, other_amp_mask))
    own_x, one, centre, tokens = after(masked_token)(
        move(own, moves(across_x)), move(own, OWN_TO_PAIR), move(own, moves(over_centre)))

    a_sum, a_coded, a_rest, token = shard_product(amps, picks, 0, [[own], [one]], tokens, split=True)
    a_far = move(a_coded, to_y(False, both))
    one_x, two_mid, two_end, own_x, a_far, tokens = after(token)(
        move(one, moves(across_x, False)), move(one, moves(over_centre, False)), move(centre, moves(outward, False)),
        own_x, a_far)

    c_sum, c_coded, token = shard_product(amps, picks, 1, [[two_mid], [two_end], [centre]], tokens)
    c_far = move(c_coded, to_y(True, early_cores))
    b_sum, ab_coded, token = shard_product(amps, picks, 2, [[own_x], [one_x]], (token,), a_rest)
    three_end, three_mid_x, two_x_end, two_x_mid, c_far, tokens = after(token)(
        move(two_mid, moves(outward)), move(own_x, moves(over_centre)),
        move(two_end, moves(across_x_ends)), move(two_mid, moves(across_x_middle)), c_far)

    d_sum, d_coded, token = shard_product(
        amps, picks, 3, [[two_x_mid], [two_x_end], [three_mid_x], [three_end]], tokens)
    ab_far = move(ab_coded, to_y(False, both))
    three_x, tokens = after(token)(move(three_end, moves(across_x_ends, False)))

    d_far = move(d_coded, to_y(True, both))
    e_sum, e_coded, token = shard_product(amps, picks, 4, [[three_x]], tokens, held=lambda part: part)
    e_far = move(e_coded, to_y(True, late_cores))
    c_far, _ = barrier((c_far, token))
    c_both, token = add_coded((c_sum,), [both_halves(c_sum, c_far)], (token, lax.ppermute(token, "col", CORES)))
    flags = [token, lax.ppermute(token, "col", CHIPS_Y)]
    a = [a_sum, (a_far, 0), (ab_far, 0)]
    b = [b_sum, *both_halves(b_sum, ab_far, a_rest.shape[0])]
    d = [d_sum, *both_halves(d_sum, d_far)]
    e = [e_sum, *both_halves(e_sum, e_far)]

    def finish():
        return lay_out(place, (a, [c_both], d), (b, d, e))

    return lax.cond(
        jnp.max(sum(flags)) > 0, lambda: dense_ladder(amplitudes, integrals, amp_mask, int_mask), finish)


def solution(mesh):
    in_specs = (P("row", "col"), P("col", "row"), P("row", "col"), P("col", "row"))
    out_specs = P("row", "col")
    here = dict(mesh.shape)
    per_device = sparse_ladder if here == {"row": Z * X, "col": Y * 2} else dense_ladder
    return jax.shard_map(
        per_device, mesh=mesh, in_specs=in_specs, out_specs=out_specs, check_vma=False
    )
```

```python
import jax
import jax.numpy as jnp
from jax import lax
from jax.experimental import pallas as pl
from jax.experimental.pallas import tpu as pltpu
from jax.sharding import PartitionSpec as P

TILE = 128
VMEM_LIMIT = 12 * 1024 * 1024


def expand(mask):
    spread = jnp.repeat(jnp.repeat(mask, TILE, axis=0), TILE, axis=1)
    return spread.astype(jnp.bfloat16)


def dense_ladder(amplitudes, integrals, amp_mask, int_mask):
    rows, cols = lax.axis_size("row"), lax.axis_size("col")
    row, col = lax.axis_index("row"), lax.axis_index("col")
    sparse_amp = amplitudes * expand(amp_mask)
    sparse_int = integrals * expand(int_mask)
    width = integrals.shape[1]
    share = rows * width // cols
    sums = jnp.zeros((amplitudes.shape[0], rows * width), jnp.float32)
    for step in range(rows):
        shard = lax.ppermute(sparse_int, "row", [((r + step) % rows, r) for r in range(rows)]) if step else sparse_int
        part = jnp.dot(sparse_amp, shard, preferred_element_type=jnp.float32)
        sums = lax.dynamic_update_slice(sums, part, (0, (row + step) % rows * width))
    ladder = lax.dynamic_slice(sums, (0, col * share), (sums.shape[0], share))
    for step in range(1, cols):
        part = lax.dynamic_slice(sums, (0, (col + step) % cols * share), (sums.shape[0], share))
        ladder = ladder + lax.ppermute(part, "col", [(c, (c + step) % cols) for c in range(cols)])
    return ladder.astype(jnp.bfloat16)


TOKEN = jax.ShapeDtypeStruct((8, TILE), jnp.float32)
LIGHT = pl.CostEstimate(flops=1, bytes_accessed=1, transcendentals=0)
STEPS = 5
TOP = 12
LOW = 4
BITS = 16 + LOW
GROUP = 128
META = 16


def in_hbm(array):
    return pltpu.with_memory_space_constraint(array, pltpu.HBM)


def call(kernel, name, cost=LIGHT, **kwargs):
    return pl.pallas_call(
        kernel,
        compiler_params=pltpu.CompilerParams(vmem_limit_bytes=VMEM_LIMIT),
        cost_estimate=cost,
        name=name,
        **kwargs,
    )


VMEM = pl.BlockSpec(memory_space=pltpu.VMEM)
SMEM = pl.BlockSpec(memory_space=pltpu.SMEM)
ANY = pl.BlockSpec(memory_space=pl.ANY)


def pack_tiles(shards, masks, swap, cap):
    wide = shards[0].shape[1] // TILE
    tiles = masks[0].size
    count = len(shards)

    def kernel(swap_ref, *refs):
        mask_refs, b_refs, out_ref = refs[:count], refs[count:-1], refs[-1]

        @pl.when(swap_ref[0] == 0)
        def _():
            pack(mask_refs, b_refs, out_ref)

        @pl.when(swap_ref[0] != 0)
        def _():
            pack(mask_refs[::-1], b_refs[::-1], out_ref)

    def pack(mask_refs, b_refs, out_ref):
        place = jnp.int32(0)
        lane = lax.broadcasted_iota(jnp.int32, (META, TILE), 1)
        sub = lax.broadcasted_iota(jnp.int32, (META, TILE), 0)
        meta = jnp.zeros((META, TILE), jnp.float32)
        for s in range(count):
            for t in range(tiles):
                k, n = divmod(t, wide)
                keep = mask_refs[s][n, k] != 0

                @pl.when(keep & (place < cap))
                def _(s=s, k=k, n=n, place=place):
                    at = pl.multiple_of(place * TILE, TILE)
                    out_ref[pl.ds(at, TILE), :] = b_refs[s][k * TILE:(k + 1) * TILE, n * TILE:(n + 1) * TILE]

                place = place + keep.astype(jnp.int32)
                meta = jnp.where((lane == s * tiles + t) & keep, 1.0, meta)
        meta = jnp.where(sub == 0, meta, jnp.where((sub == 1) & (place > cap), 1.0, 0.0))
        out_ref[cap * TILE:, :] = meta.astype(out_ref.dtype)

    return call(
        kernel, "pack_tiles",
        out_shape=jax.ShapeDtypeStruct((cap * TILE + META, TILE), shards[0].dtype),
        in_specs=[SMEM] * (1 + count) + [VMEM] * count,
        out_specs=VMEM,
    )(swap, *masks, *shards)


def mask_tiles(amplitudes, masks):
    rows, cols = amplitudes[0].shape
    count = len(amplitudes)

    def kernel(*refs):
        mask_refs, a_refs, out_refs, token_ref, sem = (
            refs[:count], refs[count:2 * count], refs[2 * count:3 * count], *refs[3 * count:])
        token_ref[...] = jnp.zeros_like(token_ref)
        copies = [
            [pltpu.make_async_copy(a_refs[s].at[pl.ds(at, TILE)], out_refs[s].at[pl.ds(at, TILE)], sem.at[s, at // TILE])
             for at in range(0, rows, TILE)] for s in range(count)]
        for copy in sum(copies, []):
            copy.start()
        for s in range(count):
            for r in range(rows // TILE):
                copies[s][r].wait()
                for t in range(cols // TILE):
                    @pl.when(mask_refs[s][r, t] == 0)
                    def _(s=s, r=r, t=t):
                        out_refs[s][r * TILE:(r + 1) * TILE, t * TILE:(t + 1) * TILE] = jnp.zeros(
                            (TILE, TILE), out_refs[s].dtype)

    return call(
        kernel, "mask_tiles",
        out_shape=tuple(jax.ShapeDtypeStruct(part.shape, part.dtype) for part in amplitudes) + (TOKEN,),
        in_specs=[SMEM] * count + [ANY] * count,
        out_specs=(VMEM,) * (count + 1),
        scratch_shapes=[pltpu.SemaphoreType.DMA((count, rows // TILE))],
    )(*masks, *amplitudes)


def shard_product(amps, picks, step, choices, tokens, before=None, split=False, held=in_hbm):
    rows, depth = amps[0].shape
    count = len(amps)
    height = sum(part.shape[0] for part in choices[0])
    cap = height - META
    wide = 2
    tiles = count * wide * depth // TILE
    word = 16
    first_row = 0 if before is None else before.shape[0]
    half_rows = coded_rows(rows // 2)
    parts = []
    for choice in choices:
        for part in choice:
            if not any(part is p for p in parts):
                parts.append(part)

    def kernel(picks_ref, *refs):
        if first_row:
            before_ref, refs = refs[0], refs[1:]
        token_refs, refs = refs[:len(tokens)], refs[len(tokens):]
        a_refs, refs = refs[:count], refs[count:]
        p_any, refs = refs[:len(parts)], refs[len(parts):]
        out_ref, *coded_refs, token_ref, packed, wide_ref, sem = refs
        pick = picks_ref[step]
        token_ref[...] = sum(ref[...] for ref in token_refs)
        for number, choice in enumerate(choices):
            @pl.when(pick == number)
            def _(choice=choice):
                at = 0
                copies = []
                for part in choice:
                    index = [part is p for p in parts].index(True)
                    copies.append(pltpu.make_async_copy(
                        p_any[index], packed.at[pl.ds(at, part.shape[0])], sem.at[len(copies)]))
                    at += part.shape[0]
                for copy in copies:
                    copy.start()
                for copy in copies:
                    copy.wait()

        @pl.when(pick >= 0)
        def _():
            meta = packed[cap:, :].astype(jnp.float32)
            lane = lax.broadcasted_iota(jnp.int32, meta.shape, 1)
            sub = lax.broadcasted_iota(jnp.int32, meta.shape, 0)
            first = (sub == 0) & (meta != 0)
            bits = [
                jnp.sum(jnp.where(
                    first & (lane >= lo) & (lane < lo + word), jnp.left_shift(1, (lane - lo) & (word - 1)), 0))
                for lo in range(0, tiles, word)]
            token_ref[...] += jnp.where(sub == 1, meta, 0.0)[:token_ref.shape[0]]
            place = jnp.int32(0)
            for s in range(count):
                for t in range(s * tiles // count, (s + 1) * tiles // count):
                    k, n = divmod(t, wide)
                    keep = ((bits[t // word] >> (t % word)) & 1) != 0
                    at = pl.multiple_of(jnp.minimum(place * TILE, cap - TILE), TILE)
                    tile = packed[pl.ds(at, TILE), :]
                    wide_ref[k * TILE:(k + 1) * TILE, n * TILE:(n + 1) * TILE] = jnp.where(
                        keep, tile, jnp.zeros_like(tile))
                    place = place + keep.astype(jnp.int32)
                term = jnp.dot(
                    a_refs[s][...], wide_ref[s * depth:(s + 1) * depth, :], preferred_element_type=jnp.float32)
                if s:
                    out_ref[...] += term
                else:
                    out_ref[...] = term

        @pl.when((pick >= 0) & (picks_ref[STEPS + step] != 0))
        def _():
            if first_row:
                coded_refs[0][:first_row, :] = before_ref[...]
            for h, (first, length, at) in enumerate(halves(rows, first_row)):
                spot = coded_refs[h] if split else coded_refs[0].at[pl.ds(at, coded_rows(length))]
                encode(out_ref.at[pl.ds(first, length)], spot)

    return call(
        kernel, "shard_product",
        out_shape=(
            jax.ShapeDtypeStruct((rows, wide * TILE), jnp.float32),
            *([jax.ShapeDtypeStruct((half_rows, wide * TILE), jnp.int16)] * 2 if split else
              [jax.ShapeDtypeStruct((first_row + 2 * half_rows, wide * TILE), jnp.int16)]),
            TOKEN),
        in_specs=[SMEM] + [VMEM] * (bool(first_row) + len(tokens) + count) + [ANY] * len(parts),
        out_specs=(VMEM,) * (4 if split else 3),
        scratch_shapes=[
            pltpu.VMEM((height, TILE), amps[0].dtype),
            pltpu.VMEM((count * depth, wide * TILE), amps[0].dtype),
            pltpu.SemaphoreType.DMA((2,)),
        ],
    )(picks, *([before] if first_row else []), *tokens, *amps, *map(held, parts))


def coded_rows(rows):
    return rows + rows // (16 // LOW) + META


def halves(rows, first_row=0):
    half = rows // 2
    return [(h * half, half, first_row + h * coded_rows(half)) for h in range(2)]


def step_factors(exponent):
    power = BITS - 1 - TOP - exponent
    factors = []
    for part in (power // 2, power - power // 2):
        factor = jnp.ones(part.shape, jnp.float32)
        for bit in range(7):
            factor = factor * jnp.where((part >> bit) & 1 != 0, 2.0 ** (1 << bit), 1.0)
        factors.append(factor)
    return factors


def encode(sums_ref, coded_ref):
    rows, cols = sums_ref.shape
    groups = rows // GROUP
    largest = jnp.concatenate([
        jnp.max(jnp.abs(sums_ref[g * GROUP:(g + 1) * GROUP, :]), axis=0, keepdims=True) for g in range(groups)])
    rest = largest * 2.0 ** -TOP
    exponent = jnp.zeros(rest.shape, jnp.int32)
    for bit in (64, 32, 16, 8, 4, 2, 1):
        small = rest < 2.0 ** -bit
        rest = jnp.where(small, rest * 2.0 ** bit, rest)
        exponent = jnp.where(small, exponent - bit, exponent)
    one, two = step_factors(exponent)
    share = 16 // LOW
    block = rows // share
    for start in range(0, block, GROUP):
        low = jnp.zeros((GROUP, cols), jnp.int32)
        for part in range(share):
            at = part * block + start
            g = at // GROUP
            value = sums_ref[at:at + GROUP, :] * one[g:g + 1] * two[g:g + 1]
            value = jnp.minimum(jnp.round(value).astype(jnp.int32), (1 << (BITS - 1)) - 1)
            coded_ref[at:at + GROUP, :] = (value >> LOW).astype(jnp.int16)
            low = low | ((value & ((1 << LOW) - 1)) << (LOW * part))
        coded_ref[rows + start:rows + start + GROUP, :] = (low - 32768).astype(jnp.int16)
    coded_ref[rows + block:, :] = jnp.concatenate([exponent] * (META // groups)).astype(jnp.int16)


def decode(coded_ref, rows, put):
    groups = rows // GROUP
    share = 16 // LOW
    block = rows // share
    one, two = step_factors(coded_ref[rows + block:, :].astype(jnp.int32)[:groups])
    one, two = 1.0 / one, 1.0 / two
    for start in range(0, block, GROUP):
        low = coded_ref[rows + start:rows + start + GROUP, :].astype(jnp.int32) + 32768
        for part in range(share):
            at = part * block + start
            g = at // GROUP
            high = coded_ref[at:at + GROUP, :].astype(jnp.int32)
            value = (high << LOW) | ((low >> (LOW * part)) & ((1 << LOW) - 1))
            put(at, value.astype(jnp.float32) * one[g:g + 1] * two[g:g + 1])


def add_coded(sums, coded, tokens=()):
    count = len(sums)
    arrays = []
    for array, _ in [pair for one in coded for pair in one]:
        if not any(array is known for known in arrays):
            arrays.append(array)

    def kernel(*refs):
        token_refs, refs = refs[:len(tokens)], refs[len(tokens):]
        sums_refs, coded_refs, out_refs, token_ref = refs[:count], refs[count:-count - 1], refs[-count - 1:-1], refs[-1]
        token_ref[...] = sum((ref[...] for ref in token_refs), jnp.zeros(token_ref.shape, token_ref.dtype))
        for number in range(count):
            for (first, length, _), (array, at) in zip(halves(sums[number].shape[0]), coded[number]):
                ref = coded_refs[[array is known for known in arrays].index(True)]
                add_half(sums_refs[number], ref.at[pl.ds(at, coded_rows(length))], out_refs[number], first, length)

    return call(
        kernel, "add_coded",
        out_shape=tuple(jax.ShapeDtypeStruct(part.shape, jnp.bfloat16) for part in sums) + (TOKEN,),
        in_specs=[VMEM] * (len(tokens) + count + len(arrays)),
        out_specs=(VMEM,) * (count + 1),
    )(*tokens, *sums, *arrays)


def add_half(sums_ref, coded_ref, out_ref, first, length):
    def put(at, far):
        spot = pl.ds(first + at, GROUP)
        out_ref[spot, :] = (sums_ref[spot, :] + far).astype(out_ref.dtype)

    decode(coded_ref, length, put)


def both_halves(sums, coded, first_row=0):
    return [(coded, at) for _, _, at in halves(sums.shape[0], first_row)]


def lay_out(place, mine, rest):
    choices = list(zip(mine, rest))
    arrays = []
    for choice in choices:
        for sums, *coded in choice:
            for array in (sums, *[array for array, _ in coded]):
                if not any(array is known for known in arrays):
                    arrays.append(array)
    rows, width = arrays[0].shape
    parts = halves(rows)

    def kernel(place_ref, *refs):
        ins = refs[:len(arrays)]
        out_any, round_ref, sums_ref, coded_ref, sems = refs[len(arrays):]

        def place_of(array):
            return ins[[array is known for known in arrays].index(True)]

        def store(side, first, length):
            at = pl.multiple_of((place_ref[1] ^ side) * width, width)
            return pltpu.make_async_copy(
                round_ref.at[side, pl.ds(first, length)], out_any.at[pl.ds(first, length), pl.ds(at, width)],
                sems.at[2, 2 * side + first // length])

        for number, choice in enumerate(choices):
            @pl.when(place_ref[0] == number)
            def _(choice=choice):
                fetch = {}
                for side, (sums, *coded) in enumerate(choice):
                    for h, (first, length, _) in enumerate(parts):
                        fetch[side, h] = [pltpu.make_async_copy(
                            place_of(sums).at[pl.ds(first, length)],
                            (sums_ref if coded else round_ref).at[side, pl.ds(first, length)], sems.at[0, 2 * side + h])]
                        if coded:
                            array, at = coded[h]
                            fetch[side, h].append(pltpu.make_async_copy(
                                place_of(array).at[pl.ds(at, coded_rows(length))], coded_ref.at[side, h],
                                sems.at[1, 2 * side + h]))
                for copy in sum(fetch.values(), []):
                    copy.start()
                for side, (sums, *coded) in enumerate(choice):
                    for h, (first, length, _) in enumerate(parts):
                        for copy in fetch[side, h]:
                            copy.wait()
                        if coded:
                            add_half(sums_ref.at[side], coded_ref.at[side, h], round_ref.at[side], first, length)
                        store(side, first, length).start()

        for side in range(2):
            for first, length, _ in parts:
                store(side, first, length).wait()

    return call(
        kernel, "lay_out",
        out_shape=pltpu.HBM((rows, 2 * width), jnp.bfloat16),
        in_specs=[SMEM] + [ANY] * len(arrays),
        out_specs=ANY,
        scratch_shapes=[
            pltpu.VMEM((2, rows, width), jnp.bfloat16),
            pltpu.VMEM((2, rows, width), jnp.float32),
            pltpu.VMEM((2, 2, coded_rows(rows // 2), width), jnp.int16),
            pltpu.SemaphoreType.DMA((3, 4))],
    )(place, *arrays)


Z, X, Y = 4, 2, 2
AXES = ("row", "col")


def device(z, x, y, c):
    return (z * X + x) * Y * 2 + y * 2 + c


def moves(to, home=True):
    pairs = []
    for z in range(Z):
        for x in range(X):
            for y in range(Y):
                if to(z, x) is not None:
                    c = z % 2 if home else 1 - z % 2
                    pairs.append((device(z, x, y, c), device(*to(z, x), y, c)))
    return pairs


def across_x(z, x):
    return z, 1 - x


def across_x_ends(z, x):
    return (z, 1 - x) if z in (0, 3) else None


def across_x_middle(z, x):
    return (z, 1 - x) if z in (1, 2) else None


def over_centre(z, x):
    return (3 - z, x) if z in (1, 2) else None


def outward(z, x):
    return (z ^ 1, x) if z in (1, 2) else None


def to_y(far, cores):
    pairs = []
    for z in range(Z):
        end = (z // 2) ^ int(far)
        for x in range(X):
            for c in cores(z):
                pairs.append((device(z, x, 1 - end, c), device(z, x, end, c)))
    return pairs


def both(z):
    return 0, 1


def early_cores(z):
    return (0, 1) if z in (1, 2) else (z % 2,)


def late_cores(z):
    return () if z in (1, 2) else (1 - z % 2,)


OWN_TO_PAIR = [
    (device(z, x, y, 1 - z % 2), device(z ^ 1, x, y, z % 2)) for z in range(Z) for x in range(X) for y in range(Y)]
CORES = [(0, 1), (1, 0), (2, 3), (3, 2)]
CHIPS_Y = [(0, 2), (2, 0), (1, 3), (3, 1)]


def sparse_ladder(amplitudes, integrals, amp_mask, int_mask):
    barrier = lax.optimization_barrier
    tiles = int_mask.size
    cap = 2 * tiles * 11 // 16
    row, col = lax.axis_index("row"), lax.axis_index("col")
    z, x = row // X, row % X
    y, c = col // 2, col % 2
    is_end = ((z == 0) | (z == Z - 1)).astype(jnp.int32)
    home = z % 2 == c

    def move(value, pairs):
        return lax.ppermute(value, AXES, pairs)

    def after(*tokens):
        return lambda *shards: barrier((*shards, tokens))

    near = z // 2 == y
    picks = jnp.stack([
        jnp.where(home, 0, 1),
        jnp.where(home, is_end, jnp.where(is_end, -1, 2)),
        jnp.where(home, 0, 1),
        jnp.where(home, is_end, 2 + is_end),
        jnp.where(home, -1, is_end - 1),
    ] + [jnp.where(near, s, 1 - s) for s in (0, 1, 0, 1, 1)]).astype(jnp.int32)

    place = jnp.stack([jnp.where(near, 0, jnp.where(home | (is_end == 0), 1, 2)), x]).astype(jnp.int32)

    other = lax.ppermute(integrals, "col", CORES)
    other_mask = lax.ppermute(int_mask.T, "col", CORES)
    other_amp_mask = lax.ppermute(amp_mask, "col", CORES)
    swap = jnp.where(home, 0, 1).astype(jnp.int32).reshape(1)
    own = pack_tiles((integrals, other), (int_mask.T, other_mask), swap, cap)
    own, picks, place, other_amp_mask, amplitudes_now = barrier((own, picks, place, other_amp_mask, amplitudes))
    other_amps = lax.ppermute(amplitudes_now, "col", CORES)

    *amps, masked_token = mask_tiles((amplitudes, other_amps), (amp_mask, other_amp_mask))
    own_x, one, centre, tokens = after(masked_token)(
        move(own, moves(across_x)), move(own, OWN_TO_PAIR), move(own, moves(over_centre)))

    a_sum, a_coded, a_rest, token = shard_product(amps, picks, 0, [[own], [one]], tokens, split=True)
    a_far = move(a_coded, to_y(False, both))
    one_x, two_mid, two_end, own_x, a_far, tokens = after(token)(
        move(one, moves(across_x, False)), move(one, moves(over_centre, False)), move(centre, moves(outward, False)),
        own_x, a_far)

    c_sum, c_coded, token = shard_product(amps, picks, 1, [[two_mid], [two_end], [centre]], tokens)
    c_far = move(c_coded, to_y(True, early_cores))
    b_sum, ab_coded, token = shard_product(amps, picks, 2, [[own_x], [one_x]], (token,), a_rest)
    two_x_end, three_end, two_x_mid, three_mid_x, c_far, tokens = after(token)(
        move(two_end, moves(across_x_ends)), move(two_mid, moves(outward)),
        move(two_mid, moves(across_x_middle)), move(own_x, moves(over_centre)), c_far)

    d_sum, d_coded, token = shard_product(
        amps, picks, 3, [[two_x_mid], [two_x_end], [three_mid_x], [three_end]], tokens)
    ab_far = move(ab_coded, to_y(False, both))
    three_x, tokens = after(token)(move(three_end, moves(across_x_ends, False)))

    d_far = move(d_coded, to_y(True, both))
    e_sum, e_coded, token = shard_product(amps, picks, 4, [[three_x]], tokens, held=lambda part: part)
    e_far = move(e_coded, to_y(True, late_cores))
    c_far, _ = barrier((c_far, token))
    c_both, token = add_coded((c_sum,), [both_halves(c_sum, c_far)], (token, lax.ppermute(token, "col", CORES)))
    flags = [token, lax.ppermute(token, "col", CHIPS_Y)]
    a = [a_sum, (a_far, 0), (ab_far, 0)]
    b = [b_sum, *both_halves(b_sum, ab_far, a_rest.shape[0])]
    d = [d_sum, *both_halves(d_sum, d_far)]
    e = [e_sum, *both_halves(e_sum, e_far)]

    def finish():
        return lay_out(place, (a, [c_both], d), (b, d, e))

    return lax.cond(
        jnp.max(sum(flags)) > 0, lambda: dense_ladder(amplitudes, integrals, amp_mask, int_mask), finish)


def solution(mesh):
    in_specs = (P("row", "col"), P("col", "row"), P("row", "col"), P("col", "row"))
    out_specs = P("row", "col")
    here = dict(mesh.shape)
    per_device = sparse_ladder if here == {"row": Z * X, "col": Y * 2} else dense_ladder
    return jax.shard_map(
        per_device, mesh=mesh, in_specs=in_specs, out_specs=out_specs, check_vma=False
    )
```

```python
import jax
import jax.numpy as jnp
from jax import lax
from jax.experimental import pallas as pl
from jax.experimental.pallas import tpu as pltpu
from jax.sharding import PartitionSpec as P

TILE = 128
VMEM_LIMIT = 12 * 1024 * 1024


def expand(mask):
    spread = jnp.repeat(jnp.repeat(mask, TILE, axis=0), TILE, axis=1)
    return spread.astype(jnp.bfloat16)


def dense_ladder(amplitudes, integrals, amp_mask, int_mask):
    rows, cols = lax.axis_size("row"), lax.axis_size("col")
    row, col = lax.axis_index("row"), lax.axis_index("col")
    sparse_amp = amplitudes * expand(amp_mask)
    sparse_int = integrals * expand(int_mask)
    width = integrals.shape[1]
    share = rows * width // cols
    sums = jnp.zeros((amplitudes.shape[0], rows * width), jnp.float32)
    for step in range(rows):
        shard = lax.ppermute(sparse_int, "row", [((r + step) % rows, r) for r in range(rows)]) if step else sparse_int
        part = jnp.dot(sparse_amp, shard, preferred_element_type=jnp.float32)
        sums = lax.dynamic_update_slice(sums, part, (0, (row + step) % rows * width))
    ladder = lax.dynamic_slice(sums, (0, col * share), (sums.shape[0], share))
    for step in range(1, cols):
        part = lax.dynamic_slice(sums, (0, (col + step) % cols * share), (sums.shape[0], share))
        ladder = ladder + lax.ppermute(part, "col", [(c, (c + step) % cols) for c in range(cols)])
    return ladder.astype(jnp.bfloat16)


TOKEN = jax.ShapeDtypeStruct((8, TILE), jnp.float32)
LIGHT = pl.CostEstimate(flops=1, bytes_accessed=1, transcendentals=0)
STEPS = 5
TOP = 12
LOW = 4
BITS = 16 + LOW
GROUP = 128
META = 16


def in_hbm(array):
    return pltpu.with_memory_space_constraint(array, pltpu.HBM)


def call(kernel, name, cost=LIGHT, **kwargs):
    return pl.pallas_call(
        kernel,
        compiler_params=pltpu.CompilerParams(vmem_limit_bytes=VMEM_LIMIT),
        cost_estimate=cost,
        name=name,
        **kwargs,
    )


VMEM = pl.BlockSpec(memory_space=pltpu.VMEM)
SMEM = pl.BlockSpec(memory_space=pltpu.SMEM)
ANY = pl.BlockSpec(memory_space=pl.ANY)


def pack_tiles(shards, masks, swap, cap):
    wide = shards[0].shape[1] // TILE
    tiles = masks[0].size
    count = len(shards)

    def kernel(swap_ref, *refs):
        mask_refs, b_refs, out_ref = refs[:count], refs[count:-1], refs[-1]

        @pl.when(swap_ref[0] == 0)
        def _():
            pack(mask_refs, b_refs, out_ref)

        @pl.when(swap_ref[0] != 0)
        def _():
            pack(mask_refs[::-1], b_refs[::-1], out_ref)

    def pack(mask_refs, b_refs, out_ref):
        place = jnp.int32(0)
        lane = lax.broadcasted_iota(jnp.int32, (META, TILE), 1)
        sub = lax.broadcasted_iota(jnp.int32, (META, TILE), 0)
        meta = jnp.zeros((META, TILE), jnp.float32)
        for s in range(count):
            for t in range(tiles):
                k, n = divmod(t, wide)
                keep = mask_refs[s][n, k] != 0

                @pl.when(keep & (place < cap))
                def _(s=s, k=k, n=n, place=place):
                    at = pl.multiple_of(place * TILE, TILE)
                    out_ref[pl.ds(at, TILE), :] = b_refs[s][k * TILE:(k + 1) * TILE, n * TILE:(n + 1) * TILE]

                place = place + keep.astype(jnp.int32)
                meta = jnp.where((lane == s * tiles + t) & keep, 1.0, meta)
        meta = jnp.where(sub == 0, meta, jnp.where((sub == 1) & (place > cap), 1.0, 0.0))
        out_ref[cap * TILE:, :] = meta.astype(out_ref.dtype)

    return call(
        kernel, "pack_tiles",
        out_shape=jax.ShapeDtypeStruct((cap * TILE + META, TILE), shards[0].dtype),
        in_specs=[SMEM] * (1 + count) + [VMEM] * count,
        out_specs=VMEM,
    )(swap, *masks, *shards)


def mask_tiles(amplitudes, masks):
    rows, cols = amplitudes[0].shape
    count = len(amplitudes)

    def kernel(*refs):
        mask_refs, a_refs, out_refs, token_ref, sem = (
            refs[:count], refs[count:2 * count], refs[2 * count:3 * count], *refs[3 * count:])
        token_ref[...] = jnp.zeros_like(token_ref)
        copies = [
            [pltpu.make_async_copy(a_refs[s].at[pl.ds(at, TILE)], out_refs[s].at[pl.ds(at, TILE)], sem.at[s, at // TILE])
             for at in range(0, rows, TILE)] for s in range(count)]
        for copy in sum(copies, []):
            copy.start()
        for s in range(count):
            for r in range(rows // TILE):
                copies[s][r].wait()
                for t in range(cols // TILE):
                    @pl.when(mask_refs[s][r, t] == 0)
                    def _(s=s, r=r, t=t):
                        out_refs[s][r * TILE:(r + 1) * TILE, t * TILE:(t + 1) * TILE] = jnp.zeros(
                            (TILE, TILE), out_refs[s].dtype)

    return call(
        kernel, "mask_tiles",
        out_shape=tuple(jax.ShapeDtypeStruct(part.shape, part.dtype) for part in amplitudes) + (TOKEN,),
        in_specs=[SMEM] * count + [ANY] * count,
        out_specs=(VMEM,) * (count + 1),
        scratch_shapes=[pltpu.SemaphoreType.DMA((count, rows // TILE))],
    )(*masks, *amplitudes)


def shard_product(amps, picks, step, choices, tokens, before=None, split=False, held=in_hbm):
    rows, depth = amps[0].shape
    count = len(amps)
    height = sum(part.shape[0] for part in choices[0])
    cap = height - META
    wide = 2
    tiles = count * wide * depth // TILE
    word = 16
    first_row = 0 if before is None else before.shape[0]
    half_rows = coded_rows(rows // 2)
    parts = []
    for choice in choices:
        for part in choice:
            if not any(part is p for p in parts):
                parts.append(part)

    def kernel(picks_ref, *refs):
        if first_row:
            before_ref, refs = refs[0], refs[1:]
        token_refs, refs = refs[:len(tokens)], refs[len(tokens):]
        a_refs, refs = refs[:count], refs[count:]
        p_any, refs = refs[:len(parts)], refs[len(parts):]
        out_ref, *coded_refs, token_ref, packed, wide_ref, sem = refs
        pick = picks_ref[step]
        token_ref[...] = sum(ref[...] for ref in token_refs)
        for number, choice in enumerate(choices):
            @pl.when(pick == number)
            def _(choice=choice):
                at = 0
                copies = []
                for part in choice:
                    index = [part is p for p in parts].index(True)
                    copies.append(pltpu.make_async_copy(
                        p_any[index], packed.at[pl.ds(at, part.shape[0])], sem.at[len(copies)]))
                    at += part.shape[0]
                for copy in copies:
                    copy.start()
                for copy in copies:
                    copy.wait()

        @pl.when(pick >= 0)
        def _():
            meta = packed[cap:, :].astype(jnp.float32)
            lane = lax.broadcasted_iota(jnp.int32, meta.shape, 1)
            sub = lax.broadcasted_iota(jnp.int32, meta.shape, 0)
            first = (sub == 0) & (meta != 0)
            bits = [
                jnp.sum(jnp.where(
                    first & (lane >= lo) & (lane < lo + word), jnp.left_shift(1, (lane - lo) & (word - 1)), 0))
                for lo in range(0, tiles, word)]
            token_ref[...] += jnp.where(sub == 1, meta, 0.0)[:token_ref.shape[0]]
            place = jnp.int32(0)
            for s in range(count):
                for t in range(s * tiles // count, (s + 1) * tiles // count):
                    k, n = divmod(t, wide)
                    keep = ((bits[t // word] >> (t % word)) & 1) != 0
                    at = pl.multiple_of(jnp.minimum(place * TILE, cap - TILE), TILE)
                    tile = packed[pl.ds(at, TILE), :]
                    wide_ref[k * TILE:(k + 1) * TILE, n * TILE:(n + 1) * TILE] = jnp.where(
                        keep, tile, jnp.zeros_like(tile))
                    place = place + keep.astype(jnp.int32)
                term = jnp.dot(
                    a_refs[s][...], wide_ref[s * depth:(s + 1) * depth, :], preferred_element_type=jnp.float32)
                if s:
                    out_ref[...] += term
                else:
                    out_ref[...] = term

        @pl.when((pick >= 0) & (picks_ref[STEPS + step] != 0))
        def _():
            if first_row:
                coded_refs[0][:first_row, :] = before_ref[...]
            for h, (first, length, at) in enumerate(halves(rows, first_row)):
                spot = coded_refs[h] if split else coded_refs[0].at[pl.ds(at, coded_rows(length))]
                encode(out_ref.at[pl.ds(first, length)], spot)

    return call(
        kernel, "shard_product",
        out_shape=(
            jax.ShapeDtypeStruct((rows, wide * TILE), jnp.float32),
            *([jax.ShapeDtypeStruct((half_rows, wide * TILE), jnp.int16)] * 2 if split else
              [jax.ShapeDtypeStruct((first_row + 2 * half_rows, wide * TILE), jnp.int16)]),
            TOKEN),
        in_specs=[SMEM] + [VMEM] * (bool(first_row) + len(tokens) + count) + [ANY] * len(parts),
        out_specs=(VMEM,) * (4 if split else 3),
        scratch_shapes=[
            pltpu.VMEM((height, TILE), amps[0].dtype),
            pltpu.VMEM((count * depth, wide * TILE), amps[0].dtype),
            pltpu.SemaphoreType.DMA((2,)),
        ],
    )(picks, *([before] if first_row else []), *tokens, *amps, *map(held, parts))


def coded_rows(rows):
    return rows + rows // (16 // LOW) + META


def halves(rows, first_row=0):
    half = rows // 2
    return [(h * half, half, first_row + h * coded_rows(half)) for h in range(2)]


def step_factors(exponent):
    power = BITS - 1 - TOP - exponent
    factors = []
    for part in (power // 2, power - power // 2):
        factor = jnp.ones(part.shape, jnp.float32)
        for bit in range(7):
            factor = factor * jnp.where((part >> bit) & 1 != 0, 2.0 ** (1 << bit), 1.0)
        factors.append(factor)
    return factors


def encode(sums_ref, coded_ref):
    rows, cols = sums_ref.shape
    groups = rows // GROUP
    largest = jnp.concatenate([
        jnp.max(jnp.abs(sums_ref[g * GROUP:(g + 1) * GROUP, :]), axis=0, keepdims=True) for g in range(groups)])
    rest = largest * 2.0 ** -TOP
    exponent = jnp.zeros(rest.shape, jnp.int32)
    for bit in (64, 32, 16, 8, 4, 2, 1):
        small = rest < 2.0 ** -bit
        rest = jnp.where(small, rest * 2.0 ** bit, rest)
        exponent = jnp.where(small, exponent - bit, exponent)
    one, two = step_factors(exponent)
    share = 16 // LOW
    block = rows // share
    for start in range(0, block, GROUP):
        low = jnp.zeros((GROUP, cols), jnp.int32)
        for part in range(share):
            at = part * block + start
            g = at // GROUP
            value = sums_ref[at:at + GROUP, :] * one[g:g + 1] * two[g:g + 1]
            value = jnp.minimum(jnp.round(value).astype(jnp.int32), (1 << (BITS - 1)) - 1)
            coded_ref[at:at + GROUP, :] = (value >> LOW).astype(jnp.int16)
            low = low | ((value & ((1 << LOW) - 1)) << (LOW * part))
        coded_ref[rows + start:rows + start + GROUP, :] = (low - 32768).astype(jnp.int16)
    coded_ref[rows + block:, :] = jnp.concatenate([exponent] * (META // groups)).astype(jnp.int16)


def decode(coded_ref, rows, put):
    groups = rows // GROUP
    share = 16 // LOW
    block = rows // share
    one, two = step_factors(coded_ref[rows + block:, :].astype(jnp.int32)[:groups])
    one, two = 1.0 / one, 1.0 / two
    for start in range(0, block, GROUP):
        low = coded_ref[rows + start:rows + start + GROUP, :].astype(jnp.int32) + 32768
        for part in range(share):
            at = part * block + start
            g = at // GROUP
            high = coded_ref[at:at + GROUP, :].astype(jnp.int32)
            value = (high << LOW) | ((low >> (LOW * part)) & ((1 << LOW) - 1))
            put(at, value.astype(jnp.float32) * one[g:g + 1] * two[g:g + 1])


def add_coded(sums, coded, tokens=()):
    count = len(sums)
    arrays = []
    for array, _ in [pair for one in coded for pair in one]:
        if not any(array is known for known in arrays):
            arrays.append(array)

    def kernel(*refs):
        token_refs, refs = refs[:len(tokens)], refs[len(tokens):]
        sums_refs, coded_refs, out_refs, token_ref = refs[:count], refs[count:-count - 1], refs[-count - 1:-1], refs[-1]
        token_ref[...] = sum((ref[...] for ref in token_refs), jnp.zeros(token_ref.shape, token_ref.dtype))
        for number in range(count):
            for (first, length, _), (array, at) in zip(halves(sums[number].shape[0]), coded[number]):
                ref = coded_refs[[array is known for known in arrays].index(True)]
                add_half(sums_refs[number], ref.at[pl.ds(at, coded_rows(length))], out_refs[number], first, length)

    return call(
        kernel, "add_coded",
        out_shape=tuple(jax.ShapeDtypeStruct(part.shape, jnp.bfloat16) for part in sums) + (TOKEN,),
        in_specs=[VMEM] * (len(tokens) + count + len(arrays)),
        out_specs=(VMEM,) * (count + 1),
    )(*tokens, *sums, *arrays)


def add_half(sums_ref, coded_ref, out_ref, first, length):
    def put(at, far):
        spot = pl.ds(first + at, GROUP)
        out_ref[spot, :] = (sums_ref[spot, :] + far).astype(out_ref.dtype)

    decode(coded_ref, length, put)


def both_halves(sums, coded, first_row=0):
    return [(coded, at) for _, _, at in halves(sums.shape[0], first_row)]


def lay_out(place, mine, rest):
    choices = list(zip(mine, rest))
    arrays = []
    for choice in choices:
        for sums, *coded in choice:
            for array in (sums, *[array for array, _ in coded]):
                if not any(array is known for known in arrays):
                    arrays.append(array)
    rows, width = arrays[0].shape
    parts = halves(rows)

    def kernel(place_ref, *refs):
        ins = refs[:len(arrays)]
        out_any, round_ref, sums_ref, coded_ref, sems = refs[len(arrays):]

        def place_of(array):
            return ins[[array is known for known in arrays].index(True)]

        def store(side, first, length):
            at = pl.multiple_of((place_ref[1] ^ side) * width, width)
            return pltpu.make_async_copy(
                round_ref.at[side, pl.ds(first, length)], out_any.at[pl.ds(first, length), pl.ds(at, width)],
                sems.at[2, 2 * side + first // length])

        for number, choice in enumerate(choices):
            @pl.when(place_ref[0] == number)
            def _(choice=choice):
                fetch = {}
                for side, (sums, *coded) in enumerate(choice):
                    for h, (first, length, _) in enumerate(parts):
                        fetch[side, h] = [pltpu.make_async_copy(
                            place_of(sums).at[pl.ds(first, length)],
                            (sums_ref if coded else round_ref).at[side, pl.ds(first, length)], sems.at[0, 2 * side + h])]
                        if coded:
                            array, at = coded[h]
                            fetch[side, h].append(pltpu.make_async_copy(
                                place_of(array).at[pl.ds(at, coded_rows(length))], coded_ref.at[side, h],
                                sems.at[1, 2 * side + h]))
                for copy in sum(fetch.values(), []):
                    copy.start()
                for side, (sums, *coded) in enumerate(choice):
                    for h, (first, length, _) in enumerate(parts):
                        for copy in fetch[side, h]:
                            copy.wait()
                        if coded:
                            add_half(sums_ref.at[side], coded_ref.at[side, h], round_ref.at[side], first, length)
                        store(side, first, length).start()

        for side in range(2):
            for first, length, _ in parts:
                store(side, first, length).wait()

    return call(
        kernel, "lay_out",
        out_shape=pltpu.HBM((rows, 2 * width), jnp.bfloat16),
        in_specs=[SMEM] + [ANY] * len(arrays),
        out_specs=ANY,
        scratch_shapes=[
            pltpu.VMEM((2, rows, width), jnp.bfloat16),
            pltpu.VMEM((2, rows, width), jnp.float32),
            pltpu.VMEM((2, 2, coded_rows(rows // 2), width), jnp.int16),
            pltpu.SemaphoreType.DMA((3, 4))],
    )(place, *arrays)


Z, X, Y = 4, 2, 2
AXES = ("row", "col")


def device(z, x, y, c):
    return (z * X + x) * Y * 2 + y * 2 + c


def moves(to, home=True):
    pairs = []
    for z in range(Z):
        for x in range(X):
            for y in range(Y):
                if to(z, x) is not None:
                    c = z % 2 if home else 1 - z % 2
                    pairs.append((device(z, x, y, c), device(*to(z, x), y, c)))
    return pairs


def across_x(z, x):
    return z, 1 - x


def across_x_ends(z, x):
    return (z, 1 - x) if z in (0, 3) else None


def across_x_middle(z, x):
    return (z, 1 - x) if z in (1, 2) else None


def over_centre(z, x):
    return (3 - z, x) if z in (1, 2) else None


def outward(z, x):
    return (z ^ 1, x) if z in (1, 2) else None


def to_y(far, cores):
    pairs = []
    for z in range(Z):
        end = (z // 2) ^ int(far)
        for x in range(X):
            for c in cores(z):
                pairs.append((device(z, x, 1 - end, c), device(z, x, end, c)))
    return pairs


def both(z):
    return 0, 1


def early_cores(z):
    return (0, 1) if z in (1, 2) else (z % 2,)


def late_cores(z):
    return () if z in (1, 2) else (1 - z % 2,)


OWN_TO_PAIR = [
    (device(z, x, y, 1 - z % 2), device(z ^ 1, x, y, z % 2)) for z in range(Z) for x in range(X) for y in range(Y)]
CORES = [(0, 1), (1, 0), (2, 3), (3, 2)]
CHIPS_Y = [(0, 2), (2, 0), (1, 3), (3, 1)]


def sparse_ladder(amplitudes, integrals, amp_mask, int_mask):
    barrier = lax.optimization_barrier
    tiles = int_mask.size
    cap = 2 * tiles * 11 // 16
    row, col = lax.axis_index("row"), lax.axis_index("col")
    z, x = row // X, row % X
    y, c = col // 2, col % 2
    is_end = ((z == 0) | (z == Z - 1)).astype(jnp.int32)
    home = z % 2 == c

    def move(value, pairs):
        return lax.ppermute(value, AXES, pairs)

    def after(*tokens):
        return lambda *shards: barrier((*shards, tokens))

    near = z // 2 == y
    picks = jnp.stack([
        jnp.where(home, 0, 1),
        jnp.where(home, is_end, jnp.where(is_end, -1, 2)),
        jnp.where(home, 0, 1),
        jnp.where(home, is_end, 2 + is_end),
        jnp.where(home, -1, is_end - 1),
    ] + [jnp.where(near, s, 1 - s) for s in (0, 1, 0, 1, 1)]).astype(jnp.int32)

    place = jnp.stack([jnp.where(near, 0, jnp.where(home | (is_end == 0), 1, 2)), x]).astype(jnp.int32)

    other = lax.ppermute(integrals, "col", CORES)
    other_mask = lax.ppermute(int_mask.T, "col", CORES)
    other_amp_mask = lax.ppermute(amp_mask, "col", CORES)
    swap = jnp.where(home, 0, 1).astype(jnp.int32).reshape(1)
    own = pack_tiles((integrals, other), (int_mask.T, other_mask), swap, cap)
    own, picks, place, other_amp_mask, amplitudes_now = barrier((own, picks, place, other_amp_mask, amplitudes))
    other_amps = lax.ppermute(amplitudes_now, "col", CORES)

    *amps, masked_token = mask_tiles((amplitudes, other_amps), (amp_mask, other_amp_mask))
    own_x, one, centre, tokens = after(masked_token)(
        move(own, moves(across_x)), move(own, OWN_TO_PAIR), move(own, moves(over_centre)))

    a_sum, a_coded, a_rest, token = shard_product(amps, picks, 0, [[own], [one]], tokens, split=True)
    a_far = move(a_coded, to_y(False, both))
    one_x, two_mid, two_end, own_x, a_far, tokens = after(token)(
        move(one, moves(across_x, False)), move(one, moves(over_centre, False)), move(centre, moves(outward, False)),
        own_x, a_far)

    c_sum, c_coded, token = shard_product(amps, picks, 1, [[two_mid], [two_end], [centre]], tokens)
    c_far = move(c_coded, to_y(True, early_cores))
    b_sum, ab_coded, token = shard_product(amps, picks, 2, [[own_x], [one_x]], (token,), a_rest)
    two_x_end, three_end, two_x_mid, three_mid_x, c_far, tokens = after(token)(
        move(two_end, moves(across_x_ends)), move(two_mid, moves(outward)),
        move(two_mid, moves(across_x_middle)), move(own_x, moves(over_centre)), c_far)

    d_sum, d_coded, token = shard_product(
        amps, picks, 3, [[two_x_mid], [two_x_end], [three_mid_x], [three_end]], tokens)
    ab_far = move(ab_coded, to_y(False, both))
    three_x, tokens = after(token)(move(three_end, moves(across_x_ends, False)))

    d_far = move(d_coded, to_y(True, both))
    e_sum, e_coded, token = shard_product(amps, picks, 4, [[three_x]], tokens, held=lambda part: part)
    e_far = move(e_coded, to_y(True, late_cores))
    c_far, _ = barrier((c_far, token))
    c_both, token = add_coded((c_sum,), [both_halves(c_sum, c_far)], (token, lax.ppermute(token, "col", CORES)))
    flags = [token, lax.ppermute(token, "col", CHIPS_Y)]
    a = [a_sum, (a_far, 0), (ab_far, 0)]
    b = [b_sum, *both_halves(b_sum, ab_far, a_rest.shape[0])]
    d_both, _ = add_coded((d_sum,), [both_halves(d_sum, d_far)])
    d = [d_both]
    e = [e_sum, *both_halves(e_sum, e_far)]

    def finish():
        return lay_out(place, (a, [c_both], d), (b, d, e))

    return lax.cond(
        jnp.max(sum(flags)) > 0, lambda: dense_ladder(amplitudes, integrals, amp_mask, int_mask), finish)


def solution(mesh):
    in_specs = (P("row", "col"), P("col", "row"), P("row", "col"), P("col", "row"))
    out_specs = P("row", "col")
    here = dict(mesh.shape)
    per_device = sparse_ladder if here == {"row": Z * X, "col": Y * 2} else dense_ladder
    return jax.shard_map(
        per_device, mesh=mesh, in_specs=in_specs, out_specs=out_specs, check_vma=False
    )
```

```python
import jax
import jax.numpy as jnp
from jax import lax
from jax.experimental import pallas as pl
from jax.experimental.pallas import tpu as pltpu
from jax.sharding import PartitionSpec as P

TILE = 128
VMEM_LIMIT = 7 * 1024 * 1024


def expand(mask):
    spread = jnp.repeat(jnp.repeat(mask, TILE, axis=0), TILE, axis=1)
    return spread.astype(jnp.bfloat16)


def dense_ladder(amplitudes, integrals, amp_mask, int_mask):
    rows, cols = lax.axis_size("row"), lax.axis_size("col")
    row, col = lax.axis_index("row"), lax.axis_index("col")
    sparse_amp = amplitudes * expand(amp_mask)
    sparse_int = integrals * expand(int_mask)
    width = integrals.shape[1]
    share = rows * width // cols
    sums = jnp.zeros((amplitudes.shape[0], rows * width), jnp.float32)
    for step in range(rows):
        shard = lax.ppermute(sparse_int, "row", [((r + step) % rows, r) for r in range(rows)]) if step else sparse_int
        part = jnp.dot(sparse_amp, shard, preferred_element_type=jnp.float32)
        sums = lax.dynamic_update_slice(sums, part, (0, (row + step) % rows * width))
    ladder = lax.dynamic_slice(sums, (0, col * share), (sums.shape[0], share))
    for step in range(1, cols):
        part = lax.dynamic_slice(sums, (0, (col + step) % cols * share), (sums.shape[0], share))
        ladder = ladder + lax.ppermute(part, "col", [(c, (c + step) % cols) for c in range(cols)])
    return ladder.astype(jnp.bfloat16)


TOKEN = jax.ShapeDtypeStruct((8, TILE), jnp.float32)
LIGHT = pl.CostEstimate(flops=1, bytes_accessed=1, transcendentals=0)
STEPS = 5
TOP = 12
LOW = 4
BITS = 16 + LOW
GROUP = 128
META = 16


def in_hbm(array):
    return pltpu.with_memory_space_constraint(array, pltpu.HBM)


def call(kernel, name, cost=LIGHT, **kwargs):
    return pl.pallas_call(
        kernel,
        compiler_params=pltpu.CompilerParams(vmem_limit_bytes=VMEM_LIMIT),
        cost_estimate=cost,
        name=name,
        **kwargs,
    )


VMEM = pl.BlockSpec(memory_space=pltpu.VMEM)
SMEM = pl.BlockSpec(memory_space=pltpu.SMEM)
ANY = pl.BlockSpec(memory_space=pl.ANY)


def pack_tiles(shards, masks, swap, cap):
    wide = shards[0].shape[1] // TILE
    tiles = masks[0].size
    count = len(shards)

    def kernel(swap_ref, *refs):
        mask_refs, b_refs, out_ref = refs[:count], refs[count:-1], refs[-1]

        @pl.when(swap_ref[0] == 0)
        def _():
            pack(mask_refs, b_refs, out_ref)

        @pl.when(swap_ref[0] != 0)
        def _():
            pack(mask_refs[::-1], b_refs[::-1], out_ref)

    def pack(mask_refs, b_refs, out_ref):
        place = jnp.int32(0)
        lane = lax.broadcasted_iota(jnp.int32, (META, TILE), 1)
        sub = lax.broadcasted_iota(jnp.int32, (META, TILE), 0)
        meta = jnp.zeros((META, TILE), jnp.float32)
        for s in range(count):
            for t in range(tiles):
                k, n = divmod(t, wide)
                keep = mask_refs[s][n, k] != 0

                @pl.when(keep & (place < cap))
                def _(s=s, k=k, n=n, place=place):
                    at = pl.multiple_of(place * TILE, TILE)
                    out_ref[pl.ds(at, TILE), :] = b_refs[s][k * TILE:(k + 1) * TILE, n * TILE:(n + 1) * TILE]

                place = place + keep.astype(jnp.int32)
                meta = jnp.where((lane == s * tiles + t) & keep, 1.0, meta)
        meta = jnp.where(sub == 0, meta, jnp.where((sub == 1) & (place > cap), 1.0, 0.0))
        out_ref[cap * TILE:, :] = meta.astype(out_ref.dtype)

    return call(
        kernel, "pack_tiles",
        out_shape=jax.ShapeDtypeStruct((cap * TILE + META, TILE), shards[0].dtype),
        in_specs=[SMEM] * (1 + count) + [VMEM] * count,
        out_specs=VMEM,
    )(swap, *masks, *shards)


def mask_tiles(amplitudes, masks):
    rows, cols = amplitudes[0].shape
    count = len(amplitudes)

    def kernel(*refs):
        mask_refs, a_refs, out_refs, token_ref, sem = (
            refs[:count], refs[count:2 * count], refs[2 * count:3 * count], *refs[3 * count:])
        token_ref[...] = jnp.zeros_like(token_ref)
        copies = [
            [pltpu.make_async_copy(a_refs[s].at[pl.ds(at, TILE)], out_refs[s].at[pl.ds(at, TILE)], sem.at[s, at // TILE])
             for at in range(0, rows, TILE)] for s in range(count)]
        for copy in sum(copies, []):
            copy.start()
        for s in range(count):
            for r in range(rows // TILE):
                copies[s][r].wait()
                for t in range(cols // TILE):
                    @pl.when(mask_refs[s][r, t] == 0)
                    def _(s=s, r=r, t=t):
                        out_refs[s][r * TILE:(r + 1) * TILE, t * TILE:(t + 1) * TILE] = jnp.zeros(
                            (TILE, TILE), out_refs[s].dtype)

    return call(
        kernel, "mask_tiles",
        out_shape=tuple(jax.ShapeDtypeStruct(part.shape, part.dtype) for part in amplitudes) + (TOKEN,),
        in_specs=[SMEM] * count + [ANY] * count,
        out_specs=(VMEM,) * (count + 1),
        scratch_shapes=[pltpu.SemaphoreType.DMA((count, rows // TILE))],
    )(*masks, *amplitudes)


def shard_product(amps, picks, step, choices, tokens, before=None, split=False, held=in_hbm):
    rows, depth = amps[0].shape
    count = len(amps)
    height = sum(part.shape[0] for part in choices[0])
    cap = height - META
    wide = 2
    tiles = count * wide * depth // TILE
    word = 16
    first_row = 0 if before is None else before.shape[0]
    half_rows = coded_rows(rows // 2)
    parts = []
    for choice in choices:
        for part in choice:
            if not any(part is p for p in parts):
                parts.append(part)

    def kernel(picks_ref, *refs):
        if first_row:
            before_ref, refs = refs[0], refs[1:]
        token_refs, refs = refs[:len(tokens)], refs[len(tokens):]
        a_refs, refs = refs[:count], refs[count:]
        p_any, refs = refs[:len(parts)], refs[len(parts):]
        out_ref, *coded_refs, token_ref, packed, wide_ref, sem = refs
        pick = picks_ref[step]
        token_ref[...] = sum(ref[...] for ref in token_refs)
        for number, choice in enumerate(choices):
            @pl.when(pick == number)
            def _(choice=choice):
                at = 0
                copies = []
                for part in choice:
                    index = [part is p for p in parts].index(True)
                    copies.append(pltpu.make_async_copy(
                        p_any[index], packed.at[pl.ds(at, part.shape[0])], sem.at[len(copies)]))
                    at += part.shape[0]
                for copy in copies:
                    copy.start()
                for copy in copies:
                    copy.wait()

        @pl.when(pick >= 0)
        def _():
            meta = packed[cap:, :].astype(jnp.float32)
            lane = lax.broadcasted_iota(jnp.int32, meta.shape, 1)
            sub = lax.broadcasted_iota(jnp.int32, meta.shape, 0)
            first = (sub == 0) & (meta != 0)
            bits = [
                jnp.sum(jnp.where(
                    first & (lane >= lo) & (lane < lo + word), jnp.left_shift(1, (lane - lo) & (word - 1)), 0))
                for lo in range(0, tiles, word)]
            token_ref[...] += jnp.where(sub == 1, meta, 0.0)[:token_ref.shape[0]]
            place = jnp.int32(0)
            for s in range(count):
                for t in range(s * tiles // count, (s + 1) * tiles // count):
                    k, n = divmod(t, wide)
                    keep = ((bits[t // word] >> (t % word)) & 1) != 0
                    at = pl.multiple_of(jnp.minimum(place * TILE, cap - TILE), TILE)
                    tile = packed[pl.ds(at, TILE), :]
                    wide_ref[k * TILE:(k + 1) * TILE, n * TILE:(n + 1) * TILE] = jnp.where(
                        keep, tile, jnp.zeros_like(tile))
                    place = place + keep.astype(jnp.int32)
                term = jnp.dot(
                    a_refs[s][...], wide_ref[s * depth:(s + 1) * depth, :], preferred_element_type=jnp.float32)
                if s:
                    out_ref[...] += term
                else:
                    out_ref[...] = term

        @pl.when((pick >= 0) & (picks_ref[STEPS + step] != 0))
        def _():
            if first_row:
                coded_refs[0][:first_row, :] = before_ref[...]
            for h, (first, length, at) in enumerate(halves(rows, first_row)):
                spot = coded_refs[h] if split else coded_refs[0].at[pl.ds(at, coded_rows(length))]
                encode(out_ref.at[pl.ds(first, length)], spot)

    return call(
        kernel, "shard_product",
        out_shape=(
            jax.ShapeDtypeStruct((rows, wide * TILE), jnp.float32),
            *([jax.ShapeDtypeStruct((half_rows, wide * TILE), jnp.int16)] * 2 if split else
              [jax.ShapeDtypeStruct((first_row + 2 * half_rows, wide * TILE), jnp.int16)]),
            TOKEN),
        in_specs=[SMEM] + [VMEM] * (bool(first_row) + len(tokens) + count) + [ANY] * len(parts),
        out_specs=(VMEM,) * (4 if split else 3),
        scratch_shapes=[
            pltpu.VMEM((height, TILE), amps[0].dtype),
            pltpu.VMEM((count * depth, wide * TILE), amps[0].dtype),
            pltpu.SemaphoreType.DMA((2,)),
        ],
    )(picks, *([before] if first_row else []), *tokens, *amps, *map(held, parts))


def coded_rows(rows):
    return rows + rows // (16 // LOW) + META


def halves(rows, first_row=0):
    half = rows // 2
    return [(h * half, half, first_row + h * coded_rows(half)) for h in range(2)]


def step_factors(exponent):
    power = BITS - 1 - TOP - exponent
    factors = []
    for part in (power // 2, power - power // 2):
        factor = jnp.ones(part.shape, jnp.float32)
        for bit in range(7):
            factor = factor * jnp.where((part >> bit) & 1 != 0, 2.0 ** (1 << bit), 1.0)
        factors.append(factor)
    return factors


def encode(sums_ref, coded_ref):
    rows, cols = sums_ref.shape
    groups = rows // GROUP
    largest = jnp.concatenate([
        jnp.max(jnp.abs(sums_ref[g * GROUP:(g + 1) * GROUP, :]), axis=0, keepdims=True) for g in range(groups)])
    rest = largest * 2.0 ** -TOP
    exponent = jnp.zeros(rest.shape, jnp.int32)
    for bit in (64, 32, 16, 8, 4, 2, 1):
        small = rest < 2.0 ** -bit
        rest = jnp.where(small, rest * 2.0 ** bit, rest)
        exponent = jnp.where(small, exponent - bit, exponent)
    one, two = step_factors(exponent)
    share = 16 // LOW
    block = rows // share
    for start in range(0, block, GROUP):
        low = jnp.zeros((GROUP, cols), jnp.int32)
        for part in range(share):
            at = part * block + start
            g = at // GROUP
            value = sums_ref[at:at + GROUP, :] * one[g:g + 1] * two[g:g + 1]
            value = jnp.minimum(jnp.round(value).astype(jnp.int32), (1 << (BITS - 1)) - 1)
            coded_ref[at:at + GROUP, :] = (value >> LOW).astype(jnp.int16)
            low = low | ((value & ((1 << LOW) - 1)) << (LOW * part))
        coded_ref[rows + start:rows + start + GROUP, :] = (low - 32768).astype(jnp.int16)
    coded_ref[rows + block:, :] = jnp.concatenate([exponent] * (META // groups)).astype(jnp.int16)


def decode(coded_ref, rows, put):
    groups = rows // GROUP
    share = 16 // LOW
    block = rows // share
    one, two = step_factors(coded_ref[rows + block:, :].astype(jnp.int32)[:groups])
    one, two = 1.0 / one, 1.0 / two
    for start in range(0, block, GROUP):
        low = coded_ref[rows + start:rows + start + GROUP, :].astype(jnp.int32) + 32768
        for part in range(share):
            at = part * block + start
            g = at // GROUP
            high = coded_ref[at:at + GROUP, :].astype(jnp.int32)
            value = (high << LOW) | ((low >> (LOW * part)) & ((1 << LOW) - 1))
            put(at, value.astype(jnp.float32) * one[g:g + 1] * two[g:g + 1])


def add_coded(sums, coded, tokens=()):
    count = len(sums)
    arrays = []
    for array, _ in [pair for one in coded for pair in one]:
        if not any(array is known for known in arrays):
            arrays.append(array)

    def kernel(*refs):
        token_refs, refs = refs[:len(tokens)], refs[len(tokens):]
        sums_refs, coded_refs, out_refs, token_ref = refs[:count], refs[count:-count - 1], refs[-count - 1:-1], refs[-1]
        token_ref[...] = sum((ref[...] for ref in token_refs), jnp.zeros(token_ref.shape, token_ref.dtype))
        for number in range(count):
            for (first, length, _), (array, at) in zip(halves(sums[number].shape[0]), coded[number]):
                ref = coded_refs[[array is known for known in arrays].index(True)]
                add_half(sums_refs[number], ref.at[pl.ds(at, coded_rows(length))], out_refs[number], first, length)

    return call(
        kernel, "add_coded",
        out_shape=tuple(jax.ShapeDtypeStruct(part.shape, jnp.bfloat16) for part in sums) + (TOKEN,),
        in_specs=[VMEM] * (len(tokens) + count + len(arrays)),
        out_specs=(VMEM,) * (count + 1),
    )(*tokens, *sums, *arrays)


def add_half(sums_ref, coded_ref, out_ref, first, length):
    def put(at, far):
        spot = pl.ds(first + at, GROUP)
        out_ref[spot, :] = (sums_ref[spot, :] + far).astype(out_ref.dtype)

    decode(coded_ref, length, put)


def both_halves(sums, coded, first_row=0):
    return [(coded, at) for _, _, at in halves(sums.shape[0], first_row)]


def lay_out(place, mine, rest):
    choices = list(zip(mine, rest))
    arrays = []
    for choice in choices:
        for sums, *coded in choice:
            for array in (sums, *[array for array, _ in coded]):
                if not any(array is known for known in arrays):
                    arrays.append(array)
    rows, width = arrays[0].shape
    parts = halves(rows)

    def kernel(place_ref, *refs):
        ins = refs[:len(arrays)]
        out_any, round_ref, sums_ref, coded_ref, sems = refs[len(arrays):]

        def place_of(array):
            return ins[[array is known for known in arrays].index(True)]

        def store(side, first, length):
            at = pl.multiple_of((place_ref[1] ^ side) * width, width)
            return pltpu.make_async_copy(
                round_ref.at[side, pl.ds(first, length)], out_any.at[pl.ds(first, length), pl.ds(at, width)],
                sems.at[2, 2 * side + first // length])

        for number, choice in enumerate(choices):
            @pl.when(place_ref[0] == number)
            def _(choice=choice):
                fetch = {}
                for side, (sums, *coded) in enumerate(choice):
                    for h, (first, length, _) in enumerate(parts):
                        fetch[side, h] = [pltpu.make_async_copy(
                            place_of(sums).at[pl.ds(first, length)],
                            (sums_ref if coded else round_ref).at[side, pl.ds(first, length)], sems.at[0, 2 * side + h])]
                        if coded:
                            array, at = coded[h]
                            fetch[side, h].append(pltpu.make_async_copy(
                                place_of(array).at[pl.ds(at, coded_rows(length))], coded_ref.at[side, h],
                                sems.at[1, 2 * side + h]))
                for copy in sum(fetch.values(), []):
                    copy.start()
                for side, (sums, *coded) in enumerate(choice):
                    for h, (first, length, _) in enumerate(parts):
                        for copy in fetch[side, h]:
                            copy.wait()
                        if coded:
                            add_half(sums_ref.at[side], coded_ref.at[side, h], round_ref.at[side], first, length)
                        store(side, first, length).start()

        for side in range(2):
            for first, length, _ in parts:
                store(side, first, length).wait()

    return call(
        kernel, "lay_out",
        out_shape=pltpu.HBM((rows, 2 * width), jnp.bfloat16),
        in_specs=[SMEM] + [ANY] * len(arrays),
        out_specs=ANY,
        scratch_shapes=[
            pltpu.VMEM((2, rows, width), jnp.bfloat16),
            pltpu.VMEM((2, rows, width), jnp.float32),
            pltpu.VMEM((2, 2, coded_rows(rows // 2), width), jnp.int16),
            pltpu.SemaphoreType.DMA((3, 4))],
    )(place, *arrays)


Z, X, Y = 4, 2, 2
AXES = ("row", "col")


def device(z, x, y, c):
    return (z * X + x) * Y * 2 + y * 2 + c


def moves(to, home=True):
    pairs = []
    for z in range(Z):
        for x in range(X):
            for y in range(Y):
                if to(z, x) is not None:
                    c = z % 2 if home else 1 - z % 2
                    pairs.append((device(z, x, y, c), device(*to(z, x), y, c)))
    return pairs


def across_x(z, x):
    return z, 1 - x


def across_x_ends(z, x):
    return (z, 1 - x) if z in (0, 3) else None


def across_x_middle(z, x):
    return (z, 1 - x) if z in (1, 2) else None


def over_centre(z, x):
    return (3 - z, x) if z in (1, 2) else None


def outward(z, x):
    return (z ^ 1, x) if z in (1, 2) else None


def to_y(far, cores):
    pairs = []
    for z in range(Z):
        end = (z // 2) ^ int(far)
        for x in range(X):
            for c in cores(z):
                pairs.append((device(z, x, 1 - end, c), device(z, x, end, c)))
    return pairs


def both(z):
    return 0, 1


def early_cores(z):
    return (0, 1) if z in (1, 2) else (z % 2,)


def late_cores(z):
    return () if z in (1, 2) else (1 - z % 2,)


OWN_TO_PAIR = [
    (device(z, x, y, 1 - z % 2), device(z ^ 1, x, y, z % 2)) for z in range(Z) for x in range(X) for y in range(Y)]
CORES = [(0, 1), (1, 0), (2, 3), (3, 2)]
CHIPS_Y = [(0, 2), (2, 0), (1, 3), (3, 1)]


def sparse_ladder(amplitudes, integrals, amp_mask, int_mask):
    barrier = lax.optimization_barrier
    tiles = int_mask.size
    cap = 2 * tiles * 11 // 16
    row, col = lax.axis_index("row"), lax.axis_index("col")
    z, x = row // X, row % X
    y, c = col // 2, col % 2
    is_end = ((z == 0) | (z == Z - 1)).astype(jnp.int32)
    home = z % 2 == c

    def move(value, pairs):
        return lax.ppermute(value, AXES, pairs)

    def after(*tokens):
        return lambda *shards: barrier((*shards, tokens))

    near = z // 2 == y
    picks = jnp.stack([
        jnp.where(home, 0, 1),
        jnp.where(home, is_end, jnp.where(is_end, -1, 2)),
        jnp.where(home, 0, 1),
        jnp.where(home, is_end, 2 + is_end),
        jnp.where(home, -1, is_end - 1),
    ] + [jnp.where(near, s, 1 - s) for s in (0, 1, 0, 1, 1)]).astype(jnp.int32)

    place = jnp.stack([jnp.where(near, 0, jnp.where(home | (is_end == 0), 1, 2)), x]).astype(jnp.int32)

    other = lax.ppermute(integrals, "col", CORES)
    other_mask = lax.ppermute(int_mask.T, "col", CORES)
    other_amp_mask = lax.ppermute(amp_mask, "col", CORES)
    swap = jnp.where(home, 0, 1).astype(jnp.int32).reshape(1)
    own = pack_tiles((integrals, other), (int_mask.T, other_mask), swap, cap)
    own, picks, place, other_amp_mask, amplitudes_now = barrier((own, picks, place, other_amp_mask, amplitudes))
    other_amps = lax.ppermute(amplitudes_now, "col", CORES)

    *amps, masked_token = mask_tiles((amplitudes, other_amps), (amp_mask, other_amp_mask))
    own_x, one, centre, tokens = after(masked_token)(
        move(own, moves(across_x)), move(own, OWN_TO_PAIR), move(own, moves(over_centre)))

    a_sum, a_coded, a_rest, token = shard_product(amps, picks, 0, [[own], [one]], tokens, split=True)
    a_far = move(a_coded, to_y(False, both))
    one_x, two_mid, two_end, own_x, a_far, tokens = after(token)(
        move(one, moves(across_x, False)), move(one, moves(over_centre, False)), move(centre, moves(outward, False)),
        own_x, a_far)

    c_sum, c_coded, token = shard_product(amps, picks, 1, [[two_mid], [two_end], [centre]], tokens)
    c_far = move(c_coded, to_y(True, early_cores))
    b_sum, ab_coded, token = shard_product(amps, picks, 2, [[own_x], [one_x]], (token,), a_rest)
    two_x_end, three_end, two_x_mid, three_mid_x, c_far, tokens = after(token)(
        move(two_end, moves(across_x_ends)), move(two_mid, moves(outward)),
        move(two_mid, moves(across_x_middle)), move(own_x, moves(over_centre)), c_far)

    d_sum, d_coded, token = shard_product(
        amps, picks, 3, [[two_x_mid], [two_x_end], [three_mid_x], [three_end]], tokens)
    ab_far = move(ab_coded, to_y(False, both))
    three_x, tokens = after(token)(move(three_end, moves(across_x_ends, False)))

    d_far = move(d_coded, to_y(True, both))
    e_sum, e_coded, token = shard_product(amps, picks, 4, [[three_x]], tokens, held=lambda part: part)
    e_far = move(e_coded, to_y(True, late_cores))
    c_far, _ = barrier((c_far, token))
    c_both, token = add_coded((c_sum,), [both_halves(c_sum, c_far)], (token, lax.ppermute(token, "col", CORES)))
    flags = [token, lax.ppermute(token, "col", CHIPS_Y)]
    a = [a_sum, (a_far, 0), (ab_far, 0)]
    b = [b_sum, *both_halves(b_sum, ab_far, a_rest.shape[0])]
    d_both, _ = add_coded((d_sum,), [both_halves(d_sum, d_far)])
    d = [d_both]
    e = [e_sum, *both_halves(e_sum, e_far)]

    def finish():
        return lay_out(place, (a, [c_both], d), (b, d, e))

    return lax.cond(
        jnp.max(sum(flags)) > 0, lambda: dense_ladder(amplitudes, integrals, amp_mask, int_mask), finish)


def solution(mesh):
    in_specs = (P("row", "col"), P("col", "row"), P("row", "col"), P("col", "row"))
    out_specs = P("row", "col")
    here = dict(mesh.shape)
    per_device = sparse_ladder if here == {"row": Z * X, "col": Y * 2} else dense_ladder
    return jax.shard_map(
        per_device, mesh=mesh, in_specs=in_specs, out_specs=out_specs, check_vma=False
    )
```

```python
import jax
import jax.numpy as jnp
from jax import lax
from jax.experimental import pallas as pl
from jax.experimental.pallas import tpu as pltpu
from jax.sharding import PartitionSpec as P

TILE = 128
VMEM_LIMIT = 7 * 1024 * 1024


def expand(mask):
    spread = jnp.repeat(jnp.repeat(mask, TILE, axis=0), TILE, axis=1)
    return spread.astype(jnp.bfloat16)


def dense_ladder(amplitudes, integrals, amp_mask, int_mask):
    rows, cols = lax.axis_size("row"), lax.axis_size("col")
    row, col = lax.axis_index("row"), lax.axis_index("col")
    sparse_amp = amplitudes * expand(amp_mask)
    sparse_int = integrals * expand(int_mask)
    width = integrals.shape[1]
    share = rows * width // cols
    sums = jnp.zeros((amplitudes.shape[0], rows * width), jnp.float32)
    for step in range(rows):
        shard = lax.ppermute(sparse_int, "row", [((r + step) % rows, r) for r in range(rows)]) if step else sparse_int
        part = jnp.dot(sparse_amp, shard, preferred_element_type=jnp.float32)
        sums = lax.dynamic_update_slice(sums, part, (0, (row + step) % rows * width))
    ladder = lax.dynamic_slice(sums, (0, col * share), (sums.shape[0], share))
    for step in range(1, cols):
        part = lax.dynamic_slice(sums, (0, (col + step) % cols * share), (sums.shape[0], share))
        ladder = ladder + lax.ppermute(part, "col", [(c, (c + step) % cols) for c in range(cols)])
    return ladder.astype(jnp.bfloat16)


TOKEN = jax.ShapeDtypeStruct((8, TILE), jnp.float32)
LIGHT = pl.CostEstimate(flops=1, bytes_accessed=1, transcendentals=0)
STEPS = 5
TOP = 12
LOW = 4
BITS = 16 + LOW
GROUP = 128
META = 16


def in_hbm(array):
    return pltpu.with_memory_space_constraint(array, pltpu.HBM)


def call(kernel, name, cost=LIGHT, **kwargs):
    return pl.pallas_call(
        kernel,
        compiler_params=pltpu.CompilerParams(vmem_limit_bytes=VMEM_LIMIT),
        cost_estimate=cost,
        name=name,
        **kwargs,
    )


VMEM = pl.BlockSpec(memory_space=pltpu.VMEM)
SMEM = pl.BlockSpec(memory_space=pltpu.SMEM)
ANY = pl.BlockSpec(memory_space=pl.ANY)


def pack_tiles(shards, masks, swap, cap):
    wide = shards[0].shape[1] // TILE
    tiles = masks[0].size
    count = len(shards)

    def kernel(swap_ref, *refs):
        mask_refs, b_refs, out_ref = refs[:count], refs[count:-1], refs[-1]

        @pl.when(swap_ref[0] == 0)
        def _():
            pack(mask_refs, b_refs, out_ref)

        @pl.when(swap_ref[0] != 0)
        def _():
            pack(mask_refs[::-1], b_refs[::-1], out_ref)

    def pack(mask_refs, b_refs, out_ref):
        place = jnp.int32(0)
        lane = lax.broadcasted_iota(jnp.int32, (META, TILE), 1)
        sub = lax.broadcasted_iota(jnp.int32, (META, TILE), 0)
        meta = jnp.zeros((META, TILE), jnp.float32)
        for s in range(count):
            for t in range(tiles):
                k, n = divmod(t, wide)
                keep = mask_refs[s][n, k] != 0

                @pl.when(keep & (place < cap))
                def _(s=s, k=k, n=n, place=place):
                    at = pl.multiple_of(place * TILE, TILE)
                    out_ref[pl.ds(at, TILE), :] = b_refs[s][k * TILE:(k + 1) * TILE, n * TILE:(n + 1) * TILE]

                place = place + keep.astype(jnp.int32)
                meta = jnp.where((lane == s * tiles + t) & keep, 1.0, meta)
        meta = jnp.where(sub == 0, meta, jnp.where((sub == 1) & (place > cap), 1.0, 0.0))
        out_ref[cap * TILE:, :] = meta.astype(out_ref.dtype)

    return call(
        kernel, "pack_tiles",
        out_shape=jax.ShapeDtypeStruct((cap * TILE + META, TILE), shards[0].dtype),
        in_specs=[SMEM] * (1 + count) + [VMEM] * count,
        out_specs=VMEM,
    )(swap, *masks, *shards)


def mask_tiles(amplitudes, masks):
    rows, cols = amplitudes[0].shape
    count = len(amplitudes)

    def kernel(*refs):
        mask_refs, a_refs, out_refs, token_ref, sem = (
            refs[:count], refs[count:2 * count], refs[2 * count:3 * count], *refs[3 * count:])
        token_ref[...] = jnp.zeros_like(token_ref)
        copies = [
            [pltpu.make_async_copy(a_refs[s].at[pl.ds(at, TILE)], out_refs[s].at[pl.ds(at, TILE)], sem.at[s, at // TILE])
             for at in range(0, rows, TILE)] for s in range(count)]
        for copy in sum(copies, []):
            copy.start()
        for s in range(count):
            for r in range(rows // TILE):
                copies[s][r].wait()
                for t in range(cols // TILE):
                    @pl.when(mask_refs[s][r, t] == 0)
                    def _(s=s, r=r, t=t):
                        out_refs[s][r * TILE:(r + 1) * TILE, t * TILE:(t + 1) * TILE] = jnp.zeros(
                            (TILE, TILE), out_refs[s].dtype)

    return call(
        kernel, "mask_tiles",
        out_shape=tuple(jax.ShapeDtypeStruct(part.shape, part.dtype) for part in amplitudes) + (TOKEN,),
        in_specs=[SMEM] * count + [ANY] * count,
        out_specs=(VMEM,) * (count + 1),
        scratch_shapes=[pltpu.SemaphoreType.DMA((count, rows // TILE))],
    )(*masks, *amplitudes)


def shard_product(amps, picks, step, choices, tokens, before=None, split=False, held=in_hbm):
    rows, depth = amps[0].shape
    count = len(amps)
    height = sum(part.shape[0] for part in choices[0])
    cap = height - META
    wide = 2
    tiles = count * wide * depth // TILE
    word = 16
    first_row = 0 if before is None else before.shape[0]
    half_rows = coded_rows(rows // 2)
    direct = len(choices) == 1
    parts = []
    for choice in choices:
        for part in choice:
            if not any(part is p for p in parts):
                parts.append(part)

    def kernel(picks_ref, *refs):
        if first_row:
            before_ref, refs = refs[0], refs[1:]
        token_refs, refs = refs[:len(tokens)], refs[len(tokens):]
        a_refs, refs = refs[:count], refs[count:]
        p_any, refs = refs[:len(parts)], refs[len(parts):]
        out_ref, *coded_refs, token_ref, packed, wide_ref, sem = refs
        if direct:
            packed = p_any[0]
        pick = picks_ref[step]
        token_ref[...] = sum(ref[...] for ref in token_refs)
        for number, choice in enumerate([] if direct else choices):
            @pl.when(pick == number)
            def _(choice=choice):
                at = 0
                copies = []
                for part in choice:
                    index = [part is p for p in parts].index(True)
                    copies.append(pltpu.make_async_copy(
                        p_any[index], packed.at[pl.ds(at, part.shape[0])], sem.at[len(copies)]))
                    at += part.shape[0]
                for copy in copies:
                    copy.start()
                for copy in copies:
                    copy.wait()

        @pl.when(pick >= 0)
        def _():
            meta = packed[cap:, :].astype(jnp.float32)
            lane = lax.broadcasted_iota(jnp.int32, meta.shape, 1)
            sub = lax.broadcasted_iota(jnp.int32, meta.shape, 0)
            first = (sub == 0) & (meta != 0)
            bits = [
                jnp.sum(jnp.where(
                    first & (lane >= lo) & (lane < lo + word), jnp.left_shift(1, (lane - lo) & (word - 1)), 0))
                for lo in range(0, tiles, word)]
            token_ref[...] += jnp.where(sub == 1, meta, 0.0)[:token_ref.shape[0]]
            place = jnp.int32(0)
            for s in range(count):
                for t in range(s * tiles // count, (s + 1) * tiles // count):
                    k, n = divmod(t, wide)
                    keep = ((bits[t // word] >> (t % word)) & 1) != 0
                    at = pl.multiple_of(jnp.minimum(place * TILE, cap - TILE), TILE)
                    tile = packed[pl.ds(at, TILE), :]
                    wide_ref[k * TILE:(k + 1) * TILE, n * TILE:(n + 1) * TILE] = jnp.where(
                        keep, tile, jnp.zeros_like(tile))
                    place = place + keep.astype(jnp.int32)
                term = jnp.dot(
                    a_refs[s][...], wide_ref[s * depth:(s + 1) * depth, :], preferred_element_type=jnp.float32)
                if s:
                    out_ref[...] += term
                else:
                    out_ref[...] = term

        @pl.when((pick >= 0) & (picks_ref[STEPS + step] != 0))
        def _():
            if first_row:
                coded_refs[0][:first_row, :] = before_ref[...]
            for h, (first, length, at) in enumerate(halves(rows, first_row)):
                spot = coded_refs[h] if split else coded_refs[0].at[pl.ds(at, coded_rows(length))]
                encode(out_ref.at[pl.ds(first, length)], spot)

    return call(
        kernel, "shard_product",
        out_shape=(
            jax.ShapeDtypeStruct((rows, wide * TILE), jnp.float32),
            *([jax.ShapeDtypeStruct((half_rows, wide * TILE), jnp.int16)] * 2 if split else
              [jax.ShapeDtypeStruct((first_row + 2 * half_rows, wide * TILE), jnp.int16)]),
            TOKEN),
        in_specs=[SMEM] + [VMEM] * (bool(first_row) + len(tokens) + count) + [VMEM if direct else ANY] * len(parts),
        out_specs=(VMEM,) * (4 if split else 3),
        scratch_shapes=[
            pltpu.VMEM((META if direct else height, TILE), amps[0].dtype),
            pltpu.VMEM((count * depth, wide * TILE), amps[0].dtype),
            pltpu.SemaphoreType.DMA((2,)),
        ],
    )(picks, *([before] if first_row else []), *tokens, *amps, *map(held, parts))


def coded_rows(rows):
    return rows + rows // (16 // LOW) + META


def halves(rows, first_row=0):
    half = rows // 2
    return [(h * half, half, first_row + h * coded_rows(half)) for h in range(2)]


def step_factors(exponent):
    power = BITS - 1 - TOP - exponent
    factors = []
    for part in (power // 2, power - power // 2):
        factor = jnp.ones(part.shape, jnp.float32)
        for bit in range(7):
            factor = factor * jnp.where((part >> bit) & 1 != 0, 2.0 ** (1 << bit), 1.0)
        factors.append(factor)
    return factors


def encode(sums_ref, coded_ref):
    rows, cols = sums_ref.shape
    groups = rows // GROUP
    largest = jnp.concatenate([
        jnp.max(jnp.abs(sums_ref[g * GROUP:(g + 1) * GROUP, :]), axis=0, keepdims=True) for g in range(groups)])
    rest = largest * 2.0 ** -TOP
    exponent = jnp.zeros(rest.shape, jnp.int32)
    for bit in (64, 32, 16, 8, 4, 2, 1):
        small = rest < 2.0 ** -bit
        rest = jnp.where(small, rest * 2.0 ** bit, rest)
        exponent = jnp.where(small, exponent - bit, exponent)
    one, two = step_factors(exponent)
    share = 16 // LOW
    block = rows // share
    for start in range(0, block, GROUP):
        low = jnp.zeros((GROUP, cols), jnp.int32)
        for part in range(share):
            at = part * block + start
            g = at // GROUP
            value = sums_ref[at:at + GROUP, :] * one[g:g + 1] * two[g:g + 1]
            value = jnp.minimum(jnp.round(value).astype(jnp.int32), (1 << (BITS - 1)) - 1)
            coded_ref[at:at + GROUP, :] = (value >> LOW).astype(jnp.int16)
            low = low | ((value & ((1 << LOW) - 1)) << (LOW * part))
        coded_ref[rows + start:rows + start + GROUP, :] = (low - 32768).astype(jnp.int16)
    coded_ref[rows + block:, :] = jnp.concatenate([exponent] * (META // groups)).astype(jnp.int16)


def decode(coded_ref, rows, put):
    groups = rows // GROUP
    share = 16 // LOW
    block = rows // share
    one, two = step_factors(coded_ref[rows + block:, :].astype(jnp.int32)[:groups])
    one, two = 1.0 / one, 1.0 / two
    for start in range(0, block, GROUP):
        low = coded_ref[rows + start:rows + start + GROUP, :].astype(jnp.int32) + 32768
        for part in range(share):
            at = part * block + start
            g = at // GROUP
            high = coded_ref[at:at + GROUP, :].astype(jnp.int32)
            value = (high << LOW) | ((low >> (LOW * part)) & ((1 << LOW) - 1))
            put(at, value.astype(jnp.float32) * one[g:g + 1] * two[g:g + 1])


def add_coded(sums, coded, tokens=()):
    count = len(sums)
    arrays = []
    for array, _ in [pair for one in coded for pair in one]:
        if not any(array is known for known in arrays):
            arrays.append(array)

    def kernel(*refs):
        token_refs, refs = refs[:len(tokens)], refs[len(tokens):]
        sums_refs, coded_refs, out_refs, token_ref = refs[:count], refs[count:-count - 1], refs[-count - 1:-1], refs[-1]
        token_ref[...] = sum((ref[...] for ref in token_refs), jnp.zeros(token_ref.shape, token_ref.dtype))
        for number in range(count):
            for (first, length, _), (array, at) in zip(halves(sums[number].shape[0]), coded[number]):
                ref = coded_refs[[array is known for known in arrays].index(True)]
                add_half(sums_refs[number], ref.at[pl.ds(at, coded_rows(length))], out_refs[number], first, length)

    return call(
        kernel, "add_coded",
        out_shape=tuple(jax.ShapeDtypeStruct(part.shape, jnp.bfloat16) for part in sums) + (TOKEN,),
        in_specs=[VMEM] * (len(tokens) + count + len(arrays)),
        out_specs=(VMEM,) * (count + 1),
    )(*tokens, *sums, *arrays)


def add_half(sums_ref, coded_ref, out_ref, first, length):
    def put(at, far):
        spot = pl.ds(first + at, GROUP)
        out_ref[spot, :] = (sums_ref[spot, :] + far).astype(out_ref.dtype)

    decode(coded_ref, length, put)


def both_halves(sums, coded, first_row=0):
    return [(coded, at) for _, _, at in halves(sums.shape[0], first_row)]


def lay_out(place, mine, rest):
    choices = list(zip(mine, rest))
    arrays = []
    for choice in choices:
        for sums, *coded in choice:
            for array in (sums, *[array for array, _ in coded]):
                if not any(array is known for known in arrays):
                    arrays.append(array)
    rows, width = arrays[0].shape
    parts = halves(rows)

    def kernel(place_ref, *refs):
        ins = refs[:len(arrays)]
        out_any, round_ref, sums_ref, coded_ref, sems = refs[len(arrays):]

        def place_of(array):
            return ins[[array is known for known in arrays].index(True)]

        def store(side, first, length):
            at = pl.multiple_of((place_ref[1] ^ side) * width, width)
            return pltpu.make_async_copy(
                round_ref.at[side, pl.ds(first, length)], out_any.at[pl.ds(first, length), pl.ds(at, width)],
                sems.at[2, 2 * side + first // length])

        for number, choice in enumerate(choices):
            @pl.when(place_ref[0] == number)
            def _(choice=choice):
                fetch = {}
                for side, (sums, *coded) in enumerate(choice):
                    for h, (first, length, _) in enumerate(parts):
                        fetch[side, h] = [pltpu.make_async_copy(
                            place_of(sums).at[pl.ds(first, length)],
                            (sums_ref if coded else round_ref).at[side, pl.ds(first, length)], sems.at[0, 2 * side + h])]
                        if coded:
                            array, at = coded[h]
                            fetch[side, h].append(pltpu.make_async_copy(
                                place_of(array).at[pl.ds(at, coded_rows(length))], coded_ref.at[side, h],
                                sems.at[1, 2 * side + h]))
                for copy in sum(fetch.values(), []):
                    copy.start()
                for side, (sums, *coded) in enumerate(choice):
                    for h, (first, length, _) in enumerate(parts):
                        for copy in fetch[side, h]:
                            copy.wait()
                        if coded:
                            add_half(sums_ref.at[side], coded_ref.at[side, h], round_ref.at[side], first, length)
                        store(side, first, length).start()

        for side in range(2):
            for first, length, _ in parts:
                store(side, first, length).wait()

    return call(
        kernel, "lay_out",
        out_shape=pltpu.HBM((rows, 2 * width), jnp.bfloat16),
        in_specs=[SMEM] + [ANY] * len(arrays),
        out_specs=ANY,
        scratch_shapes=[
            pltpu.VMEM((2, rows, width), jnp.bfloat16),
            pltpu.VMEM((2, rows, width), jnp.float32),
            pltpu.VMEM((2, 2, coded_rows(rows // 2), width), jnp.int16),
            pltpu.SemaphoreType.DMA((3, 4))],
    )(place, *arrays)


Z, X, Y = 4, 2, 2
AXES = ("row", "col")


def device(z, x, y, c):
    return (z * X + x) * Y * 2 + y * 2 + c


def moves(to, home=True):
    pairs = []
    for z in range(Z):
        for x in range(X):
            for y in range(Y):
                if to(z, x) is not None:
                    c = z % 2 if home else 1 - z % 2
                    pairs.append((device(z, x, y, c), device(*to(z, x), y, c)))
    return pairs


def across_x(z, x):
    return z, 1 - x


def across_x_ends(z, x):
    return (z, 1 - x) if z in (0, 3) else None


def across_x_middle(z, x):
    return (z, 1 - x) if z in (1, 2) else None


def over_centre(z, x):
    return (3 - z, x) if z in (1, 2) else None


def outward(z, x):
    return (z ^ 1, x) if z in (1, 2) else None


def to_y(far, cores):
    pairs = []
    for z in range(Z):
        end = (z // 2) ^ int(far)
        for x in range(X):
            for c in cores(z):
                pairs.append((device(z, x, 1 - end, c), device(z, x, end, c)))
    return pairs


def both(z):
    return 0, 1


def early_cores(z):
    return (0, 1) if z in (1, 2) else (z % 2,)


def late_cores(z):
    return () if z in (1, 2) else (1 - z % 2,)


OWN_TO_PAIR = [
    (device(z, x, y, 1 - z % 2), device(z ^ 1, x, y, z % 2)) for z in range(Z) for x in range(X) for y in range(Y)]
CORES = [(0, 1), (1, 0), (2, 3), (3, 2)]
CHIPS_Y = [(0, 2), (2, 0), (1, 3), (3, 1)]


def sparse_ladder(amplitudes, integrals, amp_mask, int_mask):
    barrier = lax.optimization_barrier
    tiles = int_mask.size
    cap = 2 * tiles * 11 // 16
    row, col = lax.axis_index("row"), lax.axis_index("col")
    z, x = row // X, row % X
    y, c = col // 2, col % 2
    is_end = ((z == 0) | (z == Z - 1)).astype(jnp.int32)
    home = z % 2 == c

    def move(value, pairs):
        return lax.ppermute(value, AXES, pairs)

    def after(*tokens):
        return lambda *shards: barrier((*shards, tokens))

    near = z // 2 == y
    picks = jnp.stack([
        jnp.where(home, 0, 1),
        jnp.where(home, is_end, jnp.where(is_end, -1, 2)),
        jnp.where(home, 0, 1),
        jnp.where(home, is_end, 2 + is_end),
        jnp.where(home, -1, is_end - 1),
    ] + [jnp.where(near, s, 1 - s) for s in (0, 1, 0, 1, 1)]).astype(jnp.int32)

    place = jnp.stack([jnp.where(near, 0, jnp.where(home | (is_end == 0), 1, 2)), x]).astype(jnp.int32)

    other = lax.ppermute(integrals, "col", CORES)
    other_mask = lax.ppermute(int_mask.T, "col", CORES)
    other_amp_mask = lax.ppermute(amp_mask, "col", CORES)
    swap = jnp.where(home, 0, 1).astype(jnp.int32).reshape(1)
    own = pack_tiles((integrals, other), (int_mask.T, other_mask), swap, cap)
    own, picks, place, other_amp_mask, amplitudes_now = barrier((own, picks, place, other_amp_mask, amplitudes))
    other_amps = lax.ppermute(amplitudes_now, "col", CORES)

    *amps, masked_token = mask_tiles((amplitudes, other_amps), (amp_mask, other_amp_mask))
    own_x, one, centre, tokens = after(masked_token)(
        move(own, moves(across_x)), move(own, OWN_TO_PAIR), move(own, moves(over_centre)))

    a_sum, a_coded, a_rest, token = shard_product(amps, picks, 0, [[own], [one]], tokens, split=True)
    a_far = move(a_coded, to_y(False, both))
    one_x, two_mid, two_end, own_x, a_far, tokens = after(token)(
        move(one, moves(across_x, False)), move(one, moves(over_centre, False)), move(centre, moves(outward, False)),
        own_x, a_far)

    c_sum, c_coded, token = shard_product(amps, picks, 1, [[two_mid], [two_end], [centre]], tokens)
    c_far = move(c_coded, to_y(True, early_cores))
    b_sum, ab_coded, token = shard_product(amps, picks, 2, [[own_x], [one_x]], (token,), a_rest)
    two_x_end, three_end, two_x_mid, three_mid_x, c_far, tokens = after(token)(
        move(two_end, moves(across_x_ends)), move(two_mid, moves(outward)),
        move(two_mid, moves(across_x_middle)), move(own_x, moves(over_centre)), c_far)

    d_sum, d_coded, token = shard_product(
        amps, picks, 3, [[two_x_mid], [two_x_end], [three_mid_x], [three_end]], tokens)
    ab_far = move(ab_coded, to_y(False, both))
    three_x, tokens = after(token)(move(three_end, moves(across_x_ends, False)))

    d_far = move(d_coded, to_y(True, both))
    e_sum, e_coded, token = shard_product(amps, picks, 4, [[three_x]], tokens, held=lambda part: part)
    e_far = move(e_coded, to_y(True, late_cores))
    c_far, _ = barrier((c_far, token))
    c_both, token = add_coded((c_sum,), [both_halves(c_sum, c_far)], (token, lax.ppermute(token, "col", CORES)))
    flags = [token, lax.ppermute(token, "col", CHIPS_Y)]
    a = [a_sum, (a_far, 0), (ab_far, 0)]
    b = [b_sum, *both_halves(b_sum, ab_far, a_rest.shape[0])]
    d_both, _ = add_coded((d_sum,), [both_halves(d_sum, d_far)])
    d = [d_both]
    e = [e_sum, *both_halves(e_sum, e_far)]

    def finish():
        return lay_out(place, (a, [c_both], d), (b, d, e))

    return lax.cond(
        jnp.max(sum(flags)) > 0, lambda: dense_ladder(amplitudes, integrals, amp_mask, int_mask), finish)


def solution(mesh):
    in_specs = (P("row", "col"), P("col", "row"), P("row", "col"), P("col", "row"))
    out_specs = P("row", "col")
    here = dict(mesh.shape)
    per_device = sparse_ladder if here == {"row": Z * X, "col": Y * 2} else dense_ladder
    return jax.shard_map(
        per_device, mesh=mesh, in_specs=in_specs, out_specs=out_specs, check_vma=False
    )
```
